32 devices in a mesh: section: 2 (over x), dp: 4 (over z), tensor: 4 (over y, core).
Axes of the slice: x: 2, y: 2, z: 4, core: 2. Of those that a mesh axis runs over, the one named last changes fastest.
Arguments:
- block_in: bfloat16 [2, 24, 256, 768], P('section', 'dp', 'tensor'), may hold values from -6 to 6
- lengths: int32 [24], P('dp'), may hold values from 129 to 256, as said below
- patch_mask: int32 [24, 256], P('dp'), may hold values 0 or 1
- pred_grad: bfloat16 [24, 256, 768], P('dp', 'tensor'), may hold values from -6 to 6
- w_qkv: bfloat16 [2, 3, 768, 768], P('section', None, None, 'tensor'), may hold values from -0.21875 to 0.21875
- w_out: bfloat16 [2, 768, 768], P('section', 'tensor'), may hold values from -0.875 to 0.875
- w_up: bfloat16 [2, 768, 3072], P('section', None, 'tensor'), may hold values from -0.21875 to 0.21875
- w_down: bfloat16 [2, 3072, 768], P('section', 'tensor'), may hold values from -0.109375 to 0.109375
- qv_bias: float32 [2, 2, 768], P('section', None, 'tensor'), may hold values from -1.8 to 1.8
- mlp_bias: float32 [2, 3072], P('section', 'tensor'), may hold values from -1.8 to 1.8
- norms: float32 [2, 8, 768], P('section'), may hold values from -0.9 to 1.6, as said below
Outputs:
- results: bfloat16 [2, 24, 256, 768], P('section', 'dp', 'tensor')
- grad_in: float32 [2, 24, 256, 768], P('section', 'dp', 'tensor')
- grad_qkv: float32 [2, 3, 768, 768], P('section', None, None, 'tensor')
- grad_out: float32 [2, 768, 768], P('section', 'tensor')
- grad_up: float32 [2, 768, 3072], P('section', None, 'tensor')
- grad_down: float32 [2, 3072, 768], P('section', 'tensor')
- grad_qv_bias: float32 [2, 2, 768], P('section', None, 'tensor')
- grad_mlp_bias: float32 [2, 3072], P('section', 'tensor')
- grad_norms: float32 [2, 8, 768], P('section')
The draws below stay inside these ranges and needn't reach their ends.
Inputs may be any that keep to these rules, and one draw needn't show every extreme that they name: `lengths`: slots at or past an image's length are padding; some image has all 256 slots real. `norms`: rows 0 and 4 are norm gains, 1 and 5 norm shifts, 2 and 6 output biases, 3 and 7 layer scales.
All inputs are finite; a program needn't handle non-finite values. No bound on the sum of `patch_mask` on one device may be relied on, other than what follows from the above.
Results may differ from the reference program's by a relative error of at most 0.018.
Values may be sent and summed in bfloat16 or wider, within the bound.
A program may use at most 192 MiB of HBM per device.

```python
import jax
import jax.numpy as jnp
from jax import lax

D = 768
HEADS = 12
HD = 64
FF = 3072
P_SIZE = 256
IMG_DEV = 6
IMGS = 24
N_DP = 4


def draw_lengths(key, part):
    key = jax.random.fold_in(key, 5)
    first_key, second_key, third_key = jax.random.split(key, 3)
    dropped = jax.random.randint(first_key, (IMGS,), 0, P_SIZE // 2)
    divisor = jax.random.randint(second_key, (IMGS,), 1, 9)
    shortened = P_SIZE - dropped // (divisor * divisor)
    full_image = jax.random.randint(third_key, (), 0, IMGS)
    return jnp.where(jnp.arange(IMGS) == full_image, P_SIZE, shortened).astype(jnp.int32)


def draw_norms(key, part):
    key = jax.random.fold_in(key, 11)
    base = jnp.clip(jax.random.normal(key, (2, 8, D), jnp.float32), -3.0, 3.0)
    row_kind = (jnp.arange(8) % 4)[None, :, None]
    gains = 1.0 + 0.2 * base
    shifts = 0.3 * base
    scales = 0.6 + 0.8 * jax.nn.sigmoid(base)
    return jnp.where(row_kind == 0, gains, jnp.where(row_kind == 3, scales, shifts)).astype(jnp.float32)


def with_ends(result, key, least, high):
    shape = result.shape
    spot = [jax.random.randint(jax.random.fold_in(key, axis), (), 0, shape[axis]) for axis in range(len(shape))]
    result = result.at[tuple(spot)].set(least)
    longest = shape.index(max(shape))
    spot[longest] = (spot[longest] + 1) % shape[longest]
    return result.at[tuple(spot)].set(high)


def level_of(stream_key, shape, cuts, low, top_value):
    def one(axis_at, blocks):
        steps = jax.random.uniform(jax.random.fold_in(jax.random.fold_in(stream_key, 6), axis_at), (blocks,), jnp.float32, low / len(cuts), top_value / len(cuts))
        return jnp.repeat(jnp.exp(steps), shape[axis_at] // blocks).reshape((-1,) + (1,) * (len(shape) - axis_at - 1))

    loudness = one(*cuts[0])
    for cut in cuts[1:]:
        loudness = loudness * one(*cut)
    return loudness


def bell_draw(key, shape, scale, most, cuts=(), held_as=jnp.bfloat16):
    entries = jax.random.normal(key, shape, jnp.float32) * scale
    if len(cuts) > 0:
        entries = level_of(key, shape, cuts, -0.22, 0.18) * entries
    return jnp.clip(entries, min=-most, max=most).astype(held_as)


def setup_inputs(seed: int = 0) -> dict:
    arg_keys = jax.random.split(jax.random.key(seed), 12)
    block_in = bell_draw(arg_keys[0], (2, IMGS, P_SIZE, D), 1.0, 6.0, ((0, 2), (1, 4), (2, 4)))
    lengths = draw_lengths(jax.random.fold_in(arg_keys[11], 71), 0)
    patch_mask = with_ends((jax.random.randint(arg_keys[2], (IMGS, P_SIZE), 0, 2) < 1).astype(jnp.int32), jax.random.fold_in(arg_keys[2], 1), 0, 1)
    pred_grad = bell_draw(arg_keys[3], (IMGS, P_SIZE, D), 1.0, 6.0, ((0, 4), (1, 4)))
    w_qkv = bell_draw(arg_keys[4], (2, 3, D, D), D ** -0.5, 0.21875, ((0, 2), (3, 4)))
    w_out = bell_draw(arg_keys[5], (2, D, D), (D // 16) ** -0.5, 0.875, ((0, 2), (1, 4)))
    w_up = bell_draw(arg_keys[6], (2, D, FF), D ** -0.5, 0.21875, ((0, 2), (2, 4)))
    w_down = bell_draw(arg_keys[7], (2, FF, D), FF ** -0.5, 0.109375, ((0, 2), (1, 4)))
    qv_bias = bell_draw(arg_keys[8], (2, 2, D), 0.3, 1.8, ((0, 2), (2, 4)), jnp.float32)
    mlp_bias = bell_draw(arg_keys[9], (2, FF), 0.3, 1.8, ((0, 2), (1, 4)), jnp.float32)
    norms = draw_norms(jax.random.fold_in(arg_keys[11], 71), 0)
    return {"block_in": block_in, "lengths": lengths, "patch_mask": patch_mask, "pred_grad": pred_grad, "w_qkv": w_qkv, "w_out": w_out, "w_up": w_up, "w_down": w_down, "qv_bias": qv_bias, "mlp_bias": mlp_bias, "norms": norms}


@jax.custom_vjp
def low(v):
    return lax.optimization_barrier(v.astype(jnp.bfloat16)).astype(jnp.float32)

@jax.custom_vjp
def low_back(v):
    return v

def low_keep(v):
    return (low(v), None)

def low_pass(kept, grad):
    return (grad,)

def back_keep(v):
    return (v, None)

def back_low(kept, grad):
    return (low(grad),)
low.defvjp(low_keep, low_pass)
low_back.defvjp(back_keep, back_low)
norm_epsilon = 1e-06
masked_score = -1000000000.0
highest = lax.Precision.HIGHEST

def layer_norm(tensor_in, norm_gain, norm_shift):
    row_mean = lax.optimization_barrier(jnp.mean(tensor_in, axis=-1, keepdims=True))
    centred = tensor_in - row_mean
    spread = lax.optimization_barrier(jnp.mean(centred * centred, axis=-1, keepdims=True))
    return centred * lax.rsqrt(spread + norm_epsilon) * norm_gain + norm_shift

def product(left_side, right_side):
    return jnp.einsum('bpd,df->bpf', left_side, right_side, precision=highest)

def layer_block(inputs, extra_rows, weights, key_ok):
    w_qkv, w_out, w_up, w_down, qv_bias, mlp_bias, norms = weights
    images = inputs.shape[0]
    normed = low(layer_norm(inputs, norms[0], norms[1]))
    normed_extra = low(layer_norm(extra_rows, norms[0], norms[1]))
    key_input = jnp.concatenate([normed_extra, normed], axis=1)
    queries = low(low_back(product(normed, w_qkv[0])) + qv_bias[0]).reshape(images, P_SIZE, HEADS, HD)
    keys_low = low(low_back(product(key_input, w_qkv[1]))).reshape(images, 2 * P_SIZE, HEADS, HD)
    values = low(low_back(product(key_input, w_qkv[2])) + qv_bias[1]).reshape(images, 2 * P_SIZE, HEADS, HD)
    raw_scores = low_back(jnp.einsum('bqhd,bkhd->bhqk', queries, keys_low, precision=highest))
    scores = jnp.where(key_ok[:, None], raw_scores * HD ** (-0.5), masked_score)
    row_top = lax.optimization_barrier(jnp.max(scores, axis=-1, keepdims=True))
    exponent = jnp.exp(scores - row_top)
    attention = low(exponent / lax.optimization_barrier(jnp.sum(exponent, axis=-1, keepdims=True)))
    mixed_low = low(low_back(jnp.einsum('bhqk,bkhd->bqhd', attention, values, precision=highest)))
    attended = low_back(product(mixed_low.reshape(images, P_SIZE, D), w_out)) + norms[2]
    middle = inputs + norms[3] * attended
    normed_mid = low(layer_norm(middle, norms[4], norms[5]))
    hidden = low(jax.nn.gelu(low_back(product(normed_mid, w_up)) + mlp_bias, approximate=False))
    return middle + norms[7] * (low_back(product(hidden, w_down)) + norms[6])

def reference(block_in, lengths, patch_mask, pred_grad, w_qkv, w_out, w_up, w_down, qv_bias, mlp_bias, norms):
    positions = jnp.arange(P_SIZE, dtype=jnp.int32)
    is_valid = positions[None, :] < lengths[:, None]
    is_seen = is_valid & (patch_mask > 0)
    covered = is_valid & (patch_mask == 0)
    params = [tensor_in.astype(jnp.float32) for tensor_in in (w_qkv, w_out, w_up, w_down, qv_bias, mlp_bias, norms)]
    encoder_w = tuple((weight_arr[0] for weight_arr in params))
    regressor_w = tuple((weight_arr[1] for weight_arr in params))
    inputs = block_in.astype(jnp.float32)

    def by_block(tensor_in):
        return tensor_in.reshape((N_DP, IMG_DEV) + tensor_in.shape[1:])

    def forward(patches, queries, encoder_p, regressor_p):

        def image_block(carried, pieces):
            patch_rows, query_rows, seen_rows, valid_rows, cover_rows = pieces
            images = patch_rows.shape[0]
            nothing = jnp.zeros((images, P_SIZE, P_SIZE), dtype=bool)
            same_group = valid_rows[:, None, :] & (seen_rows[:, :, None] == seen_rows[:, None, :])
            encoder_ok = jnp.concatenate([nothing, same_group], axis=-1)
            regressor_ok = jnp.concatenate([jnp.broadcast_to(seen_rows[:, None, :], (images, P_SIZE, P_SIZE)), jnp.broadcast_to(cover_rows[:, None, :], (images, P_SIZE, P_SIZE))], axis=-1)
            seen_float = seen_rows[..., None].astype(patch_rows.dtype)
            cover_float = cover_rows[..., None].astype(patch_rows.dtype)
            encoded = layer_block(patch_rows, jnp.zeros_like(patch_rows), encoder_p, encoder_ok)
            latent = low_back(low(encoded * seen_float))
            predicted = layer_block(query_rows, latent, regressor_p, regressor_ok) * cover_float
            return (carried, (predicted, encoded * cover_float))
        carried, (predicted, target) = lax.scan(jax.checkpoint(image_block), jnp.float32(0), (by_block(patches), by_block(queries), by_block(is_seen), by_block(is_valid), by_block(covered)))
        return (predicted.reshape(IMGS, P_SIZE, D), target.reshape(IMGS, P_SIZE, D))
    outputs, pullback = jax.vjp(forward, inputs[0], inputs[1], encoder_w, regressor_w)
    predicted, target = outputs
    gradients = pullback((pred_grad.astype(jnp.float32), jnp.zeros_like(target)))
    results = jnp.stack([target, predicted]).astype(jnp.bfloat16)
    grad_in = jnp.stack([gradients[0], gradients[1]])
    stacked = [jnp.stack([enc_grad, reg_grad]) for enc_grad, reg_grad in zip(gradients[2], gradients[3])]
    return (results, grad_in, stacked[0], stacked[1], stacked[2], stacked[3], stacked[4], stacked[5], stacked[6])
```

```python
import functools

import jax
import jax.numpy as jnp
from jax import lax
from jax.experimental import pallas as pl
from jax.experimental.pallas import tpu as pltpu
from jax.sharding import PartitionSpec as P

HD = 64
CH = 128
EPS = 1e-06
MASKED = -1000000000.0
F32 = jnp.float32
BF16 = jnp.bfloat16


class Places:
    def __init__(self):
        self.count = 0

    def take(self, many=1):
        first = self.count
        self.count += many
        return first


def nn(a, b):
    return lax.dot_general(a, b, (((1,), (0,)), ((), ())), preferred_element_type=F32)


def nt(a, b):
    return lax.dot_general(a, b, (((1,), (1,)), ((), ())), preferred_element_type=F32)


def tn(a, b):
    return lax.dot_general(a, b, (((0,), (0,)), ((), ())), preferred_element_type=F32)


def normal(u):
    mean = jnp.mean(u, axis=-1, keepdims=True)
    centred = u - mean
    spread = jnp.mean(centred * centred, axis=-1, keepdims=True)
    inverse = lax.rsqrt(spread + EPS)
    return centred * inverse, inverse


def normal_back(hat, inverse, grad):
    first = jnp.mean(grad, axis=-1, keepdims=True)
    second = jnp.mean(grad * hat, axis=-1, keepdims=True)
    return inverse * (grad - first - hat * second)


def column_sum(u):
    return jnp.sum(u, axis=0, keepdims=True)


class Sizes:
    def __init__(self, n_dp, images, slots, width, piece):
        self.n_dp = n_dp
        self.images = images
        self.slots = slots
        self.width = width
        self.piece = piece
        self.block = 2 * slots
        self.rows = images * self.block
        self.pair = 2 * piece
        self.heads = self.pair // HD
        self.parts = 3 * width // CH


def plan(z):
    p = Places()
    half = z.width // 2 // CH
    s = dict(
        x=p.take(), bias=p.take(), xc0=p.take(), xc1=p.take(), pg=p.take(),
        wy=p.take(3 * half), wz=p.take(3 * half),
        e=p.take(z.images), ec=p.take(z.images),
        attn=p.take(), h2=p.take(), br=p.take(), dbl=p.take(), dh2=p.take(), dal=p.take(), dn=p.take(),
        dlat=p.take(z.images), res=p.take(), gin=p.take(),
        gy=p.take(z.parts), ga=p.take(z.parts), gb=p.take(z.parts),
        sy=p.take(), sc=p.take(), sa=p.take(), sb=p.take(),
    )
    return s, p.count


def body(
    z, S,
    x_ref, pg_ref, wa_ref, wu_ref, wd_ref, bias_ref, norm_ref, col_ref, key_ref,
    res_ref, gin_ref, grad_ref, small_ref,
    wy, xall, pgr, br_bias, e_own, e_oth, h, kv, q, kk, vv, o, p, att, mid, h2, act, gp, brv, dy,
    snd, rcv, dbl, dal, dol, dq, dk, dv, g, yr, za, zb, dlat, outb, nacc, sml, small_in,
    ss, rs, ls,
):
    sec = lax.axis_index("section")
    dp = lax.axis_index("dp")
    t = lax.axis_index("tensor")
    y = t // 2
    c = t % 2
    to_y = {"tensor": 2 * (1 - y) + c}
    to_c = {"tensor": 2 * y + 1 - c}
    to_s = {"section": 1 - sec}
    pair_z = {"dp": dp + 1 - 2 * (dp % 2)}
    top = dp // (z.n_dp // 2)
    to_m = {"dp": dp + 1 - 2 * top}
    to_w = {"dp": dp - 1 + 2 * top}
    is_end = jnp.logical_or(dp == 0, dp == z.n_dp - 1)
    not_end = jnp.logical_not(is_end)
    is_mid = jnp.logical_or(dp == z.n_dp // 2 - 1, dp == z.n_dp // 2)
    not_mid = jnp.logical_not(is_mid)
    enc = sec == 0
    reg = sec == 1

    I, R, D, BL, SL = z.images, z.rows, z.width, z.block, z.slots
    PC, PW = z.piece, z.pair
    HALF = D // 2
    NH = HALF // CH
    KEYS = 2 * BL

    def far(src, dst, number, to, receive=None):
        return pltpu.make_async_remote_copy(
            src_ref=src, dst_ref=dst, send_sem=ss.at[number],
            recv_sem=rs.at[number if receive is None else receive],
            device_id=to, device_id_type=pl.DeviceIdType.MESH,
        )

    barrier = pltpu.get_barrier_semaphore()

    def greet(to):
        pl.semaphore_signal(barrier, inc=1, device_id=to, device_id_type=pl.DeviceIdType.MESH)

    greet(to_y)
    greet(to_c)
    greet(to_s)
    greet(to_m)

    @pl.when(not_end)
    def _():
        greet(to_w)
        pl.semaphore_wait(barrier, 5)

    @pl.when(is_end)
    def _():
        pl.semaphore_wait(barrier, 4)

    c_x = far(x_ref.at[1 - y], xall.at[0, :, 1], S["x"], to_y)
    c_x.start()
    c_bias = far(bias_ref, br_bias, S["bias"], to_y)
    c_bias.start()
    c_xc0 = far(x_ref.at[y], xall.at[1, :, 0], S["xc0"], to_c)
    c_xc0.start()
    own_w = (wa_ref, wu_ref, wd_ref)
    parity = dp % 2

    def rows_of(m, k, mine):
        which = parity if mine else 1 - parity
        return pl.ds(pl.multiple_of(which * HALF + k * CH, CH), CH)

    def w_y(m, k):
        at = rows_of(m, k, True)
        return far(own_w[m].at[at], wy.at[m, at], S["wy"] + m * NH + k, to_y)

    def w_z(m, k):
        at = rows_of(m, k, True)
        return far(wy.at[m, at], wy.at[m, at], S["wz"] + m * NH + k, pair_z)

    for m in range(3):
        for k in range(NH):
            w_y(m, k).start()
    c_pg = far(pg_ref.at[1 - y], pgr, S["pg"], to_y)
    c_pg.start()

    def forward_w(m):
        for k in range(NH):
            w_y(m, k).wait_recv()
            w_z(m, k).start()

    def finish_w(m):
        for k in range(NH):
            w_z(m, k).wait_recv()

    g0, b0 = norm_ref[0:1, :], norm_ref[1:2, :]

    def lay(block):
        return block.reshape(BL, D)

    xall[0, :, 0] = x_ref[y]
    c_x.wait_recv()
    c_xc1 = far(xall.at[0, :, 1], xall.at[1, :, 1], S["xc1"], to_c)
    c_xc1.start()

    def norm_rows(half):
        def one(i, carry):
            hat, _ = normal(lay(xall[half, i]).astype(F32))
            value = (hat * g0 + b0).astype(BF16)
            h[half, i] = value
            kv[half, i] = value
            return carry

        lax.fori_loop(0, I, one, 0)

    norm_rows(0)
    c_xc0.wait_recv()
    c_xc1.wait_recv()
    norm_rows(1)
    forward_w(0)
    c_bias.wait_recv()
    finish_w(0)
    forward_w(1)
    forward_w(2)

    def both_rows(first, many):
        return jnp.concatenate([wa_ref[first:first + many], wy[0, first:first + many]], axis=0)

    bq = bias_ref[0:1, 0:PW] + br_bias[1:2, 0:PW]
    bv = bias_ref[2:3, 0:PW] + br_bias[3:4, 0:PW]

    def flat(ref, half):
        return ref[half].reshape(R, ref.shape[-1])

    def e_hop(i):
        return far(dlat.at[0, i], e_own.at[i], S["e"] + i, to_s)

    def e_core(i):
        return far(e_own.at[i], e_oth.at[i], S["ec"] + i, to_c)

    @pl.when(reg)
    def _():
        def take(half, ref, i):
            hat, _ = normal(ref[i].astype(F32))
            value = (hat * g0 + b0).astype(BF16)
            seen = col_ref[half, i][:, 1:2] > 0.5
            kv[half, i] = jnp.where(seen, value, h[half, i])

        for i in range(I):
            e_hop(i).wait_recv()
            e_core(i).start()
            take(0, e_own, i)
        for i in range(I):
            e_core(i).wait_recv()
            take(1, e_oth, i)

    for half in range(2):
        rows_h = flat(h, half)
        rows_k = flat(kv, half)
        q[half] = ((nt(rows_h, both_rows(0, PC)) + bq).astype(BF16) * 0.125).reshape(I, BL, PW)
        kk[half] = nt(rows_k, both_rows(PC, PC)).astype(BF16).reshape(I, BL, PW)
        vv[half] = (nt(rows_k, both_rows(2 * PC, PC)) + bv).astype(BF16).reshape(I, BL, PW)

    lane = lax.broadcasted_iota(jnp.int32, (KEYS, 2 * HD), 1)
    lanes = (lane < HD, lane >= HD)
    zero16 = jnp.zeros((KEYS, 2 * HD), BF16)

    def image(ref, i, pr):
        at = slice(pr * 2 * HD, (pr + 1) * 2 * HD)
        return jnp.concatenate([ref[0, i, :, at], ref[1, i, :, at]], axis=0)

    def put(ref, i, pr, value):
        at = slice(pr * 2 * HD, (pr + 1) * 2 * HD)
        ref[0, i, :, at] = value[:BL]
        ref[1, i, :, at] = value[BL:]

    def attend(i, carry):
        codes = jnp.concatenate([col_ref[0, i][:, 0:1], col_ref[1, i][:, 0:1]], axis=0)
        shut = jnp.where(codes == key_ref[i], 0.0, MASKED)
        for pr in range(z.heads // 2):
            qp, kp, vp = image(q, i, pr), image(kk, i, pr), image(vv, i, pr)
            outs = []
            for sub in range(2):
                scores = nt(jnp.where(lanes[sub], qp, zero16), kp) + shut
                top_value = jnp.max(scores, axis=-1, keepdims=True)
                e = jnp.exp(scores - top_value)
                probs = (e * (1.0 / jnp.sum(e, axis=-1, keepdims=True))).astype(BF16)
                p[i, 2 * pr + sub] = probs
                outs.append(nn(probs, vp))
            put(o, i, pr, jnp.where(lanes[0], outs[0], outs[1]).astype(BF16))
        return carry

    lax.fori_loop(0, I, attend, 0)

    w_o = both_rows(3 * PC, PC)

    def exchange(slot, buffer, number):
        return far(snd.at[buffer], rcv.at[slot], number, to_c)

    snd[0] = nn(flat(o, 1), w_o).astype(BF16).reshape(I, BL, D)
    c_attn = exchange(0, 0, S["attn"])
    c_attn.start()
    att[...] = nn(flat(o, 0), w_o).reshape(I, BL, D)
    c_attn.wait_recv()

    def middle(i, carry):
        attn = att[i] + rcv[0, i].astype(F32) + norm_ref[2:3, :]
        att[i] = attn
        value = lay(xall[0, i]).astype(F32) + norm_ref[3:4, :] * attn
        mid[i] = value
        hat, _ = normal(value)
        h2[0, i] = (hat * norm_ref[4:5, :] + norm_ref[5:6, :]).astype(BF16)
        return carry

    lax.fori_loop(0, I, middle, 0)
    c_h2 = far(h2.at[0], h2.at[1], S["h2"], to_c)
    c_h2.start()

    TW = 256
    NT = D // TW

    def up(half, w, w_ref, b_row):
        rows2 = flat(h2, half)

        def one(n, carry):
            at = pl.ds(pl.multiple_of(n * TW, TW), TW)
            u = nn(rows2, w_ref[:, at]) + b_row[:, at]
            cdf = 0.5 + 0.5 * lax.erf(u * 0.7071067811865476)
            act[w, half, :, at] = (u * cdf).astype(BF16)
            gp[w, half, :, at] = (cdf + u * (0.3989422804014327 * jnp.exp(-0.5 * u * u))).astype(BF16)
            return carry

        lax.fori_loop(0, NT, one, 0)

    up(0, 0, wu_ref, bias_ref.at[4:5])
    c_h2.wait_recv()
    up(1, 0, wu_ref, bias_ref.at[4:5])
    finish_w(1)
    up(0, 1, wy.at[1], br_bias.at[4:5])
    up(1, 1, wy.at[1], br_bias.at[4:5])
    finish_w(2)

    def down(half):
        rows0, rows1 = act[0, half], act[1, half]
        return nn(rows0, wd_ref[...]) + nn(rows1, wy[2])

    snd[1] = down(1).astype(BF16).reshape(I, BL, D)
    c_br = exchange(1, 1, S["br"])
    c_br.start()
    brv[...] = down(0).reshape(I, BL, D)
    c_br.wait_recv()

    def finish(i):
        br = brv[i] + rcv[1, i].astype(F32) + norm_ref[6:7, :]
        brv[i] = br
        out = mid[i] + norm_ref[7:8, :] * br
        dlat[0, i] = (out * col_ref[0, i][:, 1:2]).astype(BF16)

        @pl.when(enc)
        def _():
            e_hop(i).start()

        outb[0, i] = (out * col_ref[0, i][:, 2:3]).astype(BF16).reshape(2, SL, D)

    for i in range(I):
        finish(i)

    def deliver(which, number, ref):
        return (
            pltpu.make_async_copy(outb.at[which, :, 0], ref.at[y], ls.at[z.parts + which]),
            far(outb.at[which, :, 1], ref.at[y], S[number], to_y),
        )

    for copy in deliver(0, "res", res_ref):
        copy.start()

    nacc[...] = jnp.zeros_like(nacc)

    def add_norm(row, value):
        nacc[row:row + 1, :] += value

    def d_hop(i):
        return far(dlat.at[0, i], dlat.at[1, i], S["dlat"] + i, to_s)

    c_pg.wait_recv()

    def start_back(i, carry):
        grad = dy[i]
        add_norm(7, column_sum(grad * brv[i]))
        d_branch = norm_ref[7:8, :] * grad
        add_norm(6, column_sum(d_branch))
        dbl[0, i] = d_branch.astype(BF16)
        return carry

    @pl.when(reg)
    def _():
        for i in range(I):
            dy[i] = jnp.concatenate([pg_ref[y, i], pgr[i]], axis=0).astype(F32) * col_ref[0, i][:, 2:3]

    @pl.when(enc)
    def _():
        for i in range(I):
            d_hop(i).wait_recv()
            dy[i] = dlat[1, i].astype(F32) * col_ref[0, i][:, 1:2]

    lax.fori_loop(0, I, start_back, 0)
    c_dbl = far(dbl.at[0], dbl.at[1], S["dbl"], to_c)
    c_dbl.start()

    small_in[...] = jnp.zeros_like(small_in)

    def down_back(half, w, w_ref):
        rows = flat(dbl, half)

        def one(n, carry):
            at = pl.ds(pl.multiple_of(n * TW, TW), TW)
            du = nt(rows, w_ref[at, :]) * gp[w, half, :, at].astype(F32)
            small_in[8 + w:9 + w, at] += column_sum(du)
            gp[w, half, :, at] = du.astype(BF16)
            return carry

        lax.fori_loop(0, NT, one, 0)

    def y_part(k):
        at = pl.ds(pl.multiple_of(k * CH, CH), CH)
        return far(g.at[1, at], yr.at[at], S["gy"] + k, to_y)

    first_down, first_up, first_attn = 0, D // CH, 2 * D // CH

    def outer_rows(left, right, w, first, tile):
        def one(n, carry):
            at = pl.ds(pl.multiple_of(n * tile, tile), tile)
            to = pl.ds(pl.multiple_of(first * CH + n * tile, tile), tile)
            g[w, to, :] = tn(left(at), right()).astype(BF16)
            return carry

        lax.fori_loop(0, D // tile, one, 0)

    def wide(ref, w):
        return lambda at: ref[w, :, :, at].reshape(2 * R, at.size)

    down_back(0, 1, wy.at[2])
    down_back(0, 0, wd_ref)
    c_dbl.wait_recv()
    outer_rows(wide(act, 1), lambda: dbl[...].reshape(2 * R, D), 1, first_down, TW)
    for k in range(first_down, first_up):
        y_part(k).start()
    down_back(1, 1, wy.at[2])
    down_back(1, 0, wd_ref)

    def up_back(half):
        return nt(gp[0, half], wu_ref[...]) + nt(gp[1, half], wy[1])

    c_attn.wait_send()
    snd[0] = up_back(1).astype(BF16).reshape(I, BL, D)
    c_dh2 = exchange(2, 0, S["dh2"])
    c_dh2.start()

    def h2_cols(at):
        return jnp.concatenate(
            [h2[0, :, :, at].reshape(R, at.size), h2[1, :, :, at].reshape(R, at.size)], axis=0
        )

    outer_rows(h2_cols, lambda: gp[1].reshape(2 * R, D), 1, first_up, TW)
    for k in range(first_up, first_attn):
        y_part(k).start()
    back0 = up_back(0).reshape(I, BL, D)
    c_dh2.wait_recv()

    att_rows = []
    for i in range(I):
        grad = back0[i] + rcv[2, i].astype(F32)
        hat, inverse = normal(mid[i])
        add_norm(4, column_sum(grad * hat))
        add_norm(5, column_sum(grad))
        d_mid = dy[i] + normal_back(hat, inverse, grad * norm_ref[4:5, :])
        dy[i] = d_mid
        add_norm(3, column_sum(d_mid * att[i]))
        d_att = norm_ref[3:4, :] * d_mid
        add_norm(2, column_sum(d_att))
        dal[0, i] = d_att.astype(BF16)
    c_dal = far(dal.at[0], dal.at[1], S["dal"], to_c)
    c_dal.start()
    outer_rows(wide(act, 0), lambda: dbl[...].reshape(2 * R, D), 0, first_down, TW)
    outer_rows(h2_cols, lambda: gp[0].reshape(2 * R, D), 0, first_up, TW)

    dol[0] = nt(flat(dal, 0), w_o).astype(BF16).reshape(I, BL, PW)
    c_dal.wait_recv()
    dol[1] = nt(flat(dal, 1), w_o).astype(BF16).reshape(I, BL, PW)

    def all_rows(ref):
        return ref[...].reshape(2 * R, ref.shape[-1])

    base = first_attn * CH

    def store_rows(value, first):
        g[0, base + first:base + first + PC, :] = value[:PC].astype(BF16)
        g[1, base + first:base + first + PC, :] = value[PC:].astype(BF16)

    def attend_back(i, carry):
        for pr in range(z.heads // 2):
            qp, kp, vp, gpair = image(q, i, pr), image(kk, i, pr), image(vv, i, pr), image(dol, i, pr)
            at = slice(pr * 2 * HD, (pr + 1) * 2 * HD)
            dqs, dks, dvs = [], [], []
            for sub in range(2):
                probs = p[i, 2 * pr + sub]
                wide_probs = probs.astype(F32)
                d_probs = nt(jnp.where(lanes[sub], gpair, zero16), vp)
                dvs.append(tn(probs, gpair))
                inner = jnp.sum(d_probs * wide_probs, axis=-1, keepdims=True)
                ds = (wide_probs * (d_probs - inner)).astype(BF16)
                dqs.append(nn(ds, kp))
                dks.append(tn(ds, qp))
            d_q = jnp.where(lanes[0], dqs[0], dqs[1]) * 0.125
            d_k = jnp.where(lanes[0], dks[0], dks[1])
            d_v = jnp.where(lanes[0], dvs[0], dvs[1])
            small_in[10:11, at] += column_sum(d_q)
            small_in[11:12, at] += column_sum(d_v)
            put(dq, i, pr, d_q.astype(BF16))
            put(dk, i, pr, d_k.astype(BF16))
            put(dv, i, pr, d_v.astype(BF16))
        return carry

    lax.fori_loop(0, I, attend_back, 0)

    def input_back(half):
        return (
            nn(flat(dq, half), both_rows(0, PC))
            + nn(flat(dk, half), both_rows(PC, PC))
            + nn(flat(dv, half), both_rows(2 * PC, PC))
        )

    c_br.wait_send()
    snd[1] = input_back(1).astype(BF16).reshape(I, BL, D)
    c_dn = exchange(3, 1, S["dn"])
    c_dn.start()
    back1 = input_back(0).reshape(I, BL, D)
    c_dn.wait_recv()
    for i in range(I):
        grad = back1[i] + rcv[3, i].astype(F32)
        seen = col_ref[0, i][:, 1:2]
        extra = jnp.logical_and(seen > 0.5, reg)
        own = jnp.where(extra, 0.0, grad)
        hat, inverse = normal(lay(xall[0, i]).astype(F32))
        add_norm(0, column_sum(own * hat))
        add_norm(1, column_sum(own))
        d_x = dy[i] + normal_back(hat, inverse, own * g0)
        outb[1, i] = d_x.astype(BF16).reshape(2, SL, D)

        @pl.when(reg)
        def _():
            other = jnp.where(extra, grad, 0.0)
            hat, inverse = normal(e_own[i].astype(F32))
            add_norm(0, column_sum(other * hat))
            add_norm(1, column_sum(other))
            dlat[0, i] = normal_back(hat, inverse, other * g0).astype(BF16)
            d_hop(i).start()

    store_rows(tn(all_rows(dq), all_rows(h)), 0)
    store_rows(tn(all_rows(dk), all_rows(kv)), PC)
    store_rows(tn(all_rows(dv), all_rows(kv)), 2 * PC)
    store_rows(tn(all_rows(o), all_rows(dal)), 3 * PC)
    for k in range(first_attn, z.parts):
        y_part(k).start()
    for copy in deliver(1, "gin", gin_ref):
        copy.start()

    small_in[0:8, :] = nacc[...]
    c_sy = far(small_in, sml.at[0], S["sy"], to_y)
    c_sy.start()

    def part(k):
        return pl.ds(pl.multiple_of(k * CH, CH), CH)

    def to_middle(k, start):
        at = part(k)

        @pl.when(is_mid)
        def _():
            copy = far(g.at[0, at], zb.at[at], S["ga"] + k, to_m, S["gb"] + k)
            copy.start() if start else copy.wait_send()

        @pl.when(not_mid)
        def _():
            copy = far(g.at[0, at], za.at[at], S["ga"] + k, to_m)
            copy.start() if start else copy.wait_send()

    def from_away(k):
        at = part(k)
        return far(g.at[0, at], za.at[at], S["ga"] + k, to_w)

    def total(k):
        at = part(k)
        return far(zb.at[at], zb.at[at], S["gb"] + k, to_w)

    def stage0(k):
        at = part(k)
        y_part(k).wait_recv()
        g[0, at, :] = (g[0, at, :].astype(F32) + yr[at, :].astype(F32)).astype(BF16)

        @pl.when(is_end)
        def _():
            to_middle(k, True)

    def stage1(k):
        at = part(k)

        @pl.when(not_end)
        def _():
            from_away(k).wait_recv()
            g[0, at, :] = (g[0, at, :].astype(F32) + za[at, :].astype(F32)).astype(BF16)
            to_middle(k, True)

    def stage2(k):
        at = part(k)
        total(k).wait_recv()

        @pl.when(is_mid)
        def _():
            zb[at, :] = (g[0, at, :].astype(F32) + zb[at, :].astype(F32)).astype(BF16)

        @pl.when(not_end)
        def _():
            total(k).start()

        pltpu.make_async_copy(zb.at[at], grad_ref.at[at], ls.at[k]).start()

    N = z.parts

    def step(k, carry):
        @pl.when(k < N)
        def _():
            stage0(k)

        @pl.when(jnp.logical_and(k >= 1, k < N + 1))
        def _():
            stage1(k - 1)

        @pl.when(jnp.logical_and(is_mid, jnp.logical_and(k >= 2, k < N + 2)))
        def _():
            stage2(k - 2)

        @pl.when(jnp.logical_and(not_mid, k >= 4))
        def _():
            stage2(k - 4)

        return carry

    lax.fori_loop(0, N + 4, step, 0)

    c_sy.wait_recv()
    sml[1, 0:8, :] = small_in[0:8, :] + sml[0, 0:8, :]
    sml[1, 8:9, :] = small_in[8:9, :] + sml[0, 9:10, :]
    sml[1, 9:10, :] = jnp.zeros((1, D), F32)
    sml[1, 10:12, :] = small_in[10:12, :]
    sml[1, 12:14, :] = sml[0, 10:12, :]
    sml[1, 14:16, :] = jnp.zeros((2, D), F32)
    c_sc = far(sml.at[1], sml.at[2], S["sc"], to_c)
    c_sc.start()
    c_sc.wait()
    sml[1, 0:8, :] = sml[1, 0:8, :] + sml[2, 0:8, :]

    def small_middle(start):
        @pl.when(is_mid)
        def _():
            copy = far(sml.at[1], sml.at[4], S["sa"], to_m, S["sb"])
            copy.start() if start else copy.wait_send()

        @pl.when(not_mid)
        def _():
            copy = far(sml.at[1], sml.at[3], S["sa"], to_m)
            copy.start() if start else copy.wait_send()

    @pl.when(not_end)
    def _():
        far(sml.at[1], sml.at[3], S["sa"], to_w).wait_recv()
        sml[1] = sml[1] + sml[3]

    small_middle(True)
    s_total = far(sml.at[4], sml.at[4], S["sb"], to_w)
    s_total.wait_recv()

    @pl.when(is_mid)
    def _():
        sml[4] = sml[1] + sml[4]

    @pl.when(not_end)
    def _():
        s_total.start()

    small_ref[...] = sml[4]

    small_middle(False)

    @pl.when(not_end)
    def _():
        s_total.wait_send()

    c_sy.wait_send()

    def end_parts(k, carry):
        y_part(k).wait_send()
        to_middle(k, False)

        @pl.when(not_end)
        def _():
            total(k).wait_send()

        pltpu.make_async_copy(zb.at[part(k)], grad_ref.at[part(k)], ls.at[k]).wait()
        return carry

    lax.fori_loop(0, N, end_parts, 0)
    for which, number, ref in ((0, "res", res_ref), (1, "gin", gin_ref)):
        for copy in deliver(which, number, ref):
            copy.wait()
    for copy in (c_x, c_bias, c_xc0, c_xc1, c_pg, c_h2, c_dbl, c_dh2, c_dal, c_dn):
        copy.wait_send()
    for m in range(3):
        for k in range(NH):
            w_y(m, k).wait_send()
            w_z(m, k).wait_send()
    for i in range(I):
        @pl.when(enc)
        def _():
            e_hop(i).wait_send()

        @pl.when(reg)
        def _():
            e_core(i).wait_send()
            d_hop(i).wait_send()


def fused(z, x, pg, wa, wu, wd, bias, norms, cols, keys):
    places, count = plan(z)
    I, R, D, BL, SL = z.images, z.rows, z.width, z.block, z.slots
    PW = z.pair
    KEYS = 2 * BL
    vm = pl.BlockSpec(memory_space=pltpu.VMEM)
    hbm = pl.BlockSpec(memory_space=pl.ANY)

    def b16(*shape):
        return pltpu.VMEM(shape, BF16)

    def f32(*shape):
        return pltpu.VMEM(shape, F32)

    scratch = [
        b16(3, D, D),
        b16(2, I, 2, SL, D),
        b16(I, SL, D),
        f32(8, D),
        b16(I, BL, D), b16(I, BL, D),
        b16(2, I, BL, D), b16(2, I, BL, D),
        b16(2, I, BL, PW), b16(2, I, BL, PW), b16(2, I, BL, PW), b16(2, I, BL, PW),
        b16(I, z.heads, KEYS, KEYS),
        f32(I, BL, D), f32(I, BL, D),
        b16(2, I, BL, D),
        b16(2, 2, R, D), b16(2, 2, R, D),
        f32(I, BL, D), f32(I, BL, D),
        b16(2, I, BL, D), b16(4, I, BL, D),
        b16(2, I, BL, D), b16(2, I, BL, D),
        b16(2, I, BL, PW), b16(2, I, BL, PW), b16(2, I, BL, PW), b16(2, I, BL, PW),
        b16(2, 3 * D, D),
        b16(3 * D, D), b16(3 * D, D), b16(3 * D, D),
        b16(2, I, BL, D),
        b16(2, I, 2, SL, D),
        f32(8, D), f32(5, 16, D), f32(16, D),
        pltpu.SemaphoreType.DMA((count,)),
        pltpu.SemaphoreType.DMA((count,)),
        pltpu.SemaphoreType.DMA((z.parts + 2,)),
    ]
    return pl.pallas_call(
        functools.partial(body, z, places),
        out_shape=(
            jax.ShapeDtypeStruct((2, I, SL, D), BF16),
            jax.ShapeDtypeStruct((2, I, SL, D), BF16),
            jax.ShapeDtypeStruct((3 * D, D), BF16),
            jax.ShapeDtypeStruct((16, D), F32),
        ),
        in_specs=[vm] * 9,
        out_specs=(hbm, hbm, hbm, vm),
        scratch_shapes=scratch,
        compiler_params=pltpu.CompilerParams(
            collective_id=0, has_side_effects=True, vmem_limit_bytes=121 * 2**19
        ),
    )(x, pg, wa, wu, wd, bias, norms, cols, keys)


def local(
    n_dp,
    block_in, lengths, patch_mask, pred_grad, w_qkv, w_out, w_up, w_down, qv_bias, mlp_bias, norms
):
    sec = lax.axis_index("section")
    t = lax.axis_index("tensor")
    y = t // 2
    images, slots, width = block_in.shape[1:]
    piece = w_qkv.shape[3]
    z = Sizes(n_dp, images // 2, slots, width, piece)

    x = block_in[0].reshape(2, z.images, slots, width)
    pg = pred_grad.reshape(2, z.images, slots, width)
    wa = jnp.concatenate([jnp.swapaxes(w_qkv[0], 1, 2).reshape(3 * piece, width), w_out[0]], axis=0)

    flat_q = jnp.zeros((1, width), F32)
    q_row, v_row = qv_bias[0, 0:1], qv_bias[0, 1:2]
    pad = jnp.zeros((1, width - piece), F32)
    pad2 = jnp.zeros((1, width - 2 * piece), F32)
    gap = jnp.zeros((1, piece), F32)
    bias = jnp.concatenate(
        [
            jnp.concatenate([q_row, pad], 1), jnp.concatenate([gap, q_row, pad2], 1),
            jnp.concatenate([v_row, pad], 1), jnp.concatenate([gap, v_row, pad2], 1),
            mlp_bias, flat_q, flat_q, flat_q,
        ],
        axis=0,
    )

    chip_lengths = lax.dynamic_slice_in_dim(lengths, y * z.images, z.images, 0)
    chip_mask = lax.dynamic_slice_in_dim(patch_mask, y * z.images, z.images, 0)
    order = [t, 2 * (1 - y) + t % 2, 2 * y + 1 - t % 2, 2 * (1 - y) + 1 - t % 2]
    positions = jnp.concatenate([j * slots + jnp.arange(slots, dtype=jnp.int32) for j in order])
    mask = jnp.concatenate(
        [lax.dynamic_slice_in_dim(chip_mask, j * slots, slots, 1) for j in order], axis=1
    )
    valid = positions[None, :] < chip_lengths[:, None]
    seen = (valid & (mask > 0)).astype(F32)
    covered = (valid & (mask == 0)).astype(F32)
    code = jnp.where(sec == 0, seen, 0.0)
    keys = jnp.where(valid, code, 2.0)[:, None, :]
    cols = jnp.stack([code, seen, covered, covered], axis=-1)
    cols = cols.reshape(z.images, 2, z.block, 4).swapaxes(0, 1)

    res, gin, grads, small = fused(
        z, x, pg, wa, w_up[0], w_down[0], bias, norms[0], cols, keys
    )
    g_down, g_up, g_attn = grads[:width], grads[width:2 * width], grads[2 * width:]
    g_qkv = jnp.swapaxes(g_attn[:3 * piece].reshape(3, piece, width), 1, 2).astype(F32)
    g_qv = small[10:12, :piece] + small[12:14, piece:2 * piece]
    return (
        res.reshape(1, images, slots, width),
        gin.reshape(1, images, slots, width).astype(F32),
        g_qkv[None],
        g_attn[3 * piece:].astype(F32)[None],
        g_up.astype(F32)[None],
        g_down.astype(F32)[None],
        g_qv[None],
        small[8:9],
        small[0:8][None],
    )


def solution(mesh):
    return jax.shard_map(
        functools.partial(local, mesh.shape["dp"]),
        mesh=mesh,
        in_specs=(
            P("section", "dp", "tensor", None),
            P("dp"),
            P("dp", None),
            P("dp", "tensor", None),
            P("section", None, None, "tensor"),
            P("section", "tensor", None),
            P("section", None, "tensor"),
            P("section", "tensor", None),
            P("section", None, "tensor"),
            P("section", "tensor"),
            P("section", None, None),
        ),
        out_specs=(
            P("section", "dp", "tensor", None),
            P("section", "dp", "tensor", None),
            P("section", None, None, "tensor"),
            P("section", "tensor", None),
            P("section", None, "tensor"),
            P("section", "tensor", None),
            P("section", None, "tensor"),
            P("section", "tensor"),
            P("section", None, None),
        ),
        check_vma=False,
    )
```

```python
import functools

import jax
import jax.numpy as jnp
from jax import lax
from jax.experimental import pallas as pl
from jax.experimental.pallas import tpu as pltpu
from jax.sharding import PartitionSpec as P

HD = 64
CH = 128
GC = 64
AROUND = (2, 1, 1)
EPS = 1e-06
MASKED = -1000000000.0
F32 = jnp.float32
BF16 = jnp.bfloat16


class Places:
    def __init__(self):
        self.count = 0

    def take(self, many=1):
        first = self.count
        self.count += many
        return first


def nn(a, b):
    return lax.dot_general(a, b, (((1,), (0,)), ((), ())), preferred_element_type=F32)


def nt(a, b):
    return lax.dot_general(a, b, (((1,), (1,)), ((), ())), preferred_element_type=F32)


def tn(a, b):
    return lax.dot_general(a, b, (((0,), (0,)), ((), ())), preferred_element_type=F32)


def normal(u):
    mean = jnp.mean(u, axis=-1, keepdims=True)
    centred = u - mean
    spread = jnp.mean(centred * centred, axis=-1, keepdims=True)
    inverse = lax.rsqrt(spread + EPS)
    return centred * inverse, inverse


def normal_back(hat, inverse, grad):
    first = jnp.mean(grad, axis=-1, keepdims=True)
    second = jnp.mean(grad * hat, axis=-1, keepdims=True)
    return inverse * (grad - first - hat * second)


def column_sum(u):
    return jnp.sum(u, axis=0, keepdims=True)


class Sizes:
    def __init__(self, n_dp, images, slots, width, piece):
        self.n_dp = n_dp
        self.images = images
        self.slots = slots
        self.width = width
        self.piece = piece
        self.block = 2 * slots
        self.rows = images * self.block
        self.pair = 2 * piece
        self.heads = self.pair // HD
        self.around = sum(AROUND)
        self.per_mat = width // GC
        self.parts = 3 * self.per_mat


def plan(z):
    p, d, n = Places(), Places(), Places()
    pieces = z.width // CH
    recv = dict(
        x=p.take(), bias=p.take(2), xc0=p.take(), xc1=p.take(), pg=p.take(),
        wy=p.take(3 * pieces), wz=p.take(3 * pieces // 2),
        d1=p.take(z.around), d2=p.take(z.around),
        e=p.take(z.images), ec=p.take(z.images),
        attn=p.take(z.images), h2=p.take(z.images), br=p.take(z.images), dbl=p.take(z.images),
        dh2=p.take(), dal=p.take(), dn=p.take(z.images),
        dlat=p.take(z.images), res=p.take(), gin=p.take(),
        gy=p.take(z.parts), ga=p.take(z.parts), gb=p.take(z.parts),
        sy=p.take(), sc=p.take(), sa=p.take(), sb=p.take(),
    )
    together = ("wy", "wz", "d1", "gy", "ga", "gb", "attn", "h2", "br", "dbl", "e", "ec", "dlat", "dn")
    many = dict(bias=2, d2=z.around)
    send = {name: d.take(many.get(name, 1)) for name in recv}
    send["d3"] = d.take(z.around)
    local = {name: n.take() for name in ("w0", "w1", "w2", "x", "pg", "res", "gin", "g0", "g1", "g2")}
    return recv, send, frozenset(together), local, p.count, d.count, n.count


def body(
    z, places,
    x_ref, pg_ref, wa_ref, wu_ref, wd_ref, len_ref, mask_ref, qv_ref, mlp_ref, norm_ref,
    res_ref, gin_ref, gd_ref, gu_ref, ga_ref, small_ref,
    wown, wy, xall, pgr, qv_y, mlp_y, code_c, seen_c, cov_c, key_r,
    e_own, e_oth, h, kv, q, kk, vv, o, p, att, mid, h2, act, gp, brv, dy,
    snd, rcv, dbl, dal, dol, dq, dk, dv, g, yr, za, zb, dlat, outb, nacc, sml, small_in,
    ss, rs, ls,
):
    S, SEND, TOGETHER, LOCAL = places
    sec = lax.axis_index("section")
    dp = lax.axis_index("dp")
    t = lax.axis_index("tensor")
    y = t // 2
    c = t % 2
    to_y = {"tensor": 2 * (1 - y) + c}
    to_c = {"tensor": 2 * y + 1 - c}
    to_s = {"section": 1 - sec}
    parity = dp % 2
    pair_z = {"dp": dp + 1 - 2 * parity}
    top = dp // (z.n_dp // 2)
    to_m = {"dp": dp + 1 - 2 * top}
    to_w = {"dp": dp - 1 + 2 * top}
    is_end = jnp.logical_or(dp == 0, dp == z.n_dp - 1)
    not_end = jnp.logical_not(is_end)
    is_mid = jnp.logical_or(dp == z.n_dp // 2 - 1, dp == z.n_dp // 2)
    not_mid = jnp.logical_not(is_mid)
    enc = sec == 0
    reg = sec == 1

    I, R, D, BL, SL = z.images, z.rows, z.width, z.block, z.slots
    PC, PW = z.piece, z.pair
    KEYS = 2 * BL
    WP = D // CH
    HELP = (2, WP // 2)

    def far(src, dst, name, to, index=0, receive=None, send=None):
        leave = SEND[send or name] + (0 if name in TOGETHER else index)
        return pltpu.make_async_remote_copy(
            src_ref=src, dst_ref=dst, send_sem=ss.at[leave], recv_sem=rs.at[S[receive or name] + index],
            device_id=to, device_id_type=pl.DeviceIdType.MESH,
        )

    def gone(ref, name, to):
        far(ref, ref, name, to).wait_send()

    def here(src, dst, name):
        return pltpu.make_async_copy(src, dst, ls.at[LOCAL[name]])

    w_refs = (wa_ref, wu_ref, wd_ref)
    own_w = [here(w_refs[m], wown.at[m], ("w0", "w1", "w2")[m]) for m in range(3)]
    own_x = here(x_ref.at[y], xall.at[0, :, 0], "x")
    own_pg = here(pg_ref.at[y], pgr.at[0], "pg")
    own_x.start()
    for copy in own_w:
        copy.start()
    own_pg.start()

    barrier = pltpu.get_barrier_semaphore()

    def greet(to):
        pl.semaphore_signal(barrier, inc=1, device_id=to, device_id_type=pl.DeviceIdType.MESH)

    greet(to_y)
    greet(to_c)
    greet(to_s)
    greet(to_m)

    @pl.when(not_end)
    def _():
        greet(to_w)
        pl.semaphore_wait(barrier, 5)

    @pl.when(is_end)
    def _():
        pl.semaphore_wait(barrier, 4)

    c_x = far(x_ref.at[1 - y], xall.at[0, :, 1], "x", to_y)
    c_b0 = far(qv_ref, qv_y, "bias", to_y)
    c_b1 = far(mlp_ref, mlp_y, "bias", to_y, 1)
    c_xc0 = far(x_ref.at[y], xall.at[1, :, 0], "xc0", to_c)
    c_xc1 = far(xall.at[0, :, 1], xall.at[1, :, 1], "xc1", to_c)
    c_pg = far(pg_ref.at[1 - y], pgr.at[1], "pg", to_y)

    def rows_of(j, side):
        return pl.ds(pl.multiple_of((j + side * (WP - 1 - 2 * j)) * CH, CH), CH)

    def w_y(m, j):
        at = rows_of(j, parity)
        return far(w_refs[m].at[at], wy.at[m, at], "wy", to_y, m * WP + j)

    def w_z(m, j, side=None):
        at = rows_of(j, parity if side is None else side)
        return far(wy.at[m, at], wy.at[m, at], "wz", pair_z, m * (WP // 2) + j)

    around = [(m, WP - HELP[0] - 1 - j) for m in range(3) for j in range(AROUND[m] - 1, -1, -1)]

    def d_slot(side, n):
        return g.at[side, pl.ds(n * CH, CH)]

    def d_out(n):
        m, j = around[n]
        return far(w_refs[m].at[rows_of(j, parity)], d_slot(0, n), "d1", to_s, n)

    def d_over(n):
        return far(d_slot(0, n), d_slot(1, n), "d2", to_y, n)

    def d_back(n):
        m, j = around[n]
        leave = SEND["d3"] + n
        return pltpu.make_async_remote_copy(
            src_ref=d_slot(1, n), dst_ref=wy.at[m, rows_of(j, parity)],
            send_sem=ss.at[leave], recv_sem=rs.at[S["wy"] + m * WP + j],
            device_id=to_s, device_id_type=pl.DeviceIdType.MESH,
        )

    straight = (
        [[j for j in range(WP - HELP[0]) if (m, j) not in around] for m in range(3)],
        [list(range(WP - HELP[1])) for m in range(3)],
    )

    def start_inputs():
        c_x.start()
        c_b0.start()
        c_b1.start()
        c_xc0.start()

    @pl.when(enc)
    def _():
        for n in range(len(around)):
            d_out(n).start()
        start_inputs()
        for m in range(3):
            for j in straight[0][m]:
                w_y(m, j).start()

    @pl.when(reg)
    def _():
        for n in range(len(around) + 1):
            if n < len(around):
                d_out(n).wait_recv()
                d_over(n).start()
            if n > 0:
                d_over(n - 1).wait_recv()
                d_back(n - 1).start()
            if n == max(len(around) - 1, 0):
                start_inputs()
                for m in range(3):
                    for j in straight[1][m]:
                        w_y(m, j).start()
                c_pg.start()
        for n in range(len(around)):
            d_over(n).wait_send()
            d_back(n).wait_send()

    def forward_w(m, j):
        for s, flag in enumerate((enc, reg)):
            @pl.when(jnp.logical_and(flag, j < HELP[s]))
            def _():
                w_y(m, j).wait_recv()
                w_z(m, j).start()

    def finish_w(m):
        for s, flag in enumerate((enc, reg)):
            @pl.when(flag)
            def _():
                for j in range(HELP[s], WP - HELP[s]):
                    w_y(m, j).wait_recv()
                for j in range(HELP[s]):
                    w_z(m, j, 1 - parity).wait_recv()

    rank = lax.broadcasted_iota(jnp.int32, (KEYS, KEYS), 0)
    across = lax.broadcasted_iota(jnp.int32, (KEYS, KEYS), 1)
    group = rank // SL
    y_of = y + (group % 2) * (1 - 2 * y)
    c_of = c + (group // 2) * (1 - 2 * c)
    slot = (2 * y_of + c_of) * SL + rank % SL
    here_slot = slot == across
    diagonal = rank == across
    slot_col = slot[:, 0:1]
    for i in range(I):
        picked = jnp.where(here_slot, mask_ref[pl.ds(y * I + i, 1), :].astype(F32), 0.0)
        marked = jnp.sum(picked, axis=1, keepdims=True) > 0.5
        valid = slot_col < len_ref[y * I + i]
        seen = jnp.where(jnp.logical_and(valid, marked), 1.0, 0.0)
        code = jnp.where(enc, seen, jnp.zeros_like(seen))
        seen_c[i] = seen
        cov_c[i] = jnp.where(valid, 1.0, 0.0) - seen
        code_c[i] = code
        key = jnp.where(valid, code, 2.0)
        key_r[i] = jnp.sum(jnp.where(diagonal, key, 0.0), axis=0, keepdims=True)

    g0, b0 = norm_ref[0:1, :], norm_ref[1:2, :]

    def lay(block):
        return block.reshape(BL, D)

    own_x.wait()
    c_x.wait_recv()
    c_xc1.start()

    def norm_rows(half):
        def one(i, carry):
            hat, _ = normal(lay(xall[half, i]).astype(F32))
            value = (hat * g0 + b0).astype(BF16)
            h[half, i] = value
            kv[half, i] = value
            return carry

        lax.fori_loop(0, I, one, 0)

    norm_rows(0)
    c_xc0.wait_recv()
    c_xc1.wait_recv()
    norm_rows(1)
    for j in range(HELP[1]):
        forward_w(0, j)
    c_b0.wait_recv()
    c_b1.wait_recv()
    own_w[0].wait()
    finish_w(0)

    def both_rows(first, many):
        return jnp.concatenate([wown[0, first:first + many], wy[0, first:first + many]], axis=0)

    bq = jnp.concatenate([qv_ref[0:1, :], qv_y[0:1, :]], axis=1)
    bv = jnp.concatenate([qv_ref[1:2, :], qv_y[1:2, :]], axis=1)

    def flat(ref, half):
        return ref[half].reshape(R, ref.shape[-1])

    def e_hop(i):
        return far(dlat.at[0, i], e_own.at[i], "e", to_s, i)

    def e_core(i):
        return far(e_own.at[i], e_oth.at[i], "ec", to_c, i)

    for half in range(2):
        q[half] = ((nt(flat(h, half), both_rows(0, PC)) + bq).astype(BF16) * 0.125).reshape(I, BL, PW)

    lane = lax.broadcasted_iota(jnp.int32, (KEYS, 2 * HD), 1)
    lanes = (lane < HD, lane >= HD)
    zero16 = jnp.zeros((KEYS, 2 * HD), BF16)

    def image(ref, i, pr):
        at = slice(pr * 2 * HD, (pr + 1) * 2 * HD)
        return jnp.concatenate([ref[0, i, :, at], ref[1, i, :, at]], axis=0)

    def put(ref, i, pr, value):
        at = slice(pr * 2 * HD, (pr + 1) * 2 * HD)
        ref[0, i, :, at] = value[:BL]
        ref[1, i, :, at] = value[BL:]

    def latent_keys(half, ref, i):
        hat, _ = normal(ref[i].astype(F32))
        value = (hat * g0 + b0).astype(BF16)
        seen = seen_c[i, half * BL:(half + 1) * BL] > 0.5
        kv[half, i] = jnp.where(seen, value, h[half, i])

    def attend(i):
        @pl.when(reg)
        def _():
            e_hop(i).wait_recv()
            e_core(i).start()
            latent_keys(0, e_own, i)
            e_core(i).wait_recv()
            latent_keys(1, e_oth, i)

        rows_k = kv[:, i].reshape(KEYS, D)
        kk[:, i] = nt(rows_k, both_rows(PC, PC)).astype(BF16).reshape(2, BL, PW)
        vv[:, i] = (nt(rows_k, both_rows(2 * PC, PC)) + bv).astype(BF16).reshape(2, BL, PW)
        shut = jnp.where(code_c[i] == key_r[i], 0.0, MASKED)
        for pr in range(z.heads // 2):
            qp, kp, vp = image(q, i, pr), image(kk, i, pr), image(vv, i, pr)
            outs = []
            for sub in range(2):
                scores = nt(jnp.where(lanes[sub], qp, zero16), kp) + shut
                top_value = jnp.max(scores, axis=-1, keepdims=True)
                e = jnp.exp(scores - top_value)
                probs = (e * (1.0 / jnp.sum(e, axis=-1, keepdims=True))).astype(BF16)
                p[i, 2 * pr + sub] = probs
                outs.append(nn(probs, vp))
            put(o, i, pr, jnp.where(lanes[0], outs[0], outs[1]).astype(BF16))
        attn = nn(o[:, i].reshape(KEYS, PW), both_rows(3 * PC, PC))
        snd[0, i] = attn[BL:].astype(BF16)
        exchange(0, "attn", i).start()
        att[i] = attn[:BL]

    def exchange(slot, name, i):
        return far(snd.at[slot % 2, i], rcv.at[slot, i], name, to_c, i)

    def h2_core(i):
        return far(h2.at[0, i], h2.at[1, i], "h2", to_c, i)

    def middle(i):
        exchange(0, "attn", i).wait_recv()
        attn = att[i] + rcv[0, i].astype(F32) + norm_ref[2:3, :]
        att[i] = attn
        value = lay(xall[0, i]).astype(F32) + norm_ref[3:4, :] * attn
        mid[i] = value
        hat, _ = normal(value)
        h2[0, i] = (hat * norm_ref[4:5, :] + norm_ref[5:6, :]).astype(BF16)
        h2_core(i).start()

    TW = 256
    NT = D // TW

    def rows_at(i):
        return pl.ds(i * BL, BL)

    def up(i, w, w_ref, b_row):
        rows2 = h2[:, i].reshape(KEYS, D)

        def one(n, carry):
            at = pl.ds(pl.multiple_of(n * TW, TW), TW)
            u = nn(rows2, w_ref[:, at]) + b_row[:, at]
            cdf = 0.5 + 0.5 * lax.erf(u * 0.7071067811865476)
            act[w, :, rows_at(i), at] = (u * cdf).astype(BF16).reshape(2, BL, TW)
            slope = cdf + u * (0.3989422804014327 * jnp.exp(-0.5 * u * u))
            gp[w, :, rows_at(i), at] = slope.astype(BF16).reshape(2, BL, TW)
            return carry

        lax.fori_loop(0, NT, one, 0)

    def down(i):
        br = nn(act[0, :, rows_at(i)].reshape(KEYS, D), wown[2])
        br += nn(act[1, :, rows_at(i)].reshape(KEYS, D), wy[2])
        snd[1, i] = br[BL:].astype(BF16)
        exchange(1, "br", i).start()
        brv[i] = br[:BL]

    def finish(i):
        exchange(1, "br", i).wait_recv()
        br = brv[i] + rcv[1, i].astype(F32) + norm_ref[6:7, :]
        brv[i] = br
        out = mid[i] + norm_ref[7:8, :] * br

        @pl.when(enc)
        def _():
            dlat[0, i] = (out * seen_c[i, :BL]).astype(BF16)
            e_hop(i).start()

        outb[0, i] = (out * cov_c[i, :BL]).astype(BF16).reshape(2, SL, D)

    def own_up(i):
        h2_core(i).wait_recv()
        up(i, 0, wown.at[1], mlp_ref)

    def other_up(i):
        up(i, 1, wy.at[1], mlp_y)

    for i in range(I + 2):
        if i < I:
            attend(i)
            if i < 2:
                for j in range(i * HELP[1] // 2, (i + 1) * HELP[1] // 2):
                    forward_w(1, j)
            middle(i)
        if i == 1:
            own_w[1].wait()
        if 1 <= i <= I:
            own_up(i - 1)
            for j in range((i - 1) * HELP[1] // I, i * HELP[1] // I):
                forward_w(2, j)
            if i == 1:
                finish_w(1)
            other_up(i - 1)
        if i == I:
            own_w[2].wait()
            finish_w(2)
            for n in range(I - 1):
                down(n)
        if i == I + 1:
            down(I - 1)
            for n in range(I):
                finish(n)
    w_o = both_rows(3 * PC, PC)

    def deliver(which, number, ref):
        return (
            here(outb.at[which, :, 0], ref.at[y], number),
            far(outb.at[which, :, 1], ref.at[y], number, to_y),
        )

    for copy in deliver(0, "res", res_ref):
        copy.start()

    nacc[...] = jnp.zeros_like(nacc)
    small_in[...] = jnp.zeros_like(small_in)

    def add_norm(row, value):
        nacc[row:row + 1, :] += value

    def d_hop(i):
        return far(dlat.at[0, i], dlat.at[1, i], "dlat", to_s, i)

    def dbl_core(i):
        return far(dbl.at[0, i], dbl.at[1, i], "dbl", to_c, i)

    own_pg.wait()

    @pl.when(reg)
    def _():
        c_pg.wait_recv()

    def start_back(i, carry):
        @pl.when(reg)
        def _():
            dy[i] = jnp.concatenate([pgr[0, i], pgr[1, i]], axis=0).astype(F32) * cov_c[i, :BL]

        @pl.when(enc)
        def _():
            d_hop(i).wait_recv()
            dy[i] = dlat[1, i].astype(F32) * seen_c[i, :BL]

        grad = dy[i]
        d_branch = norm_ref[7:8, :] * grad
        dbl[0, i] = d_branch.astype(BF16)
        dbl_core(i).start()
        add_norm(7, column_sum(grad * brv[i]))
        add_norm(6, column_sum(d_branch))
        return carry

    lax.fori_loop(0, I, start_back, 0)
    for i in range(I):
        dbl_core(i).wait_recv()

    N = z.parts
    PM = z.per_mat

    def part(k):
        return pl.ds(pl.multiple_of(k * GC, GC), GC)

    def y_part(k):
        at = part(k)
        return far(g.at[1, at], yr.at[at], "gy", to_y, k)

    def to_middle(k):
        at = part(k)

        @pl.when(is_mid)
        def _():
            far(g.at[0, at], zb.at[at], "ga", to_m, k, receive="gb").start()

        @pl.when(not_mid)
        def _():
            far(g.at[0, at], za.at[at], "ga", to_m, k).start()

    def from_away(k):
        at = part(k)
        return far(g.at[0, at], za.at[at], "ga", to_w, k)

    def total(k):
        at = part(k)
        return far(zb.at[at], zb.at[at], "gb", to_w, k)

    def stage0(k):
        at = part(k)
        y_part(k).wait_recv()
        g[0, at, :] = (g[0, at, :].astype(F32) + yr[at, :].astype(F32)).astype(BF16)

        @pl.when(is_end)
        def _():
            to_middle(k)

    def stage1(k):
        at = part(k)

        @pl.when(not_end)
        def _():
            from_away(k).wait_recv()
            g[0, at, :] = (g[0, at, :].astype(F32) + za[at, :].astype(F32)).astype(BF16)
            to_middle(k)

    def each_out(k, do):
        for m, ref in enumerate((gd_ref, gu_ref, ga_ref)):
            @pl.when(jnp.logical_and(k >= m * PM, k < (m + 1) * PM))
            def _():
                do(here(zb.at[part(k)], ref.at[part(k - m * PM)], ("g0", "g1", "g2")[m]))

    def stage2(k):
        at = part(k)
        total(k).wait_recv()

        @pl.when(is_mid)
        def _():
            zb[at, :] = (g[0, at, :].astype(F32) + zb[at, :].astype(F32)).astype(BF16)

        @pl.when(not_end)
        def _():
            total(k).start()

        each_out(k, lambda copy: copy.start())

    AWAY_LAG = 2
    MID_LAG = 4
    LAG = 8

    def small_middle(start):
        @pl.when(is_mid)
        def _():
            copy = far(sml.at[1], sml.at[4], "sa", to_m, receive="sb")
            copy.start() if start else copy.wait_send()

        @pl.when(not_mid)
        def _():
            copy = far(sml.at[1], sml.at[3], "sa", to_m)
            copy.start() if start else copy.wait_send()

    c_sy = far(small_in, sml.at[0], "sy", to_y)
    c_sc = far(sml.at[1], sml.at[2], "sc", to_c)
    s_total = far(sml.at[4], sml.at[4], "sb", to_w)

    def small0():
        c_sy.wait_recv()
        sml[1, 0:8, :] = small_in[0:8, :] + sml[0, 0:8, :]
        sml[1, 8:9, :] = small_in[8:9, :] + sml[0, 9:10, :]
        sml[1, 9:10, :] = jnp.zeros((1, D), F32)
        sml[1, 10:12, :] = small_in[10:12, :]
        sml[1, 12:14, :] = sml[0, 10:12, :]
        sml[1, 14:16, :] = jnp.zeros((2, D), F32)
        c_sc.start()

    def small1():
        c_sc.wait()
        sml[1, 0:8, :] = sml[1, 0:8, :] + sml[2, 0:8, :]

        @pl.when(is_end)
        def _():
            small_middle(True)

    def small2():
        @pl.when(not_end)
        def _():
            far(sml.at[1], sml.at[3], "sa", to_w).wait_recv()
            sml[1] = sml[1] + sml[3]
            small_middle(True)

    def small3():
        s_total.wait_recv()

        @pl.when(is_mid)
        def _():
            sml[4] = sml[1] + sml[4]

        @pl.when(not_end)
        def _():
            s_total.start()

        small_ref[...] = sml[4]

    def step(k, carry=0):
        @pl.when(k < N)
        def _():
            stage0(k)

        @pl.when(jnp.logical_and(k >= AWAY_LAG, k < N + AWAY_LAG))
        def _():
            stage1(k - AWAY_LAG)

        @pl.when(jnp.logical_and(is_mid, jnp.logical_and(k >= MID_LAG, k < N + MID_LAG)))
        def _():
            stage2(k - MID_LAG)

        @pl.when(jnp.logical_and(not_mid, jnp.logical_and(k >= LAG, k < N + LAG)))
        def _():
            stage2(k - LAG)

        pl.when(k == N - 6)(small0)
        pl.when(k == N - 5)(small1)
        pl.when(k == N - 4)(small2)
        pl.when(jnp.logical_and(is_mid, k == N - 2))(small3)
        pl.when(jnp.logical_and(not_mid, k == N))(small3)
        return carry

    done_steps = [0]

    def pump(many, index=0, times=1):
        first = done_steps[0] + index * many
        done_steps[0] += many * times

        @pl.when(enc)
        def _():
            lax.fori_loop(first, first + many, step, 0)

    first_down, first_up, first_attn = 0, PM, 2 * PM
    PT = TW // GC

    def outer_rows(left, right, w, first):
        def one(n, carry):
            at = pl.ds(pl.multiple_of(n * TW, TW), TW)
            to = pl.ds(pl.multiple_of(first * GC + n * TW, TW), TW)
            g[w, to, :] = tn(left(at), right()).astype(BF16)
            if w == 1:
                for k in range(PT):
                    y_part(first + n * PT + k).start()
            return carry

        lax.fori_loop(0, NT, one, 0)

    def wide(ref, w):
        return lambda at: ref[w, :, :, at].reshape(2 * R, at.size)

    def h2_cols(at):
        return jnp.concatenate(
            [h2[0, :, :, at].reshape(R, at.size), h2[1, :, :, at].reshape(R, at.size)], axis=0
        )

    def down_outer(w):
        outer_rows(wide(act, w), lambda: dbl[...].reshape(2 * R, D), w, first_down)

    def up_outer(w):
        outer_rows(h2_cols, lambda: gp[w].reshape(2 * R, D), w, first_up)

    @pl.when(enc)
    def _():
        down_outer(1)
        down_outer(0)

    def down_back(half, w, w_ref):
        rows = flat(dbl, half)

        def one(n, carry):
            at = pl.ds(pl.multiple_of(n * TW, TW), TW)
            du = nt(rows, w_ref[at, :]) * gp[w, half, :, at].astype(F32)
            small_in[8 + w:9 + w, at] += column_sum(du)
            gp[w, half, :, at] = du.astype(BF16)
            return carry

        lax.fori_loop(0, NT, one, 0)

    down_back(1, 1, wy.at[2])
    pump(1)
    down_back(1, 0, wown.at[2])
    pump(1)

    def up_back(half):
        return nt(gp[0, half], wown[1]) + nt(gp[1, half], wy[1])

    gone(snd.at[0], "attn", to_c)
    snd[0] = up_back(1).astype(BF16).reshape(I, BL, D)
    c_dh2 = far(snd.at[0], rcv.at[2], "dh2", to_c)
    c_dh2.start()
    pump(1)
    down_back(0, 1, wy.at[2])
    pump(1)
    down_back(0, 0, wown.at[2])

    @pl.when(enc)
    def _():
        up_outer(1)

    pump(1)

    @pl.when(enc)
    def _():
        up_outer(0)

    pump(1)
    back0 = up_back(0).reshape(I, BL, D)
    c_dh2.wait_recv()

    for i in range(I):
        grad = back0[i] + rcv[2, i].astype(F32)
        hat, inverse = normal(mid[i])
        add_norm(4, column_sum(grad * hat))
        add_norm(5, column_sum(grad))
        d_mid = dy[i] + normal_back(hat, inverse, grad * norm_ref[4:5, :])
        dy[i] = d_mid
        add_norm(3, column_sum(d_mid * att[i]))
        d_att = norm_ref[3:4, :] * d_mid
        add_norm(2, column_sum(d_att))
        dal[0, i] = d_att.astype(BF16)
    c_dal = far(dal.at[0], dal.at[1], "dal", to_c)
    c_dal.start()
    pump(1)

    dol[0] = nt(flat(dal, 0), w_o).astype(BF16).reshape(I, BL, PW)
    c_dal.wait_recv()
    dol[1] = nt(flat(dal, 1), w_o).astype(BF16).reshape(I, BL, PW)
    pump(1)

    def all_rows(ref):
        return ref[...].reshape(2 * R, ref.shape[-1])

    base = first_attn * GC

    def store_rows(value, first):
        g[0, base + first:base + first + PC, :] = value[:PC].astype(BF16)
        g[1, base + first:base + first + PC, :] = value[PC:].astype(BF16)

    def attend_back(i):
        for pr in range(z.heads // 2):
            qp, kp, vp, gpair = image(q, i, pr), image(kk, i, pr), image(vv, i, pr), image(dol, i, pr)
            at = slice(pr * 2 * HD, (pr + 1) * 2 * HD)
            dqs, dks, dvs = [], [], []
            for sub in range(2):
                probs = p[i, 2 * pr + sub]
                wide_probs = probs.astype(F32)
                d_probs = nt(jnp.where(lanes[sub], gpair, zero16), vp)
                dvs.append(tn(probs, gpair))
                inner = jnp.sum(d_probs * wide_probs, axis=-1, keepdims=True)
                ds = (wide_probs * (d_probs - inner)).astype(BF16)
                dqs.append(nn(ds, kp))
                dks.append(tn(ds, qp))
            d_q = jnp.where(lanes[0], dqs[0], dqs[1]) * 0.125
            d_k = jnp.where(lanes[0], dks[0], dks[1])
            d_v = jnp.where(lanes[0], dvs[0], dvs[1])
            small_in[10:11, at] += column_sum(d_q)
            small_in[11:12, at] += column_sum(d_v)
            put(dq, i, pr, d_q.astype(BF16))
            put(dk, i, pr, d_k.astype(BF16))
            put(dv, i, pr, d_v.astype(BF16))

    def dn_core(i):
        return far(snd.at[1, i], rcv.at[3, i], "dn", to_c, i)

    def input_back(i):
        grad = nn(dq[:, i].reshape(KEYS, PW), both_rows(0, PC))
        grad += nn(dk[:, i].reshape(KEYS, PW), both_rows(PC, PC))
        grad += nn(dv[:, i].reshape(KEYS, PW), both_rows(2 * PC, PC))
        snd[1, i] = grad[BL:].astype(BF16)
        dn_core(i).start()
        back1[i] = grad[:BL]

    def leave(i):
        dn_core(i).wait_recv()
        grad = back1[i] + rcv[3, i].astype(F32)
        extra = jnp.logical_and(seen_c[i, :BL] > 0.5, reg)

        @pl.when(reg)
        def _():
            other = jnp.where(extra, grad, 0.0)
            hat, inverse = normal(e_own[i].astype(F32))
            dlat[0, i] = normal_back(hat, inverse, other * g0).astype(BF16)
            d_hop(i).start()
            add_norm(0, column_sum(other * hat))
            add_norm(1, column_sum(other))

        own = jnp.where(extra, 0.0, grad)
        hat, inverse = normal(lay(xall[0, i]).astype(F32))
        add_norm(0, column_sum(own * hat))
        add_norm(1, column_sum(own))
        d_x = dy[i] + normal_back(hat, inverse, own * g0)
        outb[1, i] = d_x.astype(BF16).reshape(2, SL, D)

    back1 = brv
    gone(snd.at[1], "br", to_c)
    for i in range(I):
        attend_back(i)
        pump(1)
        input_back(i)
        pump(1)
        if i > 0:
            leave(i - 1)
    leave(I - 1)
    pump(1)

    @pl.when(reg)
    def _():
        down_outer(1)
        down_outer(0)
        up_outer(1)
        up_outer(0)

    store_rows(tn(all_rows(dq), all_rows(h)), 0)
    pump(1)
    store_rows(tn(all_rows(dk), all_rows(kv)), PC)
    pump(1)
    store_rows(tn(all_rows(dv), all_rows(kv)), 2 * PC)
    pump(1)
    store_rows(tn(all_rows(o), all_rows(dal)), 3 * PC)
    small_in[0:8, :] = nacc[...]
    c_sy.start()
    for k in range(first_attn, z.parts):
        y_part(k).start()
    for copy in deliver(1, "gin", gin_ref):
        copy.start()

    lax.fori_loop(jnp.where(enc, done_steps[0], 0), N + LAG, step, 0)

    small_middle(False)
    gone(g.at[1], "gy", to_y)
    gone(g.at[0], "ga", to_m)

    @pl.when(not_end)
    def _():
        s_total.wait_send()
        gone(zb, "gb", to_w)

    c_sy.wait_send()
    for m, ref in enumerate((gd_ref, gu_ref, ga_ref)):
        here(zb.at[0:D], ref, ("g0", "g1", "g2")[m]).wait()
    for which, number, ref in ((0, "res", res_ref), (1, "gin", gin_ref)):
        for copy in deliver(which, number, ref):
            copy.wait()
    for copy in (c_x, c_b0, c_b1, c_xc0, c_xc1, c_dh2, c_dal):
        copy.wait_send()
    gone(h2.at[0], "h2", to_c)
    gone(dbl.at[0], "dbl", to_c)
    gone(snd.at[1], "dn", to_c)

    @pl.when(enc)
    def _():
        if around:
            gone(g.at[0, 0:len(around) * CH], "d1", to_s)
        gone(e_own, "e", to_s)

    @pl.when(reg)
    def _():
        c_pg.wait_send()
        gone(e_own, "ec", to_c)
        gone(dlat.at[0], "dlat", to_s)

    for s, flag in enumerate((enc, reg)):
        @pl.when(flag)
        def _():
            gone(g.at[0, 0:sum(len(js) for js in straight[s]) * CH], "wy", to_y)
            gone(g.at[0, 0:3 * HELP[s] * CH], "wz", pair_z)


def fused(z, x, pg, wa, wu, wd, lengths, mask, qv, mlp, norms):
    *places, arrivals, departures, copies = plan(z)
    I, R, D, BL, SL = z.images, z.rows, z.width, z.block, z.slots
    PC, PW = z.piece, z.pair
    KEYS = 2 * BL
    vm = pl.BlockSpec(memory_space=pltpu.VMEM)
    sm = pl.BlockSpec(memory_space=pltpu.SMEM)
    hbm = pl.BlockSpec(memory_space=pl.ANY)

    def b16(*shape):
        return pltpu.VMEM(shape, BF16)

    def f32(*shape):
        return pltpu.VMEM(shape, F32)

    scratch = [
        b16(3, D, D), b16(3, D, D),
        b16(2, I, 2, SL, D),
        b16(2, I, SL, D),
        f32(2, PC), f32(1, D),
        f32(I, KEYS, 1), f32(I, KEYS, 1), f32(I, KEYS, 1), f32(I, 1, KEYS),
        b16(I, BL, D), b16(I, BL, D),
        b16(2, I, BL, D), b16(2, I, BL, D),
        b16(2, I, BL, PW), b16(2, I, BL, PW), b16(2, I, BL, PW), b16(2, I, BL, PW),
        b16(I, z.heads, KEYS, KEYS),
        f32(I, BL, D), f32(I, BL, D),
        b16(2, I, BL, D),
        b16(2, 2, R, D), b16(2, 2, R, D),
        f32(I, BL, D), f32(I, BL, D),
        b16(2, I, BL, D), b16(4, I, BL, D),
        b16(2, I, BL, D), b16(2, I, BL, D),
        b16(2, I, BL, PW), b16(2, I, BL, PW), b16(2, I, BL, PW), b16(2, I, BL, PW),
        b16(2, 3 * D, D),
        b16(3 * D, D), b16(3 * D, D), b16(3 * D, D),
        b16(2, I, BL, D),
        b16(2, I, 2, SL, D),
        f32(8, D), f32(5, 16, D), f32(16, D),
        pltpu.SemaphoreType.DMA((departures,)),
        pltpu.SemaphoreType.DMA((arrivals,)),
        pltpu.SemaphoreType.DMA((copies,)),
    ]
    weight = jax.ShapeDtypeStruct((D, D), BF16)
    rows = jax.ShapeDtypeStruct((2, I, SL, D), BF16)
    return pl.pallas_call(
        functools.partial(body, z, places),
        out_shape=(rows, rows, weight, weight, weight, jax.ShapeDtypeStruct((16, D), F32)),
        in_specs=[hbm] * 5 + [sm] + [vm] * 4,
        out_specs=(hbm, hbm, hbm, hbm, hbm, vm),
        scratch_shapes=scratch,
        compiler_params=pltpu.CompilerParams(
            collective_id=0, has_side_effects=True, vmem_limit_bytes=121 * 2**19
        ),
    )(x, pg, wa, wu, wd, lengths, mask, qv, mlp, norms)


def local(
    n_dp,
    block_in, lengths, patch_mask, pred_grad, w_qkv, w_out, w_up, w_down, qv_bias, mlp_bias, norms
):
    images, slots, width = block_in.shape[1:]
    piece = w_qkv.shape[3]
    z = Sizes(n_dp, images // 2, slots, width, piece)

    x = block_in.reshape(2, z.images, slots, width)
    pg = pred_grad.reshape(2, z.images, slots, width)
    wa = jnp.concatenate([jnp.swapaxes(w_qkv[0], 1, 2).reshape(3 * piece, width), w_out[0]], axis=0)
    res, gin, g_down, g_up, g_attn, small = fused(
        z, x, pg, wa, w_up[0], w_down[0], lengths, patch_mask, qv_bias[0], mlp_bias, norms[0]
    )
    g_qkv = jnp.einsum(
        "id,pod->pio", jnp.eye(width, dtype=BF16), g_attn[:3 * piece].reshape(3, piece, width),
        preferred_element_type=F32,
    )
    g_qv = small[10:12, :piece] + small[12:14, piece:2 * piece]
    return (
        res.reshape(1, images, slots, width),
        gin.reshape(1, images, slots, width).astype(F32),
        g_qkv[None],
        g_attn[3 * piece:].astype(F32)[None],
        g_up.astype(F32)[None],
        g_down.astype(F32)[None],
        g_qv[None],
        small[8:9],
        small[0:8][None],
    )


def solution(mesh):
    return jax.shard_map(
        functools.partial(local, mesh.shape["dp"]),
        mesh=mesh,
        in_specs=(
            P("section", "dp", "tensor", None),
            P("dp"),
            P("dp", None),
            P("dp", "tensor", None),
            P("section", None, None, "tensor"),
            P("section", "tensor", None),
            P("section", None, "tensor"),
            P("section", "tensor", None),
            P("section", None, "tensor"),
            P("section", "tensor"),
            P("section", None, None),
        ),
        out_specs=(
            P("section", "dp", "tensor", None),
            P("section", "dp", "tensor", None),
            P("section", None, None, "tensor"),
            P("section", "tensor", None),
            P("section", None, "tensor"),
            P("section", "tensor", None),
            P("section", None, "tensor"),
            P("section", "tensor"),
            P("section", None, None),
        ),
        check_vma=False,
    )
```

```python
import functools

import jax
import jax.numpy as jnp
from jax import lax
from jax.experimental import pallas as pl
from jax.experimental.pallas import tpu as pltpu
from jax.sharding import PartitionSpec as P

HD = 64
CH = 128
GC = 64
AROUND = (1, 1, 1)
HELP_E = (3, 2, 2)
EPS = 1e-06
MASKED = -1000000000.0
F32 = jnp.float32
BF16 = jnp.bfloat16


class Places:
    def __init__(self):
        self.count = 0

    def take(self, many=1):
        first = self.count
        self.count += many
        return first


def nn(a, b):
    return lax.dot_general(a, b, (((1,), (0,)), ((), ())), preferred_element_type=F32)


def nt(a, b):
    return lax.dot_general(a, b, (((1,), (1,)), ((), ())), preferred_element_type=F32)


def tn(a, b):
    return lax.dot_general(a, b, (((0,), (0,)), ((), ())), preferred_element_type=F32)


def normal(u):
    mean = jnp.mean(u, axis=-1, keepdims=True)
    centred = u - mean
    spread = jnp.mean(centred * centred, axis=-1, keepdims=True)
    inverse = lax.rsqrt(spread + EPS)
    return centred * inverse, inverse


def normal_back(hat, inverse, grad):
    first = jnp.mean(grad, axis=-1, keepdims=True)
    second = jnp.mean(grad * hat, axis=-1, keepdims=True)
    return inverse * (grad - first - hat * second)


def column_sum(u):
    return jnp.sum(u, axis=0, keepdims=True)


class Sizes:
    def __init__(self, n_dp, images, slots, width, piece):
        self.n_dp = n_dp
        self.images = images
        self.slots = slots
        self.width = width
        self.piece = piece
        self.block = 2 * slots
        self.rows = images * self.block
        self.pair = 2 * piece
        self.heads = self.pair // HD
        self.around = sum(AROUND)
        self.per_mat = width // GC
        self.parts = 3 * self.per_mat


def plan(z):
    p, d, n = Places(), Places(), Places()
    pieces = z.width // CH
    recv = dict(
        x=p.take(), bias=p.take(2), xc0=p.take(), xc1=p.take(), pg=p.take(),
        wy=p.take(3 * pieces), wz=p.take(3 * pieces // 2),
        d1=p.take(z.around), d2=p.take(z.around),
        e=p.take(z.images), ec=p.take(z.images),
        attn=p.take(z.images), h2=p.take(z.images), br=p.take(z.images), dbl=p.take(z.images),
        dh2=p.take(), dal=p.take(z.images), dn=p.take(z.images),
        dlat=p.take(z.images), res=p.take(), gin=p.take(),
        gy=p.take(z.parts), ga=p.take(z.parts), gb=p.take(z.parts),
        sy=p.take(), sc=p.take(), sa=p.take(), sb=p.take(),
    )
    together = ("wy", "wz", "d1", "gy", "ga", "gb", "attn", "h2", "br", "dbl", "e", "ec", "dlat", "dn", "dal")
    many = dict(bias=2, d2=z.around)
    send = {name: d.take(many.get(name, 1)) for name in recv}
    send["d3"] = d.take(z.around)
    local = {name: n.take() for name in ("w0", "wo", "w1", "w2", "x", "pg", "res", "gin", "g0", "g1", "g2")}
    return recv, send, frozenset(together), local, p.count, d.count, n.count


def body(
    z, places,
    x_ref, pg_ref, wqkv_ref, wout_ref, wu_ref, wd_ref, len_ref, mask_ref, qv_ref, mlp_ref, norm_ref,
    res_ref, gin_ref, gd_ref, gu_ref, ga_ref, small_ref,
    wown, wy, xall, pgr, qv_y, mlp_y, code_c, seen_c, cov_c, key_r,
    e_own, e_oth, h, kv, q, kk, vv, o, p, att, mid, h2, act, gp, brv, dy,
    snd, rcv, dbl, dal, dol, dq, dk, dv, g, yr, za, zb, dlat, outb, nacc, sml, small_in,
    ss, rs, ls,
):
    S, SEND, TOGETHER, LOCAL = places
    sec = lax.axis_index("section")
    dp = lax.axis_index("dp")
    t = lax.axis_index("tensor")
    y = t // 2
    c = t % 2
    to_y = {"tensor": 2 * (1 - y) + c}
    to_c = {"tensor": 2 * y + 1 - c}
    to_s = {"section": 1 - sec}
    parity = dp % 2
    pair_z = {"dp": dp + 1 - 2 * parity}
    top = dp // (z.n_dp // 2)
    to_m = {"dp": dp + 1 - 2 * top}
    to_w = {"dp": dp - 1 + 2 * top}
    is_end = jnp.logical_or(dp == 0, dp == z.n_dp - 1)
    not_end = jnp.logical_not(is_end)
    is_mid = jnp.logical_or(dp == z.n_dp // 2 - 1, dp == z.n_dp // 2)
    not_mid = jnp.logical_not(is_mid)
    enc = sec == 0
    reg = sec == 1

    I, R, D, BL, SL = z.images, z.rows, z.width, z.block, z.slots
    PC, PW = z.piece, z.pair
    KEYS = 2 * BL
    WP = D // CH
    HELP = (HELP_E, (WP // 2,) * 3)
    MOST = WP // 2

    def far(src, dst, name, to, index=0, receive=None, send=None):
        leave = SEND[send or name] + (0 if name in TOGETHER else index)
        return pltpu.make_async_remote_copy(
            src_ref=src, dst_ref=dst, send_sem=ss.at[leave], recv_sem=rs.at[S[receive or name] + index],
            device_id=to, device_id_type=pl.DeviceIdType.MESH,
        )

    def gone(ref, name, to):
        far(ref, ref, name, to).wait_send()

    def here(src, dst, name):
        return pltpu.make_async_copy(src, dst, ls.at[LOCAL[name]])

    w_refs = (wown.at[0], wu_ref, wd_ref)
    own_w = [here(w_refs[m], wown.at[m], ("w0", "w1", "w2")[m]) for m in (1, 2)]
    own_a = (here(wqkv_ref, wown.at[0, 0:3 * z.piece], "w0"), here(wout_ref, wown.at[0, 3 * z.piece:], "wo"))
    own_x = here(x_ref.at[y], xall.at[0, :, 0], "x")
    own_pg = here(pg_ref.at[y], pgr.at[0], "pg")
    for copy in (own_x, *own_a, *own_w):
        copy.start()
    own_pg.start()

    barrier = pltpu.get_barrier_semaphore()

    def greet(to):
        pl.semaphore_signal(barrier, inc=1, device_id=to, device_id_type=pl.DeviceIdType.MESH)

    greet(to_y)
    greet(to_c)
    greet(to_s)
    greet(to_m)

    @pl.when(not_end)
    def _():
        greet(to_w)
        pl.semaphore_wait(barrier, 5)

    @pl.when(is_end)
    def _():
        pl.semaphore_wait(barrier, 4)

    c_x = far(x_ref.at[1 - y], xall.at[0, :, 1], "x", to_y)
    c_b0 = far(qv_ref, qv_y, "bias", to_y)
    c_b1 = far(mlp_ref, mlp_y, "bias", to_y, 1)
    c_xc0 = far(x_ref.at[y], xall.at[1, :, 0], "xc0", to_c)
    c_xc1 = far(xall.at[0, :, 1], xall.at[1, :, 1], "xc1", to_c)
    c_pg = far(pg_ref.at[1 - y], pgr.at[1], "pg", to_y)

    def rows_of(j, side):
        return pl.ds(pl.multiple_of((j + side * (WP - 1 - 2 * j)) * CH, CH), CH)

    def w_y(m, j):
        at = rows_of(j, parity)
        return far(w_refs[m].at[at], wy.at[m, at], "wy", to_y, m * WP + j)

    def w_z(m, j, side=None):
        at = rows_of(j, parity if side is None else side)
        return far(wy.at[m, at], wy.at[m, at], "wz", pair_z, m * (WP // 2) + j)

    around = [(m, WP - HELP[0][m] - 1 - j) for m in range(3) for j in range(AROUND[m] - 1, -1, -1)]

    def d_slot(side, n):
        return g.at[side, pl.ds(n * CH, CH)]

    def d_out(n):
        m, j = around[n]
        return far(w_refs[m].at[rows_of(j, parity)], d_slot(0, n), "d1", to_s, n)

    def d_over(n):
        return far(d_slot(0, n), d_slot(1, n), "d2", to_y, n)

    def d_back(n):
        m, j = around[n]
        leave = SEND["d3"] + n
        return pltpu.make_async_remote_copy(
            src_ref=d_slot(1, n), dst_ref=wy.at[m, rows_of(j, parity)],
            send_sem=ss.at[leave], recv_sem=rs.at[S["wy"] + m * WP + j],
            device_id=to_s, device_id_type=pl.DeviceIdType.MESH,
        )

    straight = (
        [[j for j in range(WP - HELP[0][m]) if (m, j) not in around] for m in range(3)],
        [list(range(WP - HELP[1][m])) for m in range(3)],
    )

    def start_inputs():
        c_xc0.start()
        c_x.start()
        c_b0.start()
        c_b1.start()

    @pl.when(reg)
    def _():
        start_inputs()

    for copy in own_a:
        copy.wait()

    @pl.when(enc)
    def _():
        for n in range(len(around)):
            d_out(n).start()
        for m in range(3):
            for j in straight[0][m]:
                w_y(m, j).start()
                if (m, j) == (0, 1):
                    start_inputs()

    @pl.when(reg)
    def _():
        for n in range(len(around) + 1):
            if n < len(around):
                d_out(n).wait_recv()
                d_over(n).start()
            if n > 0:
                d_over(n - 1).wait_recv()
                d_back(n - 1).start()
            if n == max(len(around) - 1, 0):
                for m in range(3):
                    for j in straight[1][m]:
                        w_y(m, j).start()
                c_pg.start()
        for n in range(len(around)):
            d_over(n).wait_send()
            d_back(n).wait_send()

    def forward_w(m, j, sections=(enc, reg)):
        for s, flag in enumerate((enc, reg)):
            if any(flag is one for one in sections) and j < HELP[s][m]:
                @pl.when(flag)
                def _():
                    w_y(m, j).wait_recv()
                    w_z(m, j).start()

    def finish_w(m):
        for s, flag in enumerate((enc, reg)):
            @pl.when(flag)
            def _():
                for j in range(HELP[s][m], WP - HELP[s][m]):
                    w_y(m, j).wait_recv()
                for j in range(HELP[s][m]):
                    w_z(m, j, 1 - parity).wait_recv()

    rank = lax.broadcasted_iota(jnp.int32, (KEYS, KEYS), 0)
    across = lax.broadcasted_iota(jnp.int32, (KEYS, KEYS), 1)
    group = rank // SL
    y_of = y + (group % 2) * (1 - 2 * y)
    c_of = c + (group // 2) * (1 - 2 * c)
    slot = (2 * y_of + c_of) * SL + rank % SL
    here_slot = slot == across
    diagonal = rank == across
    slot_col = slot[:, 0:1]
    for i in range(I):
        picked = jnp.where(here_slot, mask_ref[pl.ds(y * I + i, 1), :].astype(F32), 0.0)
        marked = jnp.sum(picked, axis=1, keepdims=True) > 0.5
        valid = slot_col < len_ref[y * I + i]
        seen = jnp.where(jnp.logical_and(valid, marked), 1.0, 0.0)
        code = jnp.where(enc, seen, jnp.zeros_like(seen))
        seen_c[i] = seen
        cov_c[i] = jnp.where(valid, 1.0, 0.0) - seen
        code_c[i] = code
        key = jnp.where(valid, code, 2.0)
        key_r[i] = jnp.sum(jnp.where(diagonal, key, 0.0), axis=0, keepdims=True)

    g0, b0 = norm_ref[0:1, :], norm_ref[1:2, :]

    def lay(block):
        return block.reshape(BL, D)

    forward_w(0, 0)
    forward_w(0, 1)
    own_x.wait()
    c_x.wait_recv()
    c_xc1.start()

    def norm_rows(half):
        def one(i, carry):
            hat, _ = normal(lay(xall[half, i]).astype(F32))
            value = (hat * g0 + b0).astype(BF16)
            h[half, i] = value
            kv[half, i] = value
            return carry

        lax.fori_loop(0, I, one, 0)

    norm_rows(0)
    c_xc0.wait_recv()
    c_xc1.wait_recv()
    norm_rows(1)
    for j in range(2, MOST):
        forward_w(0, j)
    c_b0.wait_recv()
    c_b1.wait_recv()
    finish_w(0)

    def both_rows(first, many):
        return jnp.concatenate([wown[0, first:first + many], wy[0, first:first + many]], axis=0)

    bq = jnp.concatenate([qv_ref[0:1, :], qv_y[0:1, :]], axis=1)
    bv = jnp.concatenate([qv_ref[1:2, :], qv_y[1:2, :]], axis=1)

    def flat(ref, half):
        return ref[half].reshape(R, ref.shape[-1])

    def e_hop(i):
        return far(dlat.at[0, i], e_own.at[i], "e", to_s, i)

    def e_core(i):
        return far(e_own.at[i], e_oth.at[i], "ec", to_c, i)

    for half in range(2):
        q[half] = ((nt(flat(h, half), both_rows(0, PC)) + bq).astype(BF16) * 0.125).reshape(I, BL, PW)

    lane = lax.broadcasted_iota(jnp.int32, (KEYS, 2 * HD), 1)
    lanes = (lane < HD, lane >= HD)
    zero16 = jnp.zeros((KEYS, 2 * HD), BF16)

    def image(ref, i, pr):
        at = slice(pr * 2 * HD, (pr + 1) * 2 * HD)
        return jnp.concatenate([ref[0, i, :, at], ref[1, i, :, at]], axis=0)

    def put(ref, i, pr, value):
        at = slice(pr * 2 * HD, (pr + 1) * 2 * HD)
        ref[0, i, :, at] = value[:BL]
        ref[1, i, :, at] = value[BL:]

    def latent_keys(half, ref, i):
        hat, _ = normal(ref[i].astype(F32))
        value = (hat * g0 + b0).astype(BF16)
        seen = seen_c[i, half * BL:(half + 1) * BL] > 0.5
        kv[half, i] = jnp.where(seen, value, h[half, i])

    def attend(i):
        @pl.when(reg)
        def _():
            e_hop(i).wait_recv()
            e_core(i).start()
            latent_keys(0, e_own, i)
            e_core(i).wait_recv()
            latent_keys(1, e_oth, i)

        rows_k = kv[:, i].reshape(KEYS, D)
        kk[:, i] = nt(rows_k, both_rows(PC, PC)).astype(BF16).reshape(2, BL, PW)
        vv[:, i] = (nt(rows_k, both_rows(2 * PC, PC)) + bv).astype(BF16).reshape(2, BL, PW)
        shut = jnp.where(code_c[i] == key_r[i], 0.0, MASKED)
        for pr in range(z.heads // 2):
            qp, kp, vp = image(q, i, pr), image(kk, i, pr), image(vv, i, pr)
            outs = []
            for sub in range(2):
                scores = nt(jnp.where(lanes[sub], qp, zero16), kp) + shut
                top_value = jnp.max(scores, axis=-1, keepdims=True)
                e = jnp.exp(scores - top_value)
                probs = (e * (1.0 / jnp.sum(e, axis=-1, keepdims=True))).astype(BF16)
                p[i, 2 * pr + sub] = probs
                outs.append(nn(probs, vp))
            put(o, i, pr, jnp.where(lanes[0], outs[0], outs[1]).astype(BF16))
        attn = nn(o[:, i].reshape(KEYS, PW), both_rows(3 * PC, PC))
        snd[0, i] = attn[BL:].astype(BF16)
        exchange(0, "attn", i).start()
        att[i] = attn[:BL]

    def exchange(slot, name, i):
        return far(snd.at[slot % 2, i], rcv.at[slot, i], name, to_c, i)

    def h2_core(i):
        return far(h2.at[0, i], h2.at[1, i], "h2", to_c, i)

    def middle(i):
        exchange(0, "attn", i).wait_recv()
        attn = att[i] + rcv[0, i].astype(F32) + norm_ref[2:3, :]
        att[i] = attn
        value = lay(xall[0, i]).astype(F32) + norm_ref[3:4, :] * attn
        mid[i] = value
        hat, _ = normal(value)
        h2[0, i] = (hat * norm_ref[4:5, :] + norm_ref[5:6, :]).astype(BF16)
        h2_core(i).start()

    TW = 256
    NT = D // TW

    def rows_at(i):
        return pl.ds(i * BL, BL)

    def up(i, w, w_ref, b_row):
        rows2 = h2[:, i].reshape(KEYS, D)

        def one(n, carry):
            at = pl.ds(pl.multiple_of(n * TW, TW), TW)
            u = nn(rows2, w_ref[:, at]) + b_row[:, at]
            cdf = 0.5 + 0.5 * lax.erf(u * 0.7071067811865476)
            act[w, :, rows_at(i), at] = (u * cdf).astype(BF16).reshape(2, BL, TW)
            slope = cdf + u * (0.3989422804014327 * jnp.exp(-0.5 * u * u))
            gp[w, :, rows_at(i), at] = slope.astype(BF16).reshape(2, BL, TW)
            return carry

        lax.fori_loop(0, NT, one, 0)

    def down(i):
        br = nn(act[0, :, rows_at(i)].reshape(KEYS, D), wown[2])
        br += nn(act[1, :, rows_at(i)].reshape(KEYS, D), wy[2])
        snd[1, i] = br[BL:].astype(BF16)
        exchange(1, "br", i).start()
        brv[i] = br[:BL]

    def finish(i):
        exchange(1, "br", i).wait_recv()
        br = brv[i] + rcv[1, i].astype(F32) + norm_ref[6:7, :]
        brv[i] = br
        out = mid[i] + norm_ref[7:8, :] * br

        @pl.when(enc)
        def _():
            dlat[0, i] = (out * seen_c[i, :BL]).astype(BF16)
            e_hop(i).start()

        outb[0, i] = (out * cov_c[i, :BL]).astype(BF16).reshape(2, SL, D)

    def own_up(i):
        h2_core(i).wait_recv()
        up(i, 0, wown.at[1], mlp_ref)

    def other_up(i):
        up(i, 1, wy.at[1], mlp_y)

    def own_back(i):
        @pl.when(reg)
        def _():
            dy[i] = jnp.concatenate([pgr[0, i], pgr[1, i]], axis=0).astype(F32) * cov_c[i, :BL]

        @pl.when(enc)
        def _():
            d_hop(i).wait_recv()
            dy[i] = dlat[1, i].astype(F32) * seen_c[i, :BL]

        dbl[0, i] = (norm_ref[7:8, :] * dy[i]).astype(BF16)
        dbl_core(i).start()

    def d_hop(i):
        return far(dlat.at[0, i], dlat.at[1, i], "dlat", to_s, i)

    def dbl_core(i):
        return far(dbl.at[0, i], dbl.at[1, i], "dbl", to_c, i)

    for j in range(MOST):
        forward_w(1, j, (reg,))
    forward_w(2, 0, (reg,))

    for i in range(I):
        attend(i)
        if i == 0:
            forward_w(1, 0, (enc,))
            forward_w(1, 1, (enc,))
            forward_w(2, 1, (reg,))
        if i == 1:
            forward_w(1, 2, (enc,))
            forward_w(2, 2, (reg,))
        if i > 0:
            middle(i - 1)
    forward_w(2, 0, (enc,))
    own_w[0].wait()
    own_up(0)
    middle(I - 1)
    forward_w(2, 1, (enc,))
    for i in range(1, I):
        own_up(i)
        if i < MOST - 1:
            forward_w(2, i + 1, (enc,))
    finish_w(1)
    for i in range(I):
        other_up(i)

    own_pg.wait()

    @pl.when(reg)
    def _():
        c_pg.wait_recv()
        for i in range(I):
            own_back(i)

    own_w[1].wait()
    finish_w(2)
    for i in range(I):
        down(i)
        if i > 0:
            finish(i - 1)
    finish(I - 1)
    w_o = both_rows(3 * PC, PC)

    def deliver(which, number, ref):
        return (
            here(outb.at[which, :, 0], ref.at[y], number),
            far(outb.at[which, :, 1], ref.at[y], number, to_y),
        )

    for copy in deliver(0, "res", res_ref):
        copy.start()

    nacc[...] = jnp.zeros_like(nacc)
    small_in[...] = jnp.zeros_like(small_in)

    def add_norm(row, value):
        nacc[row:row + 1, :] += value

    @pl.when(enc)
    def _():
        for i in range(I):
            own_back(i)

    def branch_sums(i, carry):
        grad = dy[i]
        add_norm(7, column_sum(grad * brv[i]))
        add_norm(6, column_sum(norm_ref[7:8, :] * grad))
        return carry

    for i in range(I):
        dbl_core(i).wait_recv()

    N = z.parts
    PM = z.per_mat

    def part(k):
        return pl.ds(pl.multiple_of(k * GC, GC), GC)

    def y_part(k):
        at = part(k)
        return far(g.at[1, at], yr.at[at], "gy", to_y, k)

    def to_middle(k):
        at = part(k)

        @pl.when(is_mid)
        def _():
            far(g.at[0, at], zb.at[at], "ga", to_m, k, receive="gb").start()

        @pl.when(not_mid)
        def _():
            far(g.at[0, at], za.at[at], "ga", to_m, k).start()

    def from_away(k):
        at = part(k)
        return far(g.at[0, at], za.at[at], "ga", to_w, k)

    def total(k):
        at = part(k)
        return far(zb.at[at], zb.at[at], "gb", to_w, k)

    def stage0(k):
        at = part(k)
        y_part(k).wait_recv()
        g[0, at, :] = (g[0, at, :].astype(F32) + yr[at, :].astype(F32)).astype(BF16)

        @pl.when(is_end)
        def _():
            to_middle(k)

    def stage1(k):
        at = part(k)

        @pl.when(not_end)
        def _():
            from_away(k).wait_recv()
            g[0, at, :] = (g[0, at, :].astype(F32) + za[at, :].astype(F32)).astype(BF16)
            to_middle(k)

    def each_out(k, do):
        for m, ref in enumerate((gd_ref, gu_ref, ga_ref)):
            @pl.when(jnp.logical_and(k >= m * PM, k < (m + 1) * PM))
            def _():
                do(here(zb.at[part(k)], ref.at[part(k - m * PM)], ("g0", "g1", "g2")[m]))

    def stage2(k):
        at = part(k)
        total(k).wait_recv()

        @pl.when(is_mid)
        def _():
            zb[at, :] = (g[0, at, :].astype(F32) + zb[at, :].astype(F32)).astype(BF16)

        @pl.when(not_end)
        def _():
            total(k).start()

        each_out(k, lambda copy: copy.start())

    AWAY_LAG = 2
    MID_LAG = 4
    LAG = 8

    def small_middle(start):
        @pl.when(is_mid)
        def _():
            copy = far(sml.at[1], sml.at[4], "sa", to_m, receive="sb")
            copy.start() if start else copy.wait_send()

        @pl.when(not_mid)
        def _():
            copy = far(sml.at[1], sml.at[3], "sa", to_m)
            copy.start() if start else copy.wait_send()

    c_sy = far(small_in, sml.at[0], "sy", to_y)
    c_sc = far(sml.at[1], sml.at[2], "sc", to_c)
    s_total = far(sml.at[4], sml.at[4], "sb", to_w)

    def small0():
        c_sy.wait_recv()
        sml[1, 0:8, :] = small_in[0:8, :] + sml[0, 0:8, :]
        sml[1, 8:9, :] = small_in[8:9, :] + sml[0, 9:10, :]
        sml[1, 9:10, :] = jnp.zeros((1, D), F32)
        sml[1, 10:12, :] = small_in[10:12, :]
        sml[1, 12:14, :] = sml[0, 10:12, :]
        sml[1, 14:16, :] = jnp.zeros((2, D), F32)
        c_sc.start()

    def small1():
        c_sc.wait()
        sml[1, 0:8, :] = sml[1, 0:8, :] + sml[2, 0:8, :]

        @pl.when(is_end)
        def _():
            small_middle(True)

    def small2():
        @pl.when(not_end)
        def _():
            far(sml.at[1], sml.at[3], "sa", to_w).wait_recv()
            sml[1] = sml[1] + sml[3]
            small_middle(True)

    def small3():
        s_total.wait_recv()

        @pl.when(is_mid)
        def _():
            sml[4] = sml[1] + sml[4]

        @pl.when(not_end)
        def _():
            s_total.start()

        small_ref[...] = sml[4]

    def step(k, carry=0):
        @pl.when(k < N)
        def _():
            stage0(k)

        @pl.when(jnp.logical_and(k >= AWAY_LAG, k < N + AWAY_LAG))
        def _():
            stage1(k - AWAY_LAG)

        @pl.when(jnp.logical_and(is_mid, jnp.logical_and(k >= MID_LAG, k < N + MID_LAG)))
        def _():
            stage2(k - MID_LAG)

        @pl.when(jnp.logical_and(not_mid, jnp.logical_and(k >= LAG, k < N + LAG)))
        def _():
            stage2(k - LAG)

        pl.when(k == N - 6)(small0)
        pl.when(k == N - 5)(small1)
        pl.when(k == N - 4)(small2)
        pl.when(jnp.logical_and(is_mid, k == N - 2))(small3)
        pl.when(jnp.logical_and(not_mid, k == N))(small3)
        return carry

    done_steps = [0]

    def pump(many, index=0, times=1):
        first = done_steps[0] + index * many
        done_steps[0] += many * times

        @pl.when(enc)
        def _():
            lax.fori_loop(first, first + many, step, 0)

    first_down, first_up, first_attn = 0, PM, 2 * PM
    PT = TW // GC

    def outer_rows(left, right, w, first):
        def one(n, carry):
            at = pl.ds(pl.multiple_of(n * TW, TW), TW)
            to = pl.ds(pl.multiple_of(first * GC + n * TW, TW), TW)
            g[w, to, :] = tn(left(at), right()).astype(BF16)
            if w == 1:
                for k in range(PT):
                    y_part(first + n * PT + k).start()
            return carry

        lax.fori_loop(0, NT, one, 0)

    def wide(ref, w):
        return lambda at: ref[w, :, :, at].reshape(2 * R, at.size)

    def h2_cols(at):
        return jnp.concatenate(
            [h2[0, :, :, at].reshape(R, at.size), h2[1, :, :, at].reshape(R, at.size)], axis=0
        )

    def down_outer(w):
        outer_rows(wide(act, w), lambda: dbl[...].reshape(2 * R, D), w, first_down)

    def up_outer(w):
        outer_rows(h2_cols, lambda: gp[w].reshape(2 * R, D), w, first_up)

    @pl.when(enc)
    def _():
        down_outer(1)
        down_outer(0)

    def down_back(half, w, w_ref):
        rows = flat(dbl, half)

        def one(n, carry):
            at = pl.ds(pl.multiple_of(n * TW, TW), TW)
            du = nt(rows, w_ref[at, :]) * gp[w, half, :, at].astype(F32)
            small_in[8 + w:9 + w, at] += column_sum(du)
            gp[w, half, :, at] = du.astype(BF16)
            return carry

        lax.fori_loop(0, NT, one, 0)

    down_back(1, 1, wy.at[2])
    pump(1)
    down_back(1, 0, wown.at[2])
    pump(1)

    def up_back(half):
        return nt(gp[0, half], wown[1]) + nt(gp[1, half], wy[1])

    gone(snd.at[0], "attn", to_c)
    snd[0] = up_back(1).astype(BF16).reshape(I, BL, D)
    c_dh2 = far(snd.at[0], rcv.at[2], "dh2", to_c)
    c_dh2.start()
    lax.fori_loop(0, I, branch_sums, 0)
    pump(1)
    down_back(0, 1, wy.at[2])
    pump(1)
    down_back(0, 0, wown.at[2])

    @pl.when(enc)
    def _():
        up_outer(1)

    pump(1)

    @pl.when(enc)
    def _():
        up_outer(0)

    pump(1)
    back0 = up_back(0).reshape(I, BL, D)
    c_dh2.wait_recv()

    def dal_core(i):
        return far(dal.at[0, i], dal.at[1, i], "dal", to_c, i)

    for i in range(I):
        grad = back0[i] + rcv[2, i].astype(F32)
        hat, inverse = normal(mid[i])
        add_norm(4, column_sum(grad * hat))
        add_norm(5, column_sum(grad))
        d_mid = dy[i] + normal_back(hat, inverse, grad * norm_ref[4:5, :])
        dy[i] = d_mid
        add_norm(3, column_sum(d_mid * att[i]))
        d_att = norm_ref[3:4, :] * d_mid
        add_norm(2, column_sum(d_att))
        dal[0, i] = d_att.astype(BF16)
        dal_core(i).start()
    pump(1)

    def all_rows(ref):
        return ref[...].reshape(2 * R, ref.shape[-1])

    base = first_attn * GC

    def store_rows(value, first):
        g[0, base + first:base + first + PC, :] = value[:PC].astype(BF16)
        g[1, base + first:base + first + PC, :] = value[PC:].astype(BF16)

    def attend_back(i):
        dal_core(i).wait_recv()
        dol[:, i] = nt(dal[:, i].reshape(KEYS, D), w_o).astype(BF16).reshape(2, BL, PW)
        for pr in range(z.heads // 2):
            qp, kp, vp, gpair = image(q, i, pr), image(kk, i, pr), image(vv, i, pr), image(dol, i, pr)
            at = slice(pr * 2 * HD, (pr + 1) * 2 * HD)
            dqs, dks, dvs = [], [], []
            for sub in range(2):
                probs = p[i, 2 * pr + sub]
                wide_probs = probs.astype(F32)
                d_probs = nt(jnp.where(lanes[sub], gpair, zero16), vp)
                dvs.append(tn(probs, gpair))
                inner = jnp.sum(d_probs * wide_probs, axis=-1, keepdims=True)
                ds = (wide_probs * (d_probs - inner)).astype(BF16)
                dqs.append(nn(ds, kp))
                dks.append(tn(ds, qp))
            d_q = jnp.where(lanes[0], dqs[0], dqs[1]) * 0.125
            d_k = jnp.where(lanes[0], dks[0], dks[1])
            d_v = jnp.where(lanes[0], dvs[0], dvs[1])
            small_in[10:11, at] += column_sum(d_q)
            small_in[11:12, at] += column_sum(d_v)
            put(dq, i, pr, d_q.astype(BF16))
            put(dk, i, pr, d_k.astype(BF16))
            put(dv, i, pr, d_v.astype(BF16))

    def dn_core(i):
        return far(snd.at[1, i], rcv.at[3, i], "dn", to_c, i)

    def input_back(i):
        grad = nn(dq[:, i].reshape(KEYS, PW), both_rows(0, PC))
        grad += nn(dk[:, i].reshape(KEYS, PW), both_rows(PC, PC))
        grad += nn(dv[:, i].reshape(KEYS, PW), both_rows(2 * PC, PC))
        snd[1, i] = grad[BL:].astype(BF16)
        dn_core(i).start()
        back1[i] = grad[:BL]

    def leave(i):
        dn_core(i).wait_recv()
        grad = back1[i] + rcv[3, i].astype(F32)
        extra = jnp.logical_and(seen_c[i, :BL] > 0.5, reg)

        @pl.when(reg)
        def _():
            other = jnp.where(extra, grad, 0.0)
            hat, inverse = normal(e_own[i].astype(F32))
            dlat[0, i] = normal_back(hat, inverse, other * g0).astype(BF16)
            d_hop(i).start()
            add_norm(0, column_sum(other * hat))
            add_norm(1, column_sum(other))

        own = jnp.where(extra, 0.0, grad)
        hat, inverse = normal(lay(xall[0, i]).astype(F32))
        add_norm(0, column_sum(own * hat))
        add_norm(1, column_sum(own))
        d_x = dy[i] + normal_back(hat, inverse, own * g0)
        outb[1, i] = d_x.astype(BF16).reshape(2, SL, D)

    back1 = brv
    gone(snd.at[1], "br", to_c)
    for i in range(I):
        attend_back(i)
        pump(1)
        input_back(i)
        pump(1)
        if i > 0:
            leave(i - 1)
    leave(I - 1)
    pump(1)

    @pl.when(reg)
    def _():
        down_outer(1)
        down_outer(0)
        up_outer(1)
        up_outer(0)

    store_rows(tn(all_rows(dq), all_rows(h)), 0)
    pump(1)
    store_rows(tn(all_rows(dk), all_rows(kv)), PC)
    pump(1)
    store_rows(tn(all_rows(dv), all_rows(kv)), 2 * PC)
    pump(1)
    store_rows(tn(all_rows(o), all_rows(dal)), 3 * PC)
    small_in[0:8, :] = nacc[...]
    c_sy.start()
    for k in range(first_attn, z.parts):
        y_part(k).start()
    for copy in deliver(1, "gin", gin_ref):
        copy.start()

    lax.fori_loop(jnp.where(enc, done_steps[0], 0), N + LAG, step, 0)

    small_middle(False)
    gone(g.at[1], "gy", to_y)
    gone(g.at[0], "ga", to_m)

    @pl.when(not_end)
    def _():
        s_total.wait_send()
        gone(zb, "gb", to_w)

    c_sy.wait_send()
    for m, ref in enumerate((gd_ref, gu_ref, ga_ref)):
        here(zb.at[0:D], ref, ("g0", "g1", "g2")[m]).wait()
    for which, number, ref in ((0, "res", res_ref), (1, "gin", gin_ref)):
        for copy in deliver(which, number, ref):
            copy.wait()
    for copy in (c_x, c_b0, c_b1, c_xc0, c_xc1, c_dh2):
        copy.wait_send()
    gone(h2.at[0], "h2", to_c)
    gone(dbl.at[0], "dbl", to_c)
    gone(dal.at[0], "dal", to_c)
    gone(snd.at[1], "dn", to_c)

    @pl.when(enc)
    def _():
        if around:
            gone(g.at[0, 0:len(around) * CH], "d1", to_s)
        gone(e_own, "e", to_s)

    @pl.when(reg)
    def _():
        c_pg.wait_send()
        gone(e_own, "ec", to_c)
        gone(dlat.at[0], "dlat", to_s)

    for s, flag in enumerate((enc, reg)):
        @pl.when(flag)
        def _():
            gone(g.at[0, 0:sum(len(js) for js in straight[s]) * CH], "wy", to_y)
            gone(g.at[0, 0:sum(HELP[s]) * CH], "wz", pair_z)


def fused(z, x, pg, wqkv, wout, wu, wd, lengths, mask, qv, mlp, norms):
    *places, arrivals, departures, copies = plan(z)
    I, R, D, BL, SL = z.images, z.rows, z.width, z.block, z.slots
    PC, PW = z.piece, z.pair
    KEYS = 2 * BL
    vm = pl.BlockSpec(memory_space=pltpu.VMEM)
    sm = pl.BlockSpec(memory_space=pltpu.SMEM)
    hbm = pl.BlockSpec(memory_space=pl.ANY)

    def b16(*shape):
        return pltpu.VMEM(shape, BF16)

    def f32(*shape):
        return pltpu.VMEM(shape, F32)

    scratch = [
        b16(3, D, D), b16(3, D, D),
        b16(2, I, 2, SL, D),
        b16(2, I, SL, D),
        f32(2, PC), f32(1, D),
        f32(I, KEYS, 1), f32(I, KEYS, 1), f32(I, KEYS, 1), f32(I, 1, KEYS),
        b16(I, BL, D), b16(I, BL, D),
        b16(2, I, BL, D), b16(2, I, BL, D),
        b16(2, I, BL, PW), b16(2, I, BL, PW), b16(2, I, BL, PW), b16(2, I, BL, PW),
        b16(I, z.heads, KEYS, KEYS),
        f32(I, BL, D), f32(I, BL, D),
        b16(2, I, BL, D),
        b16(2, 2, R, D), b16(2, 2, R, D),
        f32(I, BL, D), f32(I, BL, D),
        b16(2, I, BL, D), b16(4, I, BL, D),
        b16(2, I, BL, D), b16(2, I, BL, D),
        b16(2, I, BL, PW), b16(2, I, BL, PW), b16(2, I, BL, PW), b16(2, I, BL, PW),
        b16(2, 3 * D, D),
        b16(3 * D, D), b16(3 * D, D), b16(3 * D, D),
        b16(2, I, BL, D),
        b16(2, I, 2, SL, D),
        f32(8, D), f32(5, 16, D), f32(16, D),
        pltpu.SemaphoreType.DMA((departures,)),
        pltpu.SemaphoreType.DMA((arrivals,)),
        pltpu.SemaphoreType.DMA((copies,)),
    ]
    weight = jax.ShapeDtypeStruct((D, D), BF16)
    rows = jax.ShapeDtypeStruct((2, I, SL, D), BF16)
    return pl.pallas_call(
        functools.partial(body, z, places),
        out_shape=(rows, rows, weight, weight, weight, jax.ShapeDtypeStruct((16, D), F32)),
        in_specs=[hbm] * 6 + [sm] + [vm] * 4,
        out_specs=(hbm, hbm, hbm, hbm, hbm, vm),
        scratch_shapes=scratch,
        compiler_params=pltpu.CompilerParams(
            collective_id=0, has_side_effects=True, vmem_limit_bytes=121 * 2**19
        ),
    )(x, pg, wqkv, wout, wu, wd, lengths, mask, qv, mlp, norms)


def widen(
    piece, n_qkv,
    res, gin, gd, gu, ga, small,
    o_res, o_gin, o_down, o_up, o_qkv, o_out, o_qv, o_mlp, o_norms,
):
    n = pl.program_id(0)
    o_res[...] = res[...]
    o_gin[...] = gin[...].astype(F32)
    o_down[...] = gd[...].astype(F32)
    o_up[...] = gu[...].astype(F32)

    @pl.when(n < n_qkv)
    def _():
        o_qkv[...] = ga[...].astype(F32)

    @pl.when(n >= n_qkv)
    def _():
        o_out[...] = ga[...].astype(F32)

    @pl.when(n == 0)
    def _():
        o_qv[...] = small[10:12, :piece] + small[12:14, piece:2 * piece]
        o_mlp[...] = small[8:9, :]
        o_norms[...] = small[0:8, :]


def outputs(z, res, gin, gd, gu, ga, small):
    D, PC = z.width, z.piece
    tile = 192
    steps = D // tile
    n_qkv = 3 * PC // tile
    token_rows = 2 * z.images * z.slots
    token_tile = token_rows // steps
    tokens = pl.BlockSpec((token_tile, D), lambda n: (n, 0))
    rows = pl.BlockSpec((tile, D), lambda n: (n, 0))
    once = lambda *shape: pl.BlockSpec(shape, lambda n: (0, 0))
    first = pl.BlockSpec((tile, D), lambda n: (jnp.minimum(n, n_qkv - 1), 0))
    last = pl.BlockSpec((tile, D), lambda n: (jnp.maximum(n - n_qkv, 0), 0))
    shape = jax.ShapeDtypeStruct
    return pl.pallas_call(
        functools.partial(widen, PC, n_qkv),
        grid=(steps,),
        out_shape=(
            shape((token_rows, D), BF16), shape((token_rows, D), F32), shape((D, D), F32), shape((D, D), F32),
            shape((3 * PC, D), F32), shape((PC, D), F32), shape((2, PC), F32), shape((1, D), F32), shape((8, D), F32),
        ),
        in_specs=[tokens, tokens, rows, rows, rows, once(16, D)],
        out_specs=(tokens, tokens, rows, rows, first, last, once(2, PC), once(1, D), once(8, D)),
    )(res.reshape(token_rows, D), gin.reshape(token_rows, D), gd, gu, ga, small)


def local(
    n_dp,
    block_in, lengths, patch_mask, pred_grad, w_qkv, w_out, w_up, w_down, qv_bias, mlp_bias, norms
):
    images, slots, width = block_in.shape[1:]
    piece = w_qkv.shape[3]
    z = Sizes(n_dp, images // 2, slots, width, piece)

    x = block_in.reshape(2, z.images, slots, width)
    pg = pred_grad.reshape(2, z.images, slots, width)
    wqkv = jnp.swapaxes(w_qkv[0], 1, 2).reshape(3 * piece, width)
    summed = fused(
        z, x, pg, wqkv, w_out[0], w_up[0], w_down[0], lengths, patch_mask, qv_bias[0], mlp_bias, norms[0]
    )
    res, gin, g_down, g_up, g_qkv, g_out, g_qv, g_mlp, g_norms = outputs(z, *summed)
    return (
        res.reshape(1, images, slots, width),
        gin.reshape(1, images, slots, width),
        jnp.swapaxes(g_qkv.reshape(3, piece, width), 1, 2)[None],
        g_out[None],
        g_up[None],
        g_down[None],
        g_qv[None],
        g_mlp,
        g_norms[None],
    )


def solution(mesh):
    return jax.shard_map(
        functools.partial(local, mesh.shape["dp"]),
        mesh=mesh,
        in_specs=(
            P("section", "dp", "tensor", None),
            P("dp"),
            P("dp", None),
            P("dp", "tensor", None),
            P("section", None, None, "tensor"),
            P("section", "tensor", None),
            P("section", None, "tensor"),
            P("section", "tensor", None),
            P("section", None, "tensor"),
            P("section", "tensor"),
            P("section", None, None),
        ),
        out_specs=(
            P("section", "dp", "tensor", None),
            P("section", "dp", "tensor", None),
            P("section", None, None, "tensor"),
            P("section", "tensor", None),
            P("section", None, "tensor"),
            P("section", "tensor", None),
            P("section", None, "tensor"),
            P("section", "tensor"),
            P("section", None, None),
        ),
        check_vma=False,
    )
```

```python
import functools

import jax
import jax.numpy as jnp
from jax import lax
from jax.experimental import pallas as pl
from jax.experimental.pallas import tpu as pltpu
from jax.sharding import PartitionSpec as P

HD = 64
CH = 128
GC = 64
AROUND = (1, 1, 1)
HELP_E = (3, 2, 2)
EPS = 1e-06
MASKED = -1000000000.0
F32 = jnp.float32
BF16 = jnp.bfloat16


class Places:
    def __init__(self):
        self.count = 0

    def take(self, many=1):
        first = self.count
        self.count += many
        return first


def nn(a, b):
    return lax.dot_general(a, b, (((1,), (0,)), ((), ())), preferred_element_type=F32)


def nt(a, b):
    return lax.dot_general(a, b, (((1,), (1,)), ((), ())), preferred_element_type=F32)


def tn(a, b):
    return lax.dot_general(a, b, (((0,), (0,)), ((), ())), preferred_element_type=F32)


def normal(u):
    mean = jnp.mean(u, axis=-1, keepdims=True)
    centred = u - mean
    spread = jnp.mean(centred * centred, axis=-1, keepdims=True)
    inverse = lax.rsqrt(spread + EPS)
    return centred * inverse, inverse


def normal_back(hat, inverse, grad):
    first = jnp.mean(grad, axis=-1, keepdims=True)
    second = jnp.mean(grad * hat, axis=-1, keepdims=True)
    return inverse * (grad - first - hat * second)


def column_sum(u):
    return jnp.sum(u, axis=0, keepdims=True)


class Sizes:
    def __init__(self, n_dp, images, slots, width, piece):
        self.n_dp = n_dp
        self.images = images
        self.slots = slots
        self.width = width
        self.piece = piece
        self.block = 2 * slots
        self.rows = images * self.block
        self.pair = 2 * piece
        self.heads = self.pair // HD
        self.around = sum(AROUND)
        self.per_mat = width // GC
        self.parts = 3 * self.per_mat


def plan(z):
    p, d, n = Places(), Places(), Places()
    pieces = z.width // CH
    recv = dict(
        x=p.take(), bias=p.take(2), xc0=p.take(), xc1=p.take(), pg=p.take(),
        wy=p.take(3 * pieces), wz=p.take(3 * pieces // 2),
        d1=p.take(z.around), d2=p.take(z.around),
        e=p.take(z.images), ec=p.take(z.images),
        attn=p.take(z.images), h2=p.take(z.images), br=p.take(z.images), dbl=p.take(z.images),
        dh2=p.take(), dal=p.take(z.images), dn=p.take(z.images),
        dlat=p.take(z.images), res=p.take(), gin=p.take(),
        gy=p.take(z.parts), ga=p.take(z.parts), gb=p.take(z.parts),
        sy=p.take(), sc=p.take(), sa=p.take(), sb=p.take(),
    )
    together = ("wy", "wz", "d1", "gy", "ga", "gb", "attn", "h2", "br", "dbl", "e", "ec", "dlat", "dn", "dal")
    many = dict(bias=2, d2=z.around)
    send = {name: d.take(many.get(name, 1)) for name in recv}
    send["d3"] = d.take(z.around)
    local = {name: n.take() for name in ("w0", "wo", "w1", "w2", "x", "pg", "res", "gin", "g0", "g1", "g2")}
    return recv, send, frozenset(together), local, p.count, d.count, n.count


def body(
    z, places,
    x_ref, pg_ref, wqkv_ref, wout_ref, wu_ref, wd_ref, len_ref, mask_ref, qv_ref, mlp_ref, norm_ref,
    res_ref, gin_ref, gd_ref, gu_ref, ga_ref, small_ref,
    wown, wy, xall, pgr, qv_y, mlp_y, code_c, seen_c, cov_c, key_r,
    e_own, e_oth, h, kv, q, kk, vv, o, p, att, mid, h2, act, gp, brv, dy,
    snd, rcv, dbl, dal, dol, dq, dk, dv, g, yr, za, zb, dlat, outb, nacc, sml, small_in,
    ss, rs, ls,
):
    S, SEND, TOGETHER, LOCAL = places
    sec = lax.axis_index("section")
    dp = lax.axis_index("dp")
    t = lax.axis_index("tensor")
    y = t // 2
    c = t % 2
    to_y = {"tensor": 2 * (1 - y) + c}
    to_c = {"tensor": 2 * y + 1 - c}
    to_s = {"section": 1 - sec}
    parity = dp % 2
    pair_z = {"dp": dp + 1 - 2 * parity}
    top = dp // (z.n_dp // 2)
    to_m = {"dp": dp + 1 - 2 * top}
    to_w = {"dp": dp - 1 + 2 * top}
    is_end = jnp.logical_or(dp == 0, dp == z.n_dp - 1)
    not_end = jnp.logical_not(is_end)
    is_mid = jnp.logical_or(dp == z.n_dp // 2 - 1, dp == z.n_dp // 2)
    not_mid = jnp.logical_not(is_mid)
    enc = sec == 0
    reg = sec == 1

    I, R, D, BL, SL = z.images, z.rows, z.width, z.block, z.slots
    PC, PW = z.piece, z.pair
    KEYS = 2 * BL
    WP = D // CH
    HELP = (HELP_E, (WP // 2,) * 3)
    MOST = WP // 2

    def far(src, dst, name, to, index=0, receive=None, send=None):
        leave = SEND[send or name] + (0 if name in TOGETHER else index)
        return pltpu.make_async_remote_copy(
            src_ref=src, dst_ref=dst, send_sem=ss.at[leave], recv_sem=rs.at[S[receive or name] + index],
            device_id=to, device_id_type=pl.DeviceIdType.MESH,
        )

    def gone(ref, name, to):
        far(ref, ref, name, to).wait_send()

    def here(src, dst, name):
        return pltpu.make_async_copy(src, dst, ls.at[LOCAL[name]])

    w_refs = (wown.at[0], wu_ref, wd_ref)
    own_w = [here(w_refs[m], wown.at[m], ("w0", "w1", "w2")[m]) for m in (1, 2)]
    own_a = (here(wqkv_ref, wown.at[0, 0:3 * z.piece], "w0"), here(wout_ref, wown.at[0, 3 * z.piece:], "wo"))
    own_x = here(x_ref.at[y], xall.at[0, :, 0], "x")
    own_pg = here(pg_ref.at[y], pgr.at[0], "pg")
    for copy in (own_x, *own_a, *own_w):
        copy.start()
    own_pg.start()

    barrier = pltpu.get_barrier_semaphore()

    def greet(to):
        pl.semaphore_signal(barrier, inc=1, device_id=to, device_id_type=pl.DeviceIdType.MESH)

    greet(to_y)
    greet(to_c)
    greet(to_s)
    greet(to_m)

    @pl.when(not_end)
    def _():
        greet(to_w)
        pl.semaphore_wait(barrier, 5)

    @pl.when(is_end)
    def _():
        pl.semaphore_wait(barrier, 4)

    c_x = far(x_ref.at[1 - y], xall.at[0, :, 1], "x", to_y)
    c_b0 = far(qv_ref, qv_y, "bias", to_y)
    c_b1 = far(mlp_ref, mlp_y, "bias", to_y, 1)
    c_xc0 = far(x_ref.at[y], xall.at[1, :, 0], "xc0", to_c)
    c_xc1 = far(xall.at[0, :, 1], xall.at[1, :, 1], "xc1", to_c)
    c_pg = far(pg_ref.at[1 - y], pgr.at[1], "pg", to_y)

    def rows_of(j, side):
        return pl.ds(pl.multiple_of((j + side * (WP - 1 - 2 * j)) * CH, CH), CH)

    def w_y(m, j):
        at = rows_of(j, parity)
        return far(w_refs[m].at[at], wy.at[m, at], "wy", to_y, m * WP + j)

    def w_z(m, j, side=None):
        at = rows_of(j, parity if side is None else side)
        return far(wy.at[m, at], wy.at[m, at], "wz", pair_z, m * (WP // 2) + j)

    around = [(m, WP - HELP[0][m] - 1 - j) for m in range(3) for j in range(AROUND[m] - 1, -1, -1)]

    def d_slot(side, n):
        return g.at[side, pl.ds(n * CH, CH)]

    def d_out(n):
        m, j = around[n]
        return far(w_refs[m].at[rows_of(j, parity)], d_slot(0, n), "d1", to_s, n)

    def d_over(n):
        return far(d_slot(0, n), d_slot(1, n), "d2", to_y, n)

    def d_back(n):
        m, j = around[n]
        leave = SEND["d3"] + n
        return pltpu.make_async_remote_copy(
            src_ref=d_slot(1, n), dst_ref=wy.at[m, rows_of(j, parity)],
            send_sem=ss.at[leave], recv_sem=rs.at[S["wy"] + m * WP + j],
            device_id=to_s, device_id_type=pl.DeviceIdType.MESH,
        )

    straight = (
        [[j for j in range(WP - HELP[0][m]) if (m, j) not in around] for m in range(3)],
        [list(range(WP - HELP[1][m])) for m in range(3)],
    )

    def start_inputs():
        c_xc0.start()
        c_x.start()
        c_b0.start()
        c_b1.start()

    @pl.when(reg)
    def _():
        start_inputs()

    for copy in own_a:
        copy.wait()

    @pl.when(enc)
    def _():
        for n in range(len(around)):
            d_out(n).start()
        ahead = [(m, j) for m in range(3) for j in straight[0][m] if j < HELP[0][m]]
        behind = [(m, j) for m in range(3) for j in straight[0][m] if j >= HELP[0][m]]
        for m, j in ahead + behind:
            w_y(m, j).start()
            if (m, j) == (0, 1):
                start_inputs()

    @pl.when(reg)
    def _():
        for n in range(len(around) + 1):
            if n < len(around):
                d_out(n).wait_recv()
                d_over(n).start()
            if n > 0:
                d_over(n - 1).wait_recv()
                d_back(n - 1).start()
            if n == max(len(around) - 1, 0):
                for m in range(3):
                    for j in straight[1][m]:
                        w_y(m, j).start()
                c_pg.start()
        for n in range(len(around)):
            d_over(n).wait_send()
            d_back(n).wait_send()

    def forward_w(m, j, sections=(enc, reg)):
        for s, flag in enumerate((enc, reg)):
            if any(flag is one for one in sections) and j < HELP[s][m]:
                @pl.when(flag)
                def _():
                    w_y(m, j).wait_recv()
                    w_z(m, j).start()

    def finish_w(m):
        for s, flag in enumerate((enc, reg)):
            @pl.when(flag)
            def _():
                for j in range(HELP[s][m], WP - HELP[s][m]):
                    w_y(m, j).wait_recv()
                for j in range(HELP[s][m]):
                    w_z(m, j, 1 - parity).wait_recv()

    rank = lax.broadcasted_iota(jnp.int32, (KEYS, KEYS), 0)
    across = lax.broadcasted_iota(jnp.int32, (KEYS, KEYS), 1)
    group = rank // SL
    y_of = y + (group % 2) * (1 - 2 * y)
    c_of = c + (group // 2) * (1 - 2 * c)
    slot = (2 * y_of + c_of) * SL + rank % SL
    here_slot = slot == across
    diagonal = rank == across
    slot_col = slot[:, 0:1]
    for i in range(I):
        picked = jnp.where(here_slot, mask_ref[pl.ds(y * I + i, 1), :].astype(F32), 0.0)
        marked = jnp.sum(picked, axis=1, keepdims=True) > 0.5
        valid = slot_col < len_ref[y * I + i]
        seen = jnp.where(jnp.logical_and(valid, marked), 1.0, 0.0)
        code = jnp.where(enc, seen, jnp.zeros_like(seen))
        seen_c[i] = seen
        cov_c[i] = jnp.where(valid, 1.0, 0.0) - seen
        code_c[i] = code
        key = jnp.where(valid, code, 2.0)
        key_r[i] = jnp.sum(jnp.where(diagonal, key, 0.0), axis=0, keepdims=True)

    g0, b0 = norm_ref[0:1, :], norm_ref[1:2, :]

    def lay(block):
        return block.reshape(BL, D)

    forward_w(0, 0)
    forward_w(0, 1)
    own_x.wait()
    c_x.wait_recv()
    c_xc1.start()

    def norm_rows(half):
        def one(i, carry):
            hat, _ = normal(lay(xall[half, i]).astype(F32))
            value = (hat * g0 + b0).astype(BF16)
            h[half, i] = value
            kv[half, i] = value
            return carry

        lax.fori_loop(0, I, one, 0)

    norm_rows(0)
    c_xc0.wait_recv()
    c_xc1.wait_recv()
    norm_rows(1)
    for j in range(2, MOST):
        forward_w(0, j)
    c_b0.wait_recv()
    c_b1.wait_recv()
    finish_w(0)

    def both_rows(first, many):
        return jnp.concatenate([wown[0, first:first + many], wy[0, first:first + many]], axis=0)

    bq = jnp.concatenate([qv_ref[0:1, :], qv_y[0:1, :]], axis=1)
    bv = jnp.concatenate([qv_ref[1:2, :], qv_y[1:2, :]], axis=1)

    def flat(ref, half):
        return ref[half].reshape(R, ref.shape[-1])

    def e_hop(i):
        return far(dlat.at[0, i], e_own.at[i], "e", to_s, i)

    def e_core(i):
        return far(e_own.at[i], e_oth.at[i], "ec", to_c, i)

    for half in range(2):
        q[half] = ((nt(flat(h, half), both_rows(0, PC)) + bq).astype(BF16) * 0.125).reshape(I, BL, PW)

    lane = lax.broadcasted_iota(jnp.int32, (KEYS, 2 * HD), 1)
    lanes = (lane < HD, lane >= HD)
    zero16 = jnp.zeros((KEYS, 2 * HD), BF16)

    def image(ref, i, pr):
        at = slice(pr * 2 * HD, (pr + 1) * 2 * HD)
        return jnp.concatenate([ref[0, i, :, at], ref[1, i, :, at]], axis=0)

    def put(ref, i, pr, value):
        at = slice(pr * 2 * HD, (pr + 1) * 2 * HD)
        ref[0, i, :, at] = value[:BL]
        ref[1, i, :, at] = value[BL:]

    def latent_keys(half, ref, i):
        hat, _ = normal(ref[i].astype(F32))
        value = (hat * g0 + b0).astype(BF16)
        seen = seen_c[i, half * BL:(half + 1) * BL] > 0.5
        kv[half, i] = jnp.where(seen, value, h[half, i])

    def arrive(i):
        @pl.when(reg)
        def _():
            e_hop(i).wait_recv()
            e_core(i).start()
            latent_keys(0, e_own, i)

    def attend(i):
        @pl.when(reg)
        def _():
            e_core(i).wait_recv()
            latent_keys(1, e_oth, i)

        rows_k = kv[:, i].reshape(KEYS, D)
        kk[:, i] = nt(rows_k, both_rows(PC, PC)).astype(BF16).reshape(2, BL, PW)
        vv[:, i] = (nt(rows_k, both_rows(2 * PC, PC)) + bv).astype(BF16).reshape(2, BL, PW)
        shut = jnp.where(code_c[i] == key_r[i], 0.0, MASKED)
        for pr in range(z.heads // 2):
            qp, kp, vp = image(q, i, pr), image(kk, i, pr), image(vv, i, pr)
            outs = []
            for sub in range(2):
                scores = nt(jnp.where(lanes[sub], qp, zero16), kp) + shut
                top_value = jnp.max(scores, axis=-1, keepdims=True)
                e = jnp.exp(scores - top_value)
                probs = (e * (1.0 / jnp.sum(e, axis=-1, keepdims=True))).astype(BF16)
                p[i, 2 * pr + sub] = probs
                outs.append(nn(probs, vp))
            put(o, i, pr, jnp.where(lanes[0], outs[0], outs[1]).astype(BF16))
        attn = nn(o[:, i].reshape(KEYS, PW), both_rows(3 * PC, PC))
        snd[0, i] = attn[BL:].astype(BF16)
        exchange(0, "attn", i).start()
        att[i] = attn[:BL]

    def exchange(slot, name, i):
        return far(snd.at[slot % 2, i], rcv.at[slot, i], name, to_c, i)

    def h2_core(i):
        return far(h2.at[0, i], h2.at[1, i], "h2", to_c, i)

    def middle(i):
        exchange(0, "attn", i).wait_recv()
        attn = att[i] + rcv[0, i].astype(F32) + norm_ref[2:3, :]
        att[i] = attn
        value = lay(xall[0, i]).astype(F32) + norm_ref[3:4, :] * attn
        mid[i] = value
        hat, _ = normal(value)
        h2[0, i] = (hat * norm_ref[4:5, :] + norm_ref[5:6, :]).astype(BF16)
        h2_core(i).start()

    TW = 256
    NT = D // TW

    def rows_at(i):
        return pl.ds(i * BL, BL)

    def up(i, w, w_ref, b_row):
        rows2 = h2[:, i].reshape(KEYS, D)

        def one(n, carry):
            at = pl.ds(pl.multiple_of(n * TW, TW), TW)
            u = nn(rows2, w_ref[:, at]) + b_row[:, at]
            cdf = 0.5 + 0.5 * lax.erf(u * 0.7071067811865476)
            act[w, :, rows_at(i), at] = (u * cdf).astype(BF16).reshape(2, BL, TW)
            slope = cdf + u * (0.3989422804014327 * jnp.exp(-0.5 * u * u))
            gp[w, :, rows_at(i), at] = slope.astype(BF16).reshape(2, BL, TW)
            return carry

        lax.fori_loop(0, NT, one, 0, unroll=True)

    def own_down(i):
        br = nn(act[0, :, rows_at(i)].reshape(KEYS, D), wown[2])
        brv[i] = br[:BL]
        dy[i] = br[BL:]

    def down(i):
        br = nn(act[1, :, rows_at(i)].reshape(KEYS, D), wy[2])
        snd[1, i] = (dy[i] + br[BL:]).astype(BF16)
        exchange(1, "br", i).start()
        brv[i] = brv[i] + br[:BL]

    def finish(i):
        exchange(1, "br", i).wait_recv()
        br = brv[i] + rcv[1, i].astype(F32) + norm_ref[6:7, :]
        brv[i] = br
        out = mid[i] + norm_ref[7:8, :] * br

        @pl.when(enc)
        def _():
            dlat[0, i] = (out * seen_c[i, :BL]).astype(BF16)
            e_hop(i).start()

        outb[0, i] = (out * cov_c[i, :BL]).astype(BF16).reshape(2, SL, D)

    def own_up(i):
        h2_core(i).wait_recv()
        up(i, 0, wown.at[1], mlp_ref)

    def other_up(i):
        up(i, 1, wy.at[1], mlp_y)

    def own_back(i):
        @pl.when(reg)
        def _():
            dy[i] = jnp.concatenate([pgr[0, i], pgr[1, i]], axis=0).astype(F32) * cov_c[i, :BL]

        @pl.when(enc)
        def _():
            d_hop(i).wait_recv()
            dy[i] = dlat[1, i].astype(F32) * seen_c[i, :BL]

        dbl[0, i] = (norm_ref[7:8, :] * dy[i]).astype(BF16)
        dbl_core(i).start()

    def d_hop(i):
        return far(dlat.at[0, i], dlat.at[1, i], "dlat", to_s, i)

    def dbl_core(i):
        return far(dbl.at[0, i], dbl.at[1, i], "dbl", to_c, i)

    for j in range(MOST):
        forward_w(1, j, (reg,))
    forward_w(2, 0, (reg,))

    for i in range(I):
        arrive(i)
        if i > 0:
            middle(i - 1)
        if i == 2:
            own_w[0].wait()
            own_up(0)
        if i == 0:
            forward_w(1, 0, (enc,))
        attend(i)
        if i == 0:
            for j in range(1, MOST):
                forward_w(1, j, (enc,))
            forward_w(2, 1, (reg,))
        if i == 1:
            forward_w(2, 0, (enc,))
            forward_w(2, 2, (reg,))
    forward_w(2, 1, (enc,))
    forward_w(2, 2, (enc,))
    for i in range(1, I - 1):
        own_up(i)
    middle(I - 1)
    finish_w(1)
    for i in range(I - 1):
        other_up(i)
    own_up(I - 1)
    other_up(I - 1)
    own_w[1].wait()
    for i in range(I):
        own_down(i)
    finish_w(2)
    for i in range(I):
        down(i)
        if i > 0:
            finish(i - 1)
    own_pg.wait()

    @pl.when(reg)
    def _():
        c_pg.wait_recv()
        for i in range(I):
            own_back(i)

    finish(I - 1)
    w_o = both_rows(3 * PC, PC)

    def deliver(which, number, ref):
        return (
            here(outb.at[which, :, 0], ref.at[y], number),
            far(outb.at[which, :, 1], ref.at[y], number, to_y),
        )

    for copy in deliver(0, "res", res_ref):
        copy.start()

    nacc[...] = jnp.zeros_like(nacc)
    small_in[...] = jnp.zeros_like(small_in)

    def add_norm(row, value):
        nacc[row:row + 1, :] += value

    @pl.when(enc)
    def _():
        for i in range(I):
            own_back(i)

    def branch_sums(i, carry):
        grad = dy[i]
        add_norm(7, column_sum(grad * brv[i]))
        add_norm(6, column_sum(norm_ref[7:8, :] * grad))
        return carry

    for i in range(I):
        dbl_core(i).wait_recv()

    N = z.parts
    PM = z.per_mat

    def part(k):
        return pl.ds(pl.multiple_of(k * GC, GC), GC)

    def y_part(k):
        at = part(k)
        return far(g.at[1, at], yr.at[at], "gy", to_y, k)

    def to_middle(k):
        at = part(k)

        @pl.when(is_mid)
        def _():
            far(g.at[0, at], zb.at[at], "ga", to_m, k, receive="gb").start()

        @pl.when(not_mid)
        def _():
            far(g.at[0, at], za.at[at], "ga", to_m, k).start()

    def from_away(k):
        at = part(k)
        return far(g.at[0, at], za.at[at], "ga", to_w, k)

    def total(k):
        at = part(k)
        return far(zb.at[at], zb.at[at], "gb", to_w, k)

    def stage0(k):
        at = part(k)
        y_part(k).wait_recv()
        g[0, at, :] = (g[0, at, :].astype(F32) + yr[at, :].astype(F32)).astype(BF16)

        @pl.when(is_end)
        def _():
            to_middle(k)

    def stage1(k):
        at = part(k)

        @pl.when(not_end)
        def _():
            from_away(k).wait_recv()
            g[0, at, :] = (g[0, at, :].astype(F32) + za[at, :].astype(F32)).astype(BF16)
            to_middle(k)

    def each_out(k, do):
        for m, ref in enumerate((gd_ref, gu_ref, ga_ref)):
            @pl.when(jnp.logical_and(k >= m * PM, k < (m + 1) * PM))
            def _():
                do(here(zb.at[part(k)], ref.at[part(k - m * PM)], ("g0", "g1", "g2")[m]))

    def stage2(k):
        at = part(k)
        total(k).wait_recv()

        @pl.when(is_mid)
        def _():
            zb[at, :] = (g[0, at, :].astype(F32) + zb[at, :].astype(F32)).astype(BF16)

        @pl.when(not_end)
        def _():
            total(k).start()

        each_out(k, lambda copy: copy.start())

    AWAY_LAG = 2
    MID_LAG = 4
    LAG = 8

    def small_middle(start):
        @pl.when(is_mid)
        def _():
            copy = far(sml.at[1], sml.at[4], "sa", to_m, receive="sb")
            copy.start() if start else copy.wait_send()

        @pl.when(not_mid)
        def _():
            copy = far(sml.at[1], sml.at[3], "sa", to_m)
            copy.start() if start else copy.wait_send()

    c_sy = far(small_in, sml.at[0], "sy", to_y)
    c_sc = far(sml.at[1], sml.at[2], "sc", to_c)
    s_total = far(sml.at[4], sml.at[4], "sb", to_w)

    def small0():
        c_sy.wait_recv()
        sml[1, 0:8, :] = small_in[0:8, :] + sml[0, 0:8, :]
        sml[1, 8:9, :] = small_in[8:9, :] + sml[0, 9:10, :]
        sml[1, 9:10, :] = jnp.zeros((1, D), F32)
        sml[1, 10:12, :] = small_in[10:12, :]
        sml[1, 12:14, :] = sml[0, 10:12, :]
        sml[1, 14:16, :] = jnp.zeros((2, D), F32)
        c_sc.start()

    def small1():
        c_sc.wait()
        sml[1, 0:8, :] = sml[1, 0:8, :] + sml[2, 0:8, :]

        @pl.when(is_end)
        def _():
            small_middle(True)

    def small2():
        @pl.when(not_end)
        def _():
            far(sml.at[1], sml.at[3], "sa", to_w).wait_recv()
            sml[1] = sml[1] + sml[3]
            small_middle(True)

    def small3():
        s_total.wait_recv()

        @pl.when(is_mid)
        def _():
            sml[4] = sml[1] + sml[4]

        @pl.when(not_end)
        def _():
            s_total.start()

        small_ref[...] = sml[4]

    def step(k, carry=0):
        @pl.when(k < N)
        def _():
            stage0(k)

        @pl.when(jnp.logical_and(k >= AWAY_LAG, k < N + AWAY_LAG))
        def _():
            stage1(k - AWAY_LAG)

        @pl.when(jnp.logical_and(is_mid, jnp.logical_and(k >= MID_LAG, k < N + MID_LAG)))
        def _():
            stage2(k - MID_LAG)

        @pl.when(jnp.logical_and(not_mid, jnp.logical_and(k >= LAG, k < N + LAG)))
        def _():
            stage2(k - LAG)

        pl.when(k == N - 6)(small0)
        pl.when(k == N - 5)(small1)
        pl.when(k == N - 4)(small2)
        pl.when(jnp.logical_and(is_mid, k == N - 2))(small3)
        pl.when(jnp.logical_and(not_mid, k == N))(small3)
        return carry

    done_steps = [0]

    def pump(many, index=0, times=1):
        first = done_steps[0] + index * many
        done_steps[0] += many * times

        @pl.when(enc)
        def _():
            lax.fori_loop(first, first + many, step, 0)

    first_down, first_up, first_attn = 0, PM, 2 * PM
    PT = TW // GC

    def outer_rows(left, right, w, first):
        def one(n, carry):
            at = pl.ds(pl.multiple_of(n * TW, TW), TW)
            to = pl.ds(pl.multiple_of(first * GC + n * TW, TW), TW)
            g[w, to, :] = tn(left(at), right()).astype(BF16)
            if w == 1:
                for k in range(PT):
                    y_part(first + n * PT + k).start()
            return carry

        lax.fori_loop(0, NT, one, 0, unroll=True)

    def wide(ref, w):
        return lambda at: ref[w, :, :, at].reshape(2 * R, at.size)

    def h2_cols(at):
        return jnp.concatenate(
            [h2[0, :, :, at].reshape(R, at.size), h2[1, :, :, at].reshape(R, at.size)], axis=0
        )

    def down_outer(w):
        outer_rows(wide(act, w), lambda: dbl[...].reshape(2 * R, D), w, first_down)

    def up_outer(w):
        outer_rows(h2_cols, lambda: gp[w].reshape(2 * R, D), w, first_up)

    @pl.when(enc)
    def _():
        down_outer(1)
        down_outer(0)

    def down_back(half, w, w_ref):
        rows = flat(dbl, half)

        def one(n, carry):
            at = pl.ds(pl.multiple_of(n * TW, TW), TW)
            du = nt(rows, w_ref[at, :]) * gp[w, half, :, at].astype(F32)
            small_in[8 + w:9 + w, at] += column_sum(du)
            gp[w, half, :, at] = du.astype(BF16)
            return carry

        lax.fori_loop(0, NT, one, 0, unroll=True)

    down_back(1, 1, wy.at[2])
    pump(1)
    down_back(1, 0, wown.at[2])
    pump(1)

    def up_back(half):
        return nt(gp[0, half], wown[1]) + nt(gp[1, half], wy[1])

    gone(snd.at[0], "attn", to_c)
    snd[0] = up_back(1).astype(BF16).reshape(I, BL, D)
    c_dh2 = far(snd.at[0], rcv.at[2], "dh2", to_c)
    c_dh2.start()
    lax.fori_loop(0, I, branch_sums, 0)
    pump(1)
    down_back(0, 1, wy.at[2])
    pump(1)
    down_back(0, 0, wown.at[2])

    @pl.when(enc)
    def _():
        up_outer(1)

    pump(1)

    @pl.when(enc)
    def _():
        up_outer(0)

    pump(1)
    back0 = up_back(0).reshape(I, BL, D)
    c_dh2.wait_recv()

    def dal_core(i):
        return far(dal.at[0, i], dal.at[1, i], "dal", to_c, i)

    for i in range(I):
        grad = back0[i] + rcv[2, i].astype(F32)
        hat, inverse = normal(mid[i])
        add_norm(4, column_sum(grad * hat))
        add_norm(5, column_sum(grad))
        d_mid = dy[i] + normal_back(hat, inverse, grad * norm_ref[4:5, :])
        dy[i] = d_mid
        add_norm(3, column_sum(d_mid * att[i]))
        d_att = norm_ref[3:4, :] * d_mid
        add_norm(2, column_sum(d_att))
        dal[0, i] = d_att.astype(BF16)
        dal_core(i).start()
    pump(1)

    def all_rows(ref):
        return ref[...].reshape(2 * R, ref.shape[-1])

    base = first_attn * GC

    def store_rows(value, first):
        g[0, base + first:base + first + PC, :] = value[:PC].astype(BF16)
        g[1, base + first:base + first + PC, :] = value[PC:].astype(BF16)

    def attend_back(i, between):
        dal_core(i).wait_recv()
        dol[:, i] = nt(dal[:, i].reshape(KEYS, D), w_o).astype(BF16).reshape(2, BL, PW)
        for pr in range(z.heads // 2):
            qp, kp, vp, gpair = image(q, i, pr), image(kk, i, pr), image(vv, i, pr), image(dol, i, pr)
            at = slice(pr * 2 * HD, (pr + 1) * 2 * HD)
            dqs, dks, dvs = [], [], []
            for sub in range(2):
                probs = p[i, 2 * pr + sub]
                wide_probs = probs.astype(F32)
                d_probs = nt(jnp.where(lanes[sub], gpair, zero16), vp)
                dvs.append(tn(probs, gpair))
                inner = jnp.sum(d_probs * wide_probs, axis=-1, keepdims=True)
                ds = (wide_probs * (d_probs - inner)).astype(BF16)
                dqs.append(nn(ds, kp))
                dks.append(tn(ds, qp))
            d_q = jnp.where(lanes[0], dqs[0], dqs[1]) * 0.125
            d_k = jnp.where(lanes[0], dks[0], dks[1])
            d_v = jnp.where(lanes[0], dvs[0], dvs[1])
            small_in[10:11, at] += column_sum(d_q)
            small_in[11:12, at] += column_sum(d_v)
            put(dq, i, pr, d_q.astype(BF16))
            put(dk, i, pr, d_k.astype(BF16))
            put(dv, i, pr, d_v.astype(BF16))
            if pr == 1:
                between()

    def dn_core(i):
        return far(snd.at[1, i], rcv.at[3, i], "dn", to_c, i)

    def input_back(i):
        grad = nn(dq[:, i].reshape(KEYS, PW), both_rows(0, PC))
        grad += nn(dk[:, i].reshape(KEYS, PW), both_rows(PC, PC))
        grad += nn(dv[:, i].reshape(KEYS, PW), both_rows(2 * PC, PC))
        snd[1, i] = grad[BL:].astype(BF16)
        dn_core(i).start()
        back1[i] = grad[:BL]

    def leave(i):
        dn_core(i).wait_recv()
        grad = back1[i] + rcv[3, i].astype(F32)
        extra = jnp.logical_and(seen_c[i, :BL] > 0.5, reg)

        @pl.when(reg)
        def _():
            other = jnp.where(extra, grad, 0.0)
            hat, inverse = normal(e_own[i].astype(F32))
            dlat[0, i] = normal_back(hat, inverse, other * g0).astype(BF16)
            d_hop(i).start()
            add_norm(0, column_sum(other * hat))
            add_norm(1, column_sum(other))

        own = jnp.where(extra, 0.0, grad)
        hat, inverse = normal(lay(xall[0, i]).astype(F32))
        add_norm(0, column_sum(own * hat))
        add_norm(1, column_sum(own))
        d_x = dy[i] + normal_back(hat, inverse, own * g0)
        outb[1, i] = d_x.astype(BF16).reshape(2, SL, D)

    back1 = brv
    gone(snd.at[1], "br", to_c)
    for i in range(I):
        attend_back(i, functools.partial(leave, i - 1) if i > 0 else lambda: None)
        pump(1)
        input_back(i)
        pump(1)
    leave(I - 1)
    pump(1)

    @pl.when(reg)
    def _():
        down_outer(1)
        down_outer(0)
        up_outer(1)
        up_outer(0)

    store_rows(tn(all_rows(dq), all_rows(h)), 0)
    pump(1)
    store_rows(tn(all_rows(dk), all_rows(kv)), PC)
    pump(1)
    store_rows(tn(all_rows(dv), all_rows(kv)), 2 * PC)
    pump(1)
    store_rows(tn(all_rows(o), all_rows(dal)), 3 * PC)
    small_in[0:8, :] = nacc[...]
    c_sy.start()
    for k in range(first_attn, z.parts):
        y_part(k).start()
    for copy in deliver(1, "gin", gin_ref):
        copy.start()

    lax.fori_loop(jnp.where(enc, done_steps[0], 0), N + LAG, step, 0)

    small_middle(False)
    gone(g.at[1], "gy", to_y)
    gone(g.at[0], "ga", to_m)

    @pl.when(not_end)
    def _():
        s_total.wait_send()
        gone(zb, "gb", to_w)

    c_sy.wait_send()
    for m, ref in enumerate((gd_ref, gu_ref, ga_ref)):
        here(zb.at[0:D], ref, ("g0", "g1", "g2")[m]).wait()
    for which, number, ref in ((0, "res", res_ref), (1, "gin", gin_ref)):
        for copy in deliver(which, number, ref):
            copy.wait()
    for copy in (c_x, c_b0, c_b1, c_xc0, c_xc1, c_dh2):
        copy.wait_send()
    gone(h2.at[0], "h2", to_c)
    gone(dbl.at[0], "dbl", to_c)
    gone(dal.at[0], "dal", to_c)
    gone(snd.at[1], "dn", to_c)

    @pl.when(enc)
    def _():
        if around:
            gone(g.at[0, 0:len(around) * CH], "d1", to_s)
        gone(e_own, "e", to_s)

    @pl.when(reg)
    def _():
        c_pg.wait_send()
        gone(e_own, "ec", to_c)
        gone(dlat.at[0], "dlat", to_s)

    for s, flag in enumerate((enc, reg)):
        @pl.when(flag)
        def _():
            gone(g.at[0, 0:sum(len(js) for js in straight[s]) * CH], "wy", to_y)
            gone(g.at[0, 0:sum(HELP[s]) * CH], "wz", pair_z)


def fused(z, x, pg, wqkv, wout, wu, wd, lengths, mask, qv, mlp, norms):
    *places, arrivals, departures, copies = plan(z)
    I, R, D, BL, SL = z.images, z.rows, z.width, z.block, z.slots
    PC, PW = z.piece, z.pair
    KEYS = 2 * BL
    vm = pl.BlockSpec(memory_space=pltpu.VMEM)
    sm = pl.BlockSpec(memory_space=pltpu.SMEM)
    hbm = pl.BlockSpec(memory_space=pl.ANY)

    def b16(*shape):
        return pltpu.VMEM(shape, BF16)

    def f32(*shape):
        return pltpu.VMEM(shape, F32)

    scratch = [
        b16(3, D, D), b16(3, D, D),
        b16(2, I, 2, SL, D),
        b16(2, I, SL, D),
        f32(2, PC), f32(1, D),
        f32(I, KEYS, 1), f32(I, KEYS, 1), f32(I, KEYS, 1), f32(I, 1, KEYS),
        b16(I, BL, D), b16(I, BL, D),
        b16(2, I, BL, D), b16(2, I, BL, D),
        b16(2, I, BL, PW), b16(2, I, BL, PW), b16(2, I, BL, PW), b16(2, I, BL, PW),
        b16(I, z.heads, KEYS, KEYS),
        f32(I, BL, D), f32(I, BL, D),
        b16(2, I, BL, D),
        b16(2, 2, R, D), b16(2, 2, R, D),
        f32(I, BL, D), f32(I, BL, D),
        b16(2, I, BL, D), b16(4, I, BL, D),
        b16(2, I, BL, D), b16(2, I, BL, D),
        b16(2, I, BL, PW), b16(2, I, BL, PW), b16(2, I, BL, PW), b16(2, I, BL, PW),
        b16(2, 3 * D, D),
        b16(3 * D, D), b16(3 * D, D), b16(3 * D, D),
        b16(2, I, BL, D),
        b16(2, I, 2, SL, D),
        f32(8, D), f32(5, 16, D), f32(16, D),
        pltpu.SemaphoreType.DMA((departures,)),
        pltpu.SemaphoreType.DMA((arrivals,)),
        pltpu.SemaphoreType.DMA((copies,)),
    ]
    weight = jax.ShapeDtypeStruct((D, D), BF16)
    rows = jax.ShapeDtypeStruct((2, I, SL, D), BF16)
    return pl.pallas_call(
        functools.partial(body, z, places),
        out_shape=(rows, rows, weight, weight, weight, jax.ShapeDtypeStruct((16, D), F32)),
        in_specs=[hbm] * 6 + [sm] + [vm] * 4,
        out_specs=(hbm, hbm, hbm, hbm, hbm, vm),
        scratch_shapes=scratch,
        compiler_params=pltpu.CompilerParams(
            collective_id=0, has_side_effects=True, vmem_limit_bytes=121 * 2**19
        ),
    )(x, pg, wqkv, wout, wu, wd, lengths, mask, qv, mlp, norms)


def widen(
    piece, n_qkv,
    res, gin, gd, gu, ga, small,
    o_res, o_gin, o_down, o_up, o_qkv, o_out, o_qv, o_mlp, o_norms,
):
    n = pl.program_id(0)
    o_res[...] = res[...]
    o_gin[...] = gin[...].astype(F32)
    o_down[...] = gd[...].astype(F32)
    o_up[...] = gu[...].astype(F32)

    @pl.when(n < n_qkv)
    def _():
        o_qkv[...] = ga[...].astype(F32)

    @pl.when(n >= n_qkv)
    def _():
        o_out[...] = ga[...].astype(F32)

    @pl.when(n == 0)
    def _():
        o_qv[...] = small[10:12, :piece] + small[12:14, piece:2 * piece]
        o_mlp[...] = small[8:9, :]
        o_norms[...] = small[0:8, :]


def outputs(z, res, gin, gd, gu, ga, small):
    D, PC = z.width, z.piece
    tile = 192
    steps = D // tile
    n_qkv = 3 * PC // tile
    token_rows = 2 * z.images * z.slots
    token_tile = token_rows // steps
    tokens = pl.BlockSpec((token_tile, D), lambda n: (n, 0))
    rows = pl.BlockSpec((tile, D), lambda n: (n, 0))
    once = lambda *shape: pl.BlockSpec(shape, lambda n: (0, 0))
    first = pl.BlockSpec((tile, D), lambda n: (jnp.minimum(n, n_qkv - 1), 0))
    last = pl.BlockSpec((tile, D), lambda n: (jnp.maximum(n - n_qkv, 0), 0))
    shape = jax.ShapeDtypeStruct
    return pl.pallas_call(
        functools.partial(widen, PC, n_qkv),
        grid=(steps,),
        out_shape=(
            shape((token_rows, D), BF16), shape((token_rows, D), F32), shape((D, D), F32), shape((D, D), F32),
            shape((3 * PC, D), F32), shape((PC, D), F32), shape((2, PC), F32), shape((1, D), F32), shape((8, D), F32),
        ),
        in_specs=[tokens, tokens, rows, rows, rows, once(16, D)],
        out_specs=(tokens, tokens, rows, rows, first, last, once(2, PC), once(1, D), once(8, D)),
    )(res.reshape(token_rows, D), gin.reshape(token_rows, D), gd, gu, ga, small)


def local(
    n_dp,
    block_in, lengths, patch_mask, pred_grad, w_qkv, w_out, w_up, w_down, qv_bias, mlp_bias, norms
):
    images, slots, width = block_in.shape[1:]
    piece = w_qkv.shape[3]
    z = Sizes(n_dp, images // 2, slots, width, piece)

    x = block_in.reshape(2, z.images, slots, width)
    pg = pred_grad.reshape(2, z.images, slots, width)
    wqkv = jnp.swapaxes(w_qkv[0], 1, 2).reshape(3 * piece, width)
    summed = fused(
        z, x, pg, wqkv, w_out[0], w_up[0], w_down[0], lengths, patch_mask, qv_bias[0], mlp_bias, norms[0]
    )
    res, gin, g_down, g_up, g_qkv, g_out, g_qv, g_mlp, g_norms = outputs(z, *summed)
    return (
        res.reshape(1, images, slots, width),
        gin.reshape(1, images, slots, width),
        jnp.swapaxes(g_qkv.reshape(3, piece, width), 1, 2)[None],
        g_out[None],
        g_up[None],
        g_down[None],
        g_qv[None],
        g_mlp,
        g_norms[None],
    )


def solution(mesh):
    return jax.shard_map(
        functools.partial(local, mesh.shape["dp"]),
        mesh=mesh,
        in_specs=(
            P("section", "dp", "tensor", None),
            P("dp"),
            P("dp", None),
            P("dp", "tensor", None),
            P("section", None, None, "tensor"),
            P("section", "tensor", None),
            P("section", None, "tensor"),
            P("section", "tensor", None),
            P("section", None, "tensor"),
            P("section", "tensor"),
            P("section", None, None),
        ),
        out_specs=(
            P("section", "dp", "tensor", None),
            P("section", "dp", "tensor", None),
            P("section", None, None, "tensor"),
            P("section", "tensor", None),
            P("section", None, "tensor"),
            P("section", "tensor", None),
            P("section", None, "tensor"),
            P("section", "tensor"),
            P("section", None, None),
        ),
        check_vma=False,
    )
```

```python
import functools

import jax
import jax.numpy as jnp
from jax import lax
from jax.experimental import pallas as pl
from jax.experimental.pallas import tpu as pltpu
from jax.sharding import PartitionSpec as P

HD = 64
CH = 128
GC = 64
AROUND = (1, 1, 1)
HELP_E = (3, 2, 2)
EPS = 1e-06
MASKED = -1000000000.0
F32 = jnp.float32
BF16 = jnp.bfloat16


class Places:
    def __init__(self):
        self.count = 0

    def take(self, many=1):
        first = self.count
        self.count += many
        return first


def nn(a, b):
    return lax.dot_general(a, b, (((1,), (0,)), ((), ())), preferred_element_type=F32)


def nt(a, b):
    return lax.dot_general(a, b, (((1,), (1,)), ((), ())), preferred_element_type=F32)


def tn(a, b):
    return lax.dot_general(a, b, (((0,), (0,)), ((), ())), preferred_element_type=F32)


def normal(u):
    mean = jnp.mean(u, axis=-1, keepdims=True)
    centred = u - mean
    spread = jnp.mean(centred * centred, axis=-1, keepdims=True)
    inverse = lax.rsqrt(spread + EPS)
    return centred * inverse, inverse


def normal_back(hat, inverse, grad):
    first = jnp.mean(grad, axis=-1, keepdims=True)
    second = jnp.mean(grad * hat, axis=-1, keepdims=True)
    return inverse * (grad - first - hat * second)


def column_sum(u):
    return jnp.sum(u, axis=0, keepdims=True)


class Sizes:
    def __init__(self, n_dp, images, slots, width, piece):
        self.n_dp = n_dp
        self.images = images
        self.slots = slots
        self.width = width
        self.piece = piece
        self.block = 2 * slots
        self.rows = images * self.block
        self.pair = 2 * piece
        self.heads = self.pair // HD
        self.around = sum(AROUND)
        self.per_mat = width // GC
        self.parts = 3 * self.per_mat


def plan(z):
    p, d, n = Places(), Places(), Places()
    pieces = z.width // CH
    recv = dict(
        x=p.take(), bias=p.take(2), xc0=p.take(), xc1=p.take(), pg=p.take(),
        wy=p.take(3 * pieces), wz=p.take(3 * pieces // 2),
        d1=p.take(z.around), d2=p.take(z.around),
        e=p.take(z.images), ec=p.take(z.images),
        attn=p.take(z.images), h2=p.take(z.images), br=p.take(z.images), dbl=p.take(z.images),
        dh2=p.take(), dal=p.take(z.images), dn=p.take(z.images),
        dlat=p.take(z.images), res=p.take(), gin=p.take(),
        gy=p.take(z.parts), ga=p.take(z.parts), gb=p.take(z.parts),
        sy=p.take(), sc=p.take(), sa=p.take(), sb=p.take(),
    )
    together = ("wy", "wz", "d1", "gy", "ga", "gb", "attn", "h2", "br", "dbl", "e", "ec", "dlat", "dn", "dal")
    many = dict(bias=2, d2=z.around)
    send = {name: d.take(many.get(name, 1)) for name in recv}
    send["d3"] = d.take(z.around)
    local = {name: n.take() for name in ("w0", "wo", "w1", "w2", "x", "pg", "res", "gin", "g0", "g1", "g2")}
    return recv, send, frozenset(together), local, p.count, d.count, n.count


def body(
    z, places,
    x_ref, pg_ref, wqkv_ref, wout_ref, wu_ref, wd_ref, len_ref, mask_ref, qv_ref, mlp_ref, norm_ref,
    res_ref, gin_ref, gd_ref, gu_ref, ga_ref, small_ref,
    wown, wy, xall, pgr, qv_y, mlp_y, code_c, seen_c, cov_c, key_r,
    e_own, e_oth, h, kv, q, kk, vv, o, p, att, mid, h2, act, gp, brv, dy,
    snd, rcv, dbl, dal, dol, dq, dk, dv, g, yr, za, zb, dlat, outb, nacc, sml, small_in,
    ss, rs, ls,
):
    S, SEND, TOGETHER, LOCAL = places
    sec = lax.axis_index("section")
    dp = lax.axis_index("dp")
    t = lax.axis_index("tensor")
    y = t // 2
    c = t % 2
    to_y = {"tensor": 2 * (1 - y) + c}
    to_c = {"tensor": 2 * y + 1 - c}
    to_s = {"section": 1 - sec}
    parity = dp % 2
    pair_z = {"dp": dp + 1 - 2 * parity}
    top = dp // (z.n_dp // 2)
    to_m = {"dp": dp + 1 - 2 * top}
    to_w = {"dp": dp - 1 + 2 * top}
    is_end = jnp.logical_or(dp == 0, dp == z.n_dp - 1)
    not_end = jnp.logical_not(is_end)
    is_mid = jnp.logical_or(dp == z.n_dp // 2 - 1, dp == z.n_dp // 2)
    not_mid = jnp.logical_not(is_mid)
    enc = sec == 0
    reg = sec == 1

    I, R, D, BL, SL = z.images, z.rows, z.width, z.block, z.slots
    PC, PW = z.piece, z.pair
    KEYS = 2 * BL
    WP = D // CH
    HELP = (HELP_E, (WP // 2,) * 3)
    MOST = WP // 2

    def far(src, dst, name, to, index=0, receive=None, send=None):
        leave = SEND[send or name] + (0 if name in TOGETHER else index)
        return pltpu.make_async_remote_copy(
            src_ref=src, dst_ref=dst, send_sem=ss.at[leave], recv_sem=rs.at[S[receive or name] + index],
            device_id=to, device_id_type=pl.DeviceIdType.MESH,
        )

    def gone(ref, name, to):
        far(ref, ref, name, to).wait_send()

    def here(src, dst, name):
        return pltpu.make_async_copy(src, dst, ls.at[LOCAL[name]])

    w_refs = (wown.at[0], wu_ref, wd_ref)
    own_w = [here(w_refs[m], wown.at[m], ("w0", "w1", "w2")[m]) for m in (1, 2)]
    own_a = (here(wqkv_ref, wown.at[0, 0:3 * z.piece], "w0"), here(wout_ref, wown.at[0, 3 * z.piece:], "wo"))
    own_x = here(x_ref.at[y], xall.at[0, :, 0], "x")
    own_pg = here(pg_ref.at[y], pgr.at[0], "pg")
    for copy in (own_x, *own_a, *own_w):
        copy.start()
    own_pg.start()

    barrier = pltpu.get_barrier_semaphore()

    def greet(to):
        pl.semaphore_signal(barrier, inc=1, device_id=to, device_id_type=pl.DeviceIdType.MESH)

    greet(to_y)
    greet(to_c)
    greet(to_s)
    greet(to_m)

    @pl.when(not_end)
    def _():
        greet(to_w)
        pl.semaphore_wait(barrier, 5)

    @pl.when(is_end)
    def _():
        pl.semaphore_wait(barrier, 4)

    c_x = far(x_ref.at[1 - y], xall.at[0, :, 1], "x", to_y)
    c_b0 = far(qv_ref, qv_y, "bias", to_y)
    c_b1 = far(mlp_ref, mlp_y, "bias", to_y, 1)
    c_xc0 = far(x_ref.at[y], xall.at[1, :, 0], "xc0", to_c)
    c_xc1 = far(xall.at[0, :, 1], xall.at[1, :, 1], "xc1", to_c)
    c_pg = far(pg_ref.at[1 - y], pgr.at[1], "pg", to_y)

    def rows_of(j, side):
        return pl.ds(pl.multiple_of((j + side * (WP - 1 - 2 * j)) * CH, CH), CH)

    def w_y(m, j):
        at = rows_of(j, parity)
        return far(w_refs[m].at[at], wy.at[m, at], "wy", to_y, m * WP + j)

    def w_z(m, j, side=None):
        at = rows_of(j, parity if side is None else side)
        return far(wy.at[m, at], wy.at[m, at], "wz", pair_z, m * (WP // 2) + j)

    around = [(m, WP - HELP[0][m] - 1 - j) for m in range(3) for j in range(AROUND[m] - 1, -1, -1)]

    def d_slot(side, n):
        return g.at[side, pl.ds(n * CH, CH)]

    def d_out(n):
        m, j = around[n]
        return far(w_refs[m].at[rows_of(j, parity)], d_slot(0, n), "d1", to_s, n)

    def d_over(n):
        return far(d_slot(0, n), d_slot(1, n), "d2", to_y, n)

    def d_back(n):
        m, j = around[n]
        leave = SEND["d3"] + n
        return pltpu.make_async_remote_copy(
            src_ref=d_slot(1, n), dst_ref=wy.at[m, rows_of(j, parity)],
            send_sem=ss.at[leave], recv_sem=rs.at[S["wy"] + m * WP + j],
            device_id=to_s, device_id_type=pl.DeviceIdType.MESH,
        )

    straight = (
        [[j for j in range(WP - HELP[0][m]) if (m, j) not in around] for m in range(3)],
        [list(range(WP - HELP[1][m])) for m in range(3)],
    )

    def start_inputs():
        c_xc0.start()
        c_x.start()
        c_b0.start()
        c_b1.start()

    @pl.when(reg)
    def _():
        start_inputs()

    for copy in own_a:
        copy.wait()

    @pl.when(enc)
    def _():
        for n in range(len(around)):
            d_out(n).start()
        ahead = [(m, j) for m in range(3) for j in straight[0][m] if j < HELP[0][m]]
        behind = [(m, j) for m in range(3) for j in straight[0][m] if j >= HELP[0][m]]
        for m, j in ahead + behind:
            w_y(m, j).start()
            if (m, j) == (0, 1):
                start_inputs()

    @pl.when(reg)
    def _():
        for n in range(len(around) + 1):
            if n < len(around):
                d_out(n).wait_recv()
                d_over(n).start()
            if n > 0:
                d_over(n - 1).wait_recv()
                d_back(n - 1).start()
            if n == max(len(around) - 1, 0):
                for m in range(3):
                    for j in straight[1][m]:
                        w_y(m, j).start()
                c_pg.start()
        for n in range(len(around)):
            d_over(n).wait_send()
            d_back(n).wait_send()

    def forward_w(m, j, sections=(enc, reg)):
        for s, flag in enumerate((enc, reg)):
            if any(flag is one for one in sections) and j < HELP[s][m]:
                @pl.when(flag)
                def _():
                    w_y(m, j).wait_recv()
                    w_z(m, j).start()

    def finish_w(m):
        for s, flag in enumerate((enc, reg)):
            @pl.when(flag)
            def _():
                for j in range(HELP[s][m], WP - HELP[s][m]):
                    w_y(m, j).wait_recv()
                for j in range(HELP[s][m]):
                    w_z(m, j, 1 - parity).wait_recv()

    rank = lax.broadcasted_iota(jnp.int32, (KEYS, KEYS), 0)
    across = lax.broadcasted_iota(jnp.int32, (KEYS, KEYS), 1)
    group = rank // SL
    y_of = y + (group % 2) * (1 - 2 * y)
    c_of = c + (group // 2) * (1 - 2 * c)
    slot = (2 * y_of + c_of) * SL + rank % SL
    here_slot = slot == across
    diagonal = rank == across
    slot_col = slot[:, 0:1]
    for i in range(I):
        picked = jnp.where(here_slot, mask_ref[pl.ds(y * I + i, 1), :].astype(F32), 0.0)
        marked = jnp.sum(picked, axis=1, keepdims=True) > 0.5
        valid = slot_col < len_ref[y * I + i]
        seen = jnp.where(jnp.logical_and(valid, marked), 1.0, 0.0)
        code = jnp.where(enc, seen, jnp.zeros_like(seen))
        seen_c[i] = seen
        cov_c[i] = jnp.where(valid, 1.0, 0.0) - seen
        code_c[i] = code
        key = jnp.where(valid, code, 2.0)
        key_r[i] = jnp.sum(jnp.where(diagonal, key, 0.0), axis=0, keepdims=True)

    g0, b0 = norm_ref[0:1, :], norm_ref[1:2, :]

    def lay(block):
        return block.reshape(BL, D)

    forward_w(0, 0)
    forward_w(0, 1)
    own_x.wait()
    c_x.wait_recv()
    c_xc1.start()

    def norm_rows(half):
        def one(i, carry):
            hat, _ = normal(lay(xall[half, i]).astype(F32))
            value = (hat * g0 + b0).astype(BF16)
            h[half, i] = value
            kv[half, i] = value
            return carry

        lax.fori_loop(0, I, one, 0)

    norm_rows(0)
    c_xc0.wait_recv()
    c_xc1.wait_recv()
    norm_rows(1)
    for j in range(2, MOST):
        forward_w(0, j)
    c_b0.wait_recv()
    c_b1.wait_recv()
    finish_w(0)

    def both_rows(first, many):
        return jnp.concatenate([wown[0, first:first + many], wy[0, first:first + many]], axis=0)

    bq = jnp.concatenate([qv_ref[0:1, :], qv_y[0:1, :]], axis=1)
    bv = jnp.concatenate([qv_ref[1:2, :], qv_y[1:2, :]], axis=1)

    def flat(ref, half):
        return ref[half].reshape(R, ref.shape[-1])

    def e_hop(i):
        return far(dlat.at[0, i], e_own.at[i], "e", to_s, i)

    def e_core(i):
        return far(e_own.at[i], e_oth.at[i], "ec", to_c, i)

    for half in range(2):
        q[half] = ((nt(flat(h, half), both_rows(0, PC)) + bq).astype(BF16) * 0.125).reshape(I, BL, PW)

    lane = lax.broadcasted_iota(jnp.int32, (KEYS, 2 * HD), 1)
    lanes = (lane < HD, lane >= HD)
    zero16 = jnp.zeros((KEYS, 2 * HD), BF16)

    def image(ref, i, pr):
        at = slice(pr * 2 * HD, (pr + 1) * 2 * HD)
        return jnp.concatenate([ref[0, i, :, at], ref[1, i, :, at]], axis=0)

    def put(ref, i, pr, value):
        at = slice(pr * 2 * HD, (pr + 1) * 2 * HD)
        ref[0, i, :, at] = value[:BL]
        ref[1, i, :, at] = value[BL:]

    def latent_keys(half, ref, i):
        hat, _ = normal(ref[i].astype(F32))
        value = (hat * g0 + b0).astype(BF16)
        seen = seen_c[i, half * BL:(half + 1) * BL] > 0.5
        kv[half, i] = jnp.where(seen, value, h[half, i])

    def arrive(i):
        @pl.when(reg)
        def _():
            e_hop(i).wait_recv()
            e_core(i).start()
            latent_keys(0, e_own, i)

    def attend(i):
        @pl.when(reg)
        def _():
            e_core(i).wait_recv()
            latent_keys(1, e_oth, i)

        rows_k = kv[:, i].reshape(KEYS, D)
        kk[:, i] = nt(rows_k, both_rows(PC, PC)).astype(BF16).reshape(2, BL, PW)
        vv[:, i] = (nt(rows_k, both_rows(2 * PC, PC)) + bv).astype(BF16).reshape(2, BL, PW)
        shut = jnp.where(code_c[i] == key_r[i], 0.0, MASKED)
        for pr in range(z.heads // 2):
            qp, kp, vp = image(q, i, pr), image(kk, i, pr), image(vv, i, pr)
            outs = []
            for sub in range(2):
                scores = nt(jnp.where(lanes[sub], qp, zero16), kp) + shut
                top_value = jnp.max(scores, axis=-1, keepdims=True)
                e = jnp.exp(scores - top_value)
                probs = (e * (1.0 / jnp.sum(e, axis=-1, keepdims=True))).astype(BF16)
                p[i, 2 * pr + sub] = probs
                outs.append(nn(probs, vp))
            put(o, i, pr, jnp.where(lanes[0], outs[0], outs[1]).astype(BF16))
        attn = nn(o[:, i].reshape(KEYS, PW), both_rows(3 * PC, PC))
        snd[0, i] = attn[BL:].astype(BF16)
        exchange(0, "attn", i).start()
        att[i] = attn[:BL]

    def exchange(slot, name, i):
        return far(snd.at[slot % 2, i], rcv.at[slot, i], name, to_c, i)

    def h2_core(i):
        return far(h2.at[0, i], h2.at[1, i], "h2", to_c, i)

    def middle(i):
        exchange(0, "attn", i).wait_recv()
        attn = att[i] + rcv[0, i].astype(F32) + norm_ref[2:3, :]
        att[i] = attn
        value = lay(xall[0, i]).astype(F32) + norm_ref[3:4, :] * attn
        mid[i] = value
        hat, _ = normal(value)
        h2[0, i] = (hat * norm_ref[4:5, :] + norm_ref[5:6, :]).astype(BF16)
        h2_core(i).start()

    TW = 256
    NT = D // TW

    def rows_at(i):
        return pl.ds(i * BL, BL)

    def up(i, w, w_ref, b_row):
        rows2 = h2[:, i].reshape(KEYS, D)

        def one(n, carry):
            at = pl.ds(pl.multiple_of(n * TW, TW), TW)
            u = nn(rows2, w_ref[:, at]) + b_row[:, at]
            cdf = 0.5 + 0.5 * lax.erf(u * 0.7071067811865476)
            act[w, :, rows_at(i), at] = (u * cdf).astype(BF16).reshape(2, BL, TW)
            slope = cdf + u * (0.3989422804014327 * jnp.exp(-0.5 * u * u))
            gp[w, :, rows_at(i), at] = slope.astype(BF16).reshape(2, BL, TW)
            return carry

        lax.fori_loop(0, NT, one, 0, unroll=True)

    def own_down(i):
        br = nn(act[0, :, rows_at(i)].reshape(KEYS, D), wown[2])
        brv[i] = br[:BL]
        dy[i] = br[BL:]

    def down(i):
        br = nn(act[1, :, rows_at(i)].reshape(KEYS, D), wy[2])
        snd[1, i] = (dy[i] + br[BL:]).astype(BF16)
        exchange(1, "br", i).start()
        brv[i] = brv[i] + br[:BL]

    def finish(i):
        exchange(1, "br", i).wait_recv()
        br = brv[i] + rcv[1, i].astype(F32) + norm_ref[6:7, :]
        brv[i] = br
        out = mid[i] + norm_ref[7:8, :] * br

        @pl.when(enc)
        def _():
            dlat[0, i] = (out * seen_c[i, :BL]).astype(BF16)
            e_hop(i).start()

        outb[0, i] = (out * cov_c[i, :BL]).astype(BF16).reshape(2, SL, D)

    def own_up(i):
        h2_core(i).wait_recv()
        up(i, 0, wown.at[1], mlp_ref)

    def other_up(i):
        up(i, 1, wy.at[1], mlp_y)

    def own_back(i):
        @pl.when(reg)
        def _():
            dy[i] = jnp.concatenate([pgr[0, i], pgr[1, i]], axis=0).astype(F32) * cov_c[i, :BL]

        @pl.when(enc)
        def _():
            d_hop(i).wait_recv()
            dy[i] = dlat[1, i].astype(F32) * seen_c[i, :BL]

        dbl[0, i] = (norm_ref[7:8, :] * dy[i]).astype(BF16)
        dbl_core(i).start()

    def d_hop(i):
        return far(dlat.at[0, i], dlat.at[1, i], "dlat", to_s, i)

    def dbl_core(i):
        return far(dbl.at[0, i], dbl.at[1, i], "dbl", to_c, i)

    for j in range(MOST):
        forward_w(1, j, (reg,))
    forward_w(2, 0, (reg,))

    for i in range(I):
        arrive(i)
        if i > 0:
            middle(i - 1)
        if i == 2:
            own_w[0].wait()
            own_up(0)
        if i == 0:
            forward_w(1, 0, (enc,))
        attend(i)
        if i == 0:
            for j in range(1, MOST):
                forward_w(1, j, (enc,))
            forward_w(2, 1, (reg,))
        if i == 1:
            forward_w(2, 0, (enc,))
            forward_w(2, 2, (reg,))
    forward_w(2, 1, (enc,))
    forward_w(2, 2, (enc,))
    for i in range(1, I - 1):
        own_up(i)
    middle(I - 1)
    finish_w(1)
    for i in range(I - 1):
        other_up(i)
    own_up(I - 1)
    other_up(I - 1)
    own_w[1].wait()
    for i in range(I):
        own_down(i)
    finish_w(2)
    for i in range(I):
        down(i)
        if i > 0:
            finish(i - 1)
    own_pg.wait()

    @pl.when(reg)
    def _():
        c_pg.wait_recv()
        for i in range(I):
            own_back(i)

    finish(I - 1)
    w_o = both_rows(3 * PC, PC)

    def deliver(which, number, ref):
        return (
            here(outb.at[which, :, 0], ref.at[y], number),
            far(outb.at[which, :, 1], ref.at[y], number, to_y),
        )

    for copy in deliver(0, "res", res_ref):
        copy.start()

    nacc[...] = jnp.zeros_like(nacc)
    small_in[...] = jnp.zeros_like(small_in)

    def add_norm(row, value):
        nacc[row:row + 1, :] += value

    @pl.when(enc)
    def _():
        for i in range(I):
            own_back(i)

    def branch_sums(i, carry):
        grad = dy[i]
        add_norm(7, column_sum(grad * brv[i]))
        add_norm(6, column_sum(norm_ref[7:8, :] * grad))
        return carry

    for i in range(I):
        dbl_core(i).wait_recv()

    N = z.parts
    PM = z.per_mat

    def part(k):
        return pl.ds(pl.multiple_of(k * GC, GC), GC)

    def y_part(k):
        at = part(k)
        return far(g.at[1, at], yr.at[at], "gy", to_y, k)

    def to_middle(k):
        at = part(k)

        @pl.when(is_mid)
        def _():
            far(g.at[0, at], zb.at[at], "ga", to_m, k, receive="gb").start()

        @pl.when(not_mid)
        def _():
            far(g.at[0, at], za.at[at], "ga", to_m, k).start()

    def from_away(k):
        at = part(k)
        return far(g.at[0, at], za.at[at], "ga", to_w, k)

    def total(k):
        at = part(k)
        return far(zb.at[at], zb.at[at], "gb", to_w, k)

    def stage0(k):
        at = part(k)
        y_part(k).wait_recv()
        g[0, at, :] = (g[0, at, :].astype(F32) + yr[at, :].astype(F32)).astype(BF16)

        @pl.when(is_end)
        def _():
            to_middle(k)

    def stage1(k):
        at = part(k)

        @pl.when(not_end)
        def _():
            from_away(k).wait_recv()
            g[0, at, :] = (g[0, at, :].astype(F32) + za[at, :].astype(F32)).astype(BF16)
            to_middle(k)

    def each_out(k, do):
        for m, ref in enumerate((gd_ref, gu_ref, ga_ref)):
            @pl.when(jnp.logical_and(k >= m * PM, k < (m + 1) * PM))
            def _():
                do(here(zb.at[part(k)], ref.at[part(k - m * PM)], ("g0", "g1", "g2")[m]))

    def stage2(k):
        at = part(k)
        total(k).wait_recv()

        @pl.when(is_mid)
        def _():
            zb[at, :] = (g[0, at, :].astype(F32) + zb[at, :].astype(F32)).astype(BF16)

        @pl.when(not_end)
        def _():
            total(k).start()

        each_out(k, lambda copy: copy.start())

    AWAY_LAG = 2
    MID_LAG = 4
    LAG = 8

    def small_middle(start):
        @pl.when(is_mid)
        def _():
            copy = far(sml.at[1], sml.at[4], "sa", to_m, receive="sb")
            copy.start() if start else copy.wait_send()

        @pl.when(not_mid)
        def _():
            copy = far(sml.at[1], sml.at[3], "sa", to_m)
            copy.start() if start else copy.wait_send()

    c_sy = far(small_in, sml.at[0], "sy", to_y)
    c_sc = far(sml.at[1], sml.at[2], "sc", to_c)
    s_total = far(sml.at[4], sml.at[4], "sb", to_w)

    def small0():
        c_sy.wait_recv()
        sml[1, 0:8, :] = small_in[0:8, :] + sml[0, 0:8, :]
        sml[1, 8:9, :] = small_in[8:9, :] + sml[0, 9:10, :]
        sml[1, 9:10, :] = jnp.zeros((1, D), F32)
        sml[1, 10:12, :] = small_in[10:12, :]
        sml[1, 12:14, :] = sml[0, 10:12, :]
        sml[1, 14:16, :] = jnp.zeros((2, D), F32)
        c_sc.start()

    def small1():
        c_sc.wait()
        sml[1, 0:8, :] = sml[1, 0:8, :] + sml[2, 0:8, :]

        @pl.when(is_end)
        def _():
            small_middle(True)

    def small2():
        @pl.when(not_end)
        def _():
            far(sml.at[1], sml.at[3], "sa", to_w).wait_recv()
            sml[1] = sml[1] + sml[3]
            small_middle(True)

    def small3():
        s_total.wait_recv()

        @pl.when(is_mid)
        def _():
            sml[4] = sml[1] + sml[4]

        @pl.when(not_end)
        def _():
            s_total.start()

        small_ref[...] = sml[4]

    def step(k, carry=0):
        @pl.when(k < N)
        def _():
            stage0(k)

        @pl.when(jnp.logical_and(k >= AWAY_LAG, k < N + AWAY_LAG))
        def _():
            stage1(k - AWAY_LAG)

        @pl.when(jnp.logical_and(is_mid, jnp.logical_and(k >= MID_LAG, k < N + MID_LAG)))
        def _():
            stage2(k - MID_LAG)

        @pl.when(jnp.logical_and(not_mid, jnp.logical_and(k >= LAG, k < N + LAG)))
        def _():
            stage2(k - LAG)

        pl.when(k == N - 6)(small0)
        pl.when(k == N - 5)(small1)
        pl.when(k == N - 4)(small2)
        pl.when(jnp.logical_and(is_mid, k == N - 2))(small3)
        pl.when(jnp.logical_and(not_mid, k == N))(small3)
        return carry

    done_steps = [0]

    def pump(many, index=0, times=1):
        first = done_steps[0] + index * many
        done_steps[0] += many * times

        @pl.when(enc)
        def _():
            lax.fori_loop(first, first + many, step, 0)

    first_down, first_up, first_attn = 0, PM, 2 * PM
    PT = TW // GC

    def outer_rows(left, right, w, first):
        def one(n, carry):
            at = pl.ds(pl.multiple_of(n * TW, TW), TW)
            to = pl.ds(pl.multiple_of(first * GC + n * TW, TW), TW)
            g[w, to, :] = tn(left(at), right()).astype(BF16)
            if w == 1:
                for k in range(PT):
                    y_part(first + n * PT + k).start()
            return carry

        lax.fori_loop(0, NT, one, 0, unroll=True)

    def wide(ref, w):
        return lambda at: ref[w, :, :, at].reshape(2 * R, at.size)

    def h2_cols(at):
        return jnp.concatenate(
            [h2[0, :, :, at].reshape(R, at.size), h2[1, :, :, at].reshape(R, at.size)], axis=0
        )

    def down_outer(w):
        outer_rows(wide(act, w), lambda: dbl[...].reshape(2 * R, D), w, first_down)

    def up_outer(w):
        outer_rows(h2_cols, lambda: gp[w].reshape(2 * R, D), w, first_up)

    @pl.when(enc)
    def _():
        down_outer(1)
        down_outer(0)

    def down_back(half, w, w_ref):
        rows = flat(dbl, half)

        def one(n, carry):
            at = pl.ds(pl.multiple_of(n * TW, TW), TW)
            du = nt(rows, w_ref[at, :]) * gp[w, half, :, at].astype(F32)
            small_in[8 + w:9 + w, at] += column_sum(du)
            gp[w, half, :, at] = du.astype(BF16)
            return carry

        lax.fori_loop(0, NT, one, 0, unroll=True)

    down_back(1, 1, wy.at[2])
    pump(1)
    down_back(1, 0, wown.at[2])
    pump(1)

    def up_back(half):
        return nt(gp[0, half], wown[1]) + nt(gp[1, half], wy[1])

    gone(snd.at[0], "attn", to_c)
    snd[0] = up_back(1).astype(BF16).reshape(I, BL, D)
    c_dh2 = far(snd.at[0], rcv.at[2], "dh2", to_c)
    c_dh2.start()
    lax.fori_loop(0, I, branch_sums, 0)
    pump(1)
    down_back(0, 1, wy.at[2])
    pump(1)
    down_back(0, 0, wown.at[2])

    @pl.when(enc)
    def _():
        up_outer(1)

    pump(1)

    @pl.when(enc)
    def _():
        up_outer(0)

    pump(1)
    back0 = up_back(0).reshape(I, BL, D)
    c_dh2.wait_recv()

    def dal_core(i):
        return far(dal.at[0, i], dal.at[1, i], "dal", to_c, i)

    for i in range(I):
        grad = back0[i] + rcv[2, i].astype(F32)
        hat, inverse = normal(mid[i])
        add_norm(4, column_sum(grad * hat))
        add_norm(5, column_sum(grad))
        d_mid = dy[i] + normal_back(hat, inverse, grad * norm_ref[4:5, :])
        dy[i] = d_mid
        add_norm(3, column_sum(d_mid * att[i]))
        d_att = norm_ref[3:4, :] * d_mid
        add_norm(2, column_sum(d_att))
        dal[0, i] = d_att.astype(BF16)
        dal_core(i).start()
    pump(1)

    def all_rows(ref):
        return ref[...].reshape(2 * R, ref.shape[-1])

    base = first_attn * GC

    def store_rows(value, first):
        g[0, base + first:base + first + PC, :] = value[:PC].astype(BF16)
        g[1, base + first:base + first + PC, :] = value[PC:].astype(BF16)

    def attend_back(i, between):
        dal_core(i).wait_recv()
        dol[:, i] = nt(dal[:, i].reshape(KEYS, D), w_o).astype(BF16).reshape(2, BL, PW)
        for pr in range(z.heads // 2):
            qp, kp, vp, gpair = image(q, i, pr), image(kk, i, pr), image(vv, i, pr), image(dol, i, pr)
            at = slice(pr * 2 * HD, (pr + 1) * 2 * HD)
            k_cols = jnp.transpose(kp)
            dqs, dks, dvs = [], [], []
            for sub in range(2):
                probs = jnp.transpose(p[i, 2 * pr + sub])
                wide_probs = probs.astype(F32)
                d_probs = nt(vp, jnp.where(lanes[sub], gpair, zero16))
                dvs.append(nn(probs, gpair))
                inner = jnp.sum(d_probs * wide_probs, axis=0, keepdims=True)
                ds = (wide_probs * (d_probs - inner)).astype(BF16)
                dqs.append(nn(k_cols, ds))
                dks.append(nn(ds, qp))
            d_q = jnp.transpose(jnp.concatenate([dqs[0][:HD], dqs[1][HD:]], axis=0)) * 0.125
            d_k = jnp.where(lanes[0], dks[0], dks[1])
            d_v = jnp.where(lanes[0], dvs[0], dvs[1])
            small_in[10:11, at] += column_sum(d_q)
            small_in[11:12, at] += column_sum(d_v)
            put(dq, i, pr, d_q.astype(BF16))
            put(dk, i, pr, d_k.astype(BF16))
            put(dv, i, pr, d_v.astype(BF16))
            if pr == 1:
                between()

    def dn_core(i):
        return far(snd.at[1, i], rcv.at[3, i], "dn", to_c, i)

    def input_back(i):
        grad = nn(dq[:, i].reshape(KEYS, PW), both_rows(0, PC))
        grad += nn(dk[:, i].reshape(KEYS, PW), both_rows(PC, PC))
        grad += nn(dv[:, i].reshape(KEYS, PW), both_rows(2 * PC, PC))
        snd[1, i] = grad[BL:].astype(BF16)
        dn_core(i).start()
        back1[i] = grad[:BL]

    def leave(i):
        dn_core(i).wait_recv()
        grad = back1[i] + rcv[3, i].astype(F32)
        extra = jnp.logical_and(seen_c[i, :BL] > 0.5, reg)

        @pl.when(reg)
        def _():
            other = jnp.where(extra, grad, 0.0)
            hat, inverse = normal(e_own[i].astype(F32))
            dlat[0, i] = normal_back(hat, inverse, other * g0).astype(BF16)
            d_hop(i).start()
            add_norm(0, column_sum(other * hat))
            add_norm(1, column_sum(other))

        own = jnp.where(extra, 0.0, grad)
        hat, inverse = normal(lay(xall[0, i]).astype(F32))
        add_norm(0, column_sum(own * hat))
        add_norm(1, column_sum(own))
        d_x = dy[i] + normal_back(hat, inverse, own * g0)
        outb[1, i] = d_x.astype(BF16).reshape(2, SL, D)

    back1 = brv
    gone(snd.at[1], "br", to_c)
    for i in range(I):
        attend_back(i, functools.partial(leave, i - 1) if i > 0 else lambda: None)
        pump(1)
        input_back(i)
        pump(1)
    leave(I - 1)
    pump(1)

    @pl.when(reg)
    def _():
        down_outer(1)
        down_outer(0)
        up_outer(1)
        up_outer(0)

    store_rows(tn(all_rows(dq), all_rows(h)), 0)
    pump(1)
    store_rows(tn(all_rows(dk), all_rows(kv)), PC)
    pump(1)
    store_rows(tn(all_rows(dv), all_rows(kv)), 2 * PC)
    pump(1)
    store_rows(tn(all_rows(o), all_rows(dal)), 3 * PC)
    small_in[0:8, :] = nacc[...]
    c_sy.start()
    for k in range(first_attn, z.parts):
        y_part(k).start()
    for copy in deliver(1, "gin", gin_ref):
        copy.start()

    lax.fori_loop(jnp.where(enc, done_steps[0], 0), N + LAG, step, 0)

    small_middle(False)
    gone(g.at[1], "gy", to_y)
    gone(g.at[0], "ga", to_m)

    @pl.when(not_end)
    def _():
        s_total.wait_send()
        gone(zb, "gb", to_w)

    c_sy.wait_send()
    for m, ref in enumerate((gd_ref, gu_ref, ga_ref)):
        here(zb.at[0:D], ref, ("g0", "g1", "g2")[m]).wait()
    for which, number, ref in ((0, "res", res_ref), (1, "gin", gin_ref)):
        for copy in deliver(which, number, ref):
            copy.wait()
    for copy in (c_x, c_b0, c_b1, c_xc0, c_xc1, c_dh2):
        copy.wait_send()
    gone(h2.at[0], "h2", to_c)
    gone(dbl.at[0], "dbl", to_c)
    gone(dal.at[0], "dal", to_c)
    gone(snd.at[1], "dn", to_c)

    @pl.when(enc)
    def _():
        if around:
            gone(g.at[0, 0:len(around) * CH], "d1", to_s)
        gone(e_own, "e", to_s)

    @pl.when(reg)
    def _():
        c_pg.wait_send()
        gone(e_own, "ec", to_c)
        gone(dlat.at[0], "dlat", to_s)

    for s, flag in enumerate((enc, reg)):
        @pl.when(flag)
        def _():
            gone(g.at[0, 0:sum(len(js) for js in straight[s]) * CH], "wy", to_y)
            gone(g.at[0, 0:sum(HELP[s]) * CH], "wz", pair_z)


def fused(z, x, pg, wqkv, wout, wu, wd, lengths, mask, qv, mlp, norms):
    *places, arrivals, departures, copies = plan(z)
    I, R, D, BL, SL = z.images, z.rows, z.width, z.block, z.slots
    PC, PW = z.piece, z.pair
    KEYS = 2 * BL
    vm = pl.BlockSpec(memory_space=pltpu.VMEM)
    sm = pl.BlockSpec(memory_space=pltpu.SMEM)
    hbm = pl.BlockSpec(memory_space=pl.ANY)

    def b16(*shape):
        return pltpu.VMEM(shape, BF16)

    def f32(*shape):
        return pltpu.VMEM(shape, F32)

    scratch = [
        b16(3, D, D), b16(3, D, D),
        b16(2, I, 2, SL, D),
        b16(2, I, SL, D),
        f32(2, PC), f32(1, D),
        f32(I, KEYS, 1), f32(I, KEYS, 1), f32(I, KEYS, 1), f32(I, 1, KEYS),
        b16(I, BL, D), b16(I, BL, D),
        b16(2, I, BL, D), b16(2, I, BL, D),
        b16(2, I, BL, PW), b16(2, I, BL, PW), b16(2, I, BL, PW), b16(2, I, BL, PW),
        b16(I, z.heads, KEYS, KEYS),
        f32(I, BL, D), f32(I, BL, D),
        b16(2, I, BL, D),
        b16(2, 2, R, D), b16(2, 2, R, D),
        f32(I, BL, D), f32(I, BL, D),
        b16(2, I, BL, D), b16(4, I, BL, D),
        b16(2, I, BL, D), b16(2, I, BL, D),
        b16(2, I, BL, PW), b16(2, I, BL, PW), b16(2, I, BL, PW), b16(2, I, BL, PW),
        b16(2, 3 * D, D),
        b16(3 * D, D), b16(3 * D, D), b16(3 * D, D),
        b16(2, I, BL, D),
        b16(2, I, 2, SL, D),
        f32(8, D), f32(5, 16, D), f32(16, D),
        pltpu.SemaphoreType.DMA((departures,)),
        pltpu.SemaphoreType.DMA((arrivals,)),
        pltpu.SemaphoreType.DMA((copies,)),
    ]
    weight = jax.ShapeDtypeStruct((D, D), BF16)
    rows = jax.ShapeDtypeStruct((2, I, SL, D), BF16)
    return pl.pallas_call(
        functools.partial(body, z, places),
        out_shape=(rows, rows, weight, weight, weight, jax.ShapeDtypeStruct((16, D), F32)),
        in_specs=[hbm] * 6 + [sm] + [vm] * 4,
        out_specs=(hbm, hbm, hbm, hbm, hbm, vm),
        scratch_shapes=scratch,
        compiler_params=pltpu.CompilerParams(
            collective_id=0, has_side_effects=True, vmem_limit_bytes=121 * 2**19
        ),
    )(x, pg, wqkv, wout, wu, wd, lengths, mask, qv, mlp, norms)


def widen(
    piece, n_qkv,
    res, gin, gd, gu, ga, small,
    o_res, o_gin, o_down, o_up, o_qkv, o_out, o_qv, o_mlp, o_norms,
):
    n = pl.program_id(0)
    o_res[...] = res[...]
    o_gin[...] = gin[...].astype(F32)
    o_down[...] = gd[...].astype(F32)
    o_up[...] = gu[...].astype(F32)

    @pl.when(n < n_qkv)
    def _():
        o_qkv[...] = ga[...].astype(F32)

    @pl.when(n >= n_qkv)
    def _():
        o_out[...] = ga[...].astype(F32)

    @pl.when(n == 0)
    def _():
        o_qv[...] = small[10:12, :piece] + small[12:14, piece:2 * piece]
        o_mlp[...] = small[8:9, :]
        o_norms[...] = small[0:8, :]


def outputs(z, res, gin, gd, gu, ga, small):
    D, PC = z.width, z.piece
    tile = 192
    steps = D // tile
    n_qkv = 3 * PC // tile
    token_rows = 2 * z.images * z.slots
    token_tile = token_rows // steps
    tokens = pl.BlockSpec((token_tile, D), lambda n: (n, 0))
    rows = pl.BlockSpec((tile, D), lambda n: (n, 0))
    once = lambda *shape: pl.BlockSpec(shape, lambda n: (0, 0))
    first = pl.BlockSpec((tile, D), lambda n: (jnp.minimum(n, n_qkv - 1), 0))
    last = pl.BlockSpec((tile, D), lambda n: (jnp.maximum(n - n_qkv, 0), 0))
    shape = jax.ShapeDtypeStruct
    return pl.pallas_call(
        functools.partial(widen, PC, n_qkv),
        grid=(steps,),
        out_shape=(
            shape((token_rows, D), BF16), shape((token_rows, D), F32), shape((D, D), F32), shape((D, D), F32),
            shape((3 * PC, D), F32), shape((PC, D), F32), shape((2, PC), F32), shape((1, D), F32), shape((8, D), F32),
        ),
        in_specs=[tokens, tokens, rows, rows, rows, once(16, D)],
        out_specs=(tokens, tokens, rows, rows, first, last, once(2, PC), once(1, D), once(8, D)),
    )(res.reshape(token_rows, D), gin.reshape(token_rows, D), gd, gu, ga, small)


def local(
    n_dp,
    block_in, lengths, patch_mask, pred_grad, w_qkv, w_out, w_up, w_down, qv_bias, mlp_bias, norms
):
    images, slots, width = block_in.shape[1:]
    piece = w_qkv.shape[3]
    z = Sizes(n_dp, images // 2, slots, width, piece)

    x = block_in.reshape(2, z.images, slots, width)
    pg = pred_grad.reshape(2, z.images, slots, width)
    wqkv = jnp.swapaxes(w_qkv[0], 1, 2).reshape(3 * piece, width)
    summed = fused(
        z, x, pg, wqkv, w_out[0], w_up[0], w_down[0], lengths, patch_mask, qv_bias[0], mlp_bias, norms[0]
    )
    res, gin, g_down, g_up, g_qkv, g_out, g_qv, g_mlp, g_norms = outputs(z, *summed)
    return (
        res.reshape(1, images, slots, width),
        gin.reshape(1, images, slots, width),
        jnp.swapaxes(g_qkv.reshape(3, piece, width), 1, 2)[None],
        g_out[None],
        g_up[None],
        g_down[None],
        g_qv[None],
        g_mlp,
        g_norms[None],
    )


def solution(mesh):
    return jax.shard_map(
        functools.partial(local, mesh.shape["dp"]),
        mesh=mesh,
        in_specs=(
            P("section", "dp", "tensor", None),
            P("dp"),
            P("dp", None),
            P("dp", "tensor", None),
            P("section", None, None, "tensor"),
            P("section", "tensor", None),
            P("section", None, "tensor"),
            P("section", "tensor", None),
            P("section", None, "tensor"),
            P("section", "tensor"),
            P("section", None, None),
        ),
        out_specs=(
            P("section", "dp", "tensor", None),
            P("section", "dp", "tensor", None),
            P("section", None, None, "tensor"),
            P("section", "tensor", None),
            P("section", None, "tensor"),
            P("section", "tensor", None),
            P("section", None, "tensor"),
            P("section", "tensor"),
            P("section", None, None),
        ),
        check_vma=False,
    )
```

```python
import functools

import jax
import jax.numpy as jnp
from jax import lax
from jax.experimental import pallas as pl
from jax.experimental.pallas import tpu as pltpu
from jax.sharding import PartitionSpec as P

HD = 64
CH = 128
GC = 64
AROUND = (1, 1, 1)
HELP_E = (3, 2, 2)
EPS = 1e-06
MASKED = -1000000000.0
F32 = jnp.float32
BF16 = jnp.bfloat16


class Places:
    def __init__(self):
        self.count = 0

    def take(self, many=1):
        first = self.count
        self.count += many
        return first


def nn(a, b):
    return lax.dot_general(a, b, (((1,), (0,)), ((), ())), preferred_element_type=F32)


def nt(a, b):
    return lax.dot_general(a, b, (((1,), (1,)), ((), ())), preferred_element_type=F32)


def tn(a, b):
    return lax.dot_general(a, b, (((0,), (0,)), ((), ())), preferred_element_type=F32)


def normal(u):
    mean = jnp.mean(u, axis=-1, keepdims=True)
    centred = u - mean
    spread = jnp.mean(centred * centred, axis=-1, keepdims=True)
    inverse = lax.rsqrt(spread + EPS)
    return centred * inverse, inverse


def normal_back(hat, inverse, grad):
    first = jnp.mean(grad, axis=-1, keepdims=True)
    second = jnp.mean(grad * hat, axis=-1, keepdims=True)
    return inverse * (grad - first - hat * second)


def column_sum(u):
    return jnp.sum(u, axis=0, keepdims=True)


class Sizes:
    def __init__(self, n_dp, images, slots, width, piece):
        self.n_dp = n_dp
        self.images = images
        self.slots = slots
        self.width = width
        self.piece = piece
        self.block = 2 * slots
        self.rows = images * self.block
        self.pair = 2 * piece
        self.heads = self.pair // HD
        self.around = sum(AROUND)
        self.per_mat = width // GC
        self.parts = 3 * self.per_mat


def plan(z):
    p, d, n = Places(), Places(), Places()
    pieces = z.width // CH
    recv = dict(
        x=p.take(), bias=p.take(2), xc0=p.take(), xc1=p.take(), pg=p.take(),
        wy=p.take(3 * pieces), wz=p.take(3 * pieces // 2),
        d1=p.take(z.around), d2=p.take(z.around),
        e=p.take(z.images), ec=p.take(z.images),
        attn=p.take(z.images), h2=p.take(z.images), br=p.take(z.images), dbl=p.take(z.images),
        dh2=p.take(), dal=p.take(z.images), dn=p.take(z.images),
        dlat=p.take(z.images), res=p.take(), gin=p.take(),
        gy=p.take(z.parts), ga=p.take(z.parts), gb=p.take(z.parts),
        sy=p.take(), sc=p.take(), sa=p.take(), sb=p.take(),
    )
    together = ("wy", "wz", "d1", "gy", "ga", "gb", "attn", "h2", "br", "dbl", "e", "ec", "dlat", "dn", "dal")
    many = dict(bias=2, d2=z.around)
    send = {name: d.take(many.get(name, 1)) for name in recv}
    send["d3"] = d.take(z.around)
    local = {name: n.take() for name in ("mask", "qv", "mlp", "norm", "w0", "wo", "w1", "w2", "x", "pg", "res", "gin", "g0", "g1", "g2")}
    return recv, send, frozenset(together), local, p.count, d.count, n.count


def body(
    z, places,
    x_ref, pg_ref, wqkv_ref, wout_ref, wu_ref, wd_ref, len_ref, mask_in, qv_in, mlp_in, norm_in,
    res_ref, gin_ref, gd_ref, gu_ref, ga_ref, small_ref,
    mask_ref, qv_ref, mlp_ref, norm_ref, wown, wy, xall, pgr, qv_y, mlp_y, code_c, seen_c, cov_c, key_r,
    e_own, e_oth, h, kv, q, kk, vv, o, p, att, mid, h2, act, gp, brv, dy,
    snd, rcv, dbl, dal, dol, dq, dk, dv, g, yr, za, zb, dlat, outb, nacc, sml, small_in,
    ss, rs, ls,
):
    S, SEND, TOGETHER, LOCAL = places
    sec = lax.axis_index("section")
    dp = lax.axis_index("dp")
    t = lax.axis_index("tensor")
    y = t // 2
    c = t % 2
    to_y = {"tensor": 2 * (1 - y) + c}
    to_c = {"tensor": 2 * y + 1 - c}
    to_s = {"section": 1 - sec}
    parity = dp % 2
    pair_z = {"dp": dp + 1 - 2 * parity}
    top = dp // (z.n_dp // 2)
    to_m = {"dp": dp + 1 - 2 * top}
    to_w = {"dp": dp - 1 + 2 * top}
    is_end = jnp.logical_or(dp == 0, dp == z.n_dp - 1)
    not_end = jnp.logical_not(is_end)
    is_mid = jnp.logical_or(dp == z.n_dp // 2 - 1, dp == z.n_dp // 2)
    not_mid = jnp.logical_not(is_mid)
    enc = sec == 0
    reg = sec == 1

    I, R, D, BL, SL = z.images, z.rows, z.width, z.block, z.slots
    PC, PW = z.piece, z.pair
    KEYS = 2 * BL
    WP = D // CH
    HELP = (HELP_E, (WP // 2,) * 3)
    MOST = WP // 2

    def far(src, dst, name, to, index=0, receive=None, send=None):
        leave = SEND[send or name] + (0 if name in TOGETHER else index)
        return pltpu.make_async_remote_copy(
            src_ref=src, dst_ref=dst, send_sem=ss.at[leave], recv_sem=rs.at[S[receive or name] + index],
            device_id=to, device_id_type=pl.DeviceIdType.MESH,
        )

    def gone(ref, name, to):
        far(ref, ref, name, to).wait_send()

    def here(src, dst, name):
        return pltpu.make_async_copy(src, dst, ls.at[LOCAL[name]])

    w_refs = (wown.at[0], wu_ref, wd_ref)
    own_w = [here(w_refs[m], wown.at[m], ("w0", "w1", "w2")[m]) for m in (1, 2)]
    own_a = (here(wqkv_ref, wown.at[0, 0:3 * z.piece], "w0"), here(wout_ref, wown.at[0, 3 * z.piece:], "wo"))
    own_x = here(x_ref.at[y], xall.at[0, :, 0], "x")
    own_pg = here(pg_ref.at[y], pgr.at[0], "pg")
    own_small = (
        here(mask_in, mask_ref, "mask"), here(qv_in, qv_ref, "qv"),
        here(mlp_in, mlp_ref, "mlp"), here(norm_in, norm_ref, "norm"),
    )
    for copy in (own_x, *own_a, *own_small, *own_w):
        copy.start()
    own_pg.start()

    barrier = pltpu.get_barrier_semaphore()

    def greet(to):
        pl.semaphore_signal(barrier, inc=1, device_id=to, device_id_type=pl.DeviceIdType.MESH)

    greet(to_y)
    greet(to_c)
    greet(to_s)
    greet(to_m)

    @pl.when(not_end)
    def _():
        greet(to_w)
        pl.semaphore_wait(barrier, 5)

    @pl.when(is_end)
    def _():
        pl.semaphore_wait(barrier, 4)

    c_x = far(x_ref.at[1 - y], xall.at[0, :, 1], "x", to_y)
    c_b0 = far(qv_in, qv_y, "bias", to_y)
    c_b1 = far(mlp_in, mlp_y, "bias", to_y, 1)
    c_xc0 = far(x_ref.at[y], xall.at[1, :, 0], "xc0", to_c)
    c_xc1 = far(xall.at[0, :, 1], xall.at[1, :, 1], "xc1", to_c)
    c_pg = far(pg_ref.at[1 - y], pgr.at[1], "pg", to_y)

    def rows_of(j, side):
        return pl.ds(pl.multiple_of((j + side * (WP - 1 - 2 * j)) * CH, CH), CH)

    def w_y(m, j):
        at = rows_of(j, parity)
        return far(w_refs[m].at[at], wy.at[m, at], "wy", to_y, m * WP + j)

    def w_z(m, j, side=None):
        at = rows_of(j, parity if side is None else side)
        return far(wy.at[m, at], wy.at[m, at], "wz", pair_z, m * (WP // 2) + j)

    around = [(m, WP - HELP[0][m] - 1 - j) for m in range(3) for j in range(AROUND[m] - 1, -1, -1)]

    def d_slot(side, n):
        return g.at[side, pl.ds(n * CH, CH)]

    def d_out(n):
        m, j = around[n]
        return far(w_refs[m].at[rows_of(j, parity)], d_slot(0, n), "d1", to_s, n)

    def d_over(n):
        return far(d_slot(0, n), d_slot(1, n), "d2", to_y, n)

    def d_back(n):
        m, j = around[n]
        leave = SEND["d3"] + n
        return pltpu.make_async_remote_copy(
            src_ref=d_slot(1, n), dst_ref=wy.at[m, rows_of(j, parity)],
            send_sem=ss.at[leave], recv_sem=rs.at[S["wy"] + m * WP + j],
            device_id=to_s, device_id_type=pl.DeviceIdType.MESH,
        )

    straight = (
        [[j for j in range(WP - HELP[0][m]) if (m, j) not in around] for m in range(3)],
        [list(range(WP - HELP[1][m])) for m in range(3)],
    )

    def start_inputs():
        c_xc0.start()
        c_x.start()
        c_b0.start()
        c_b1.start()

    @pl.when(reg)
    def _():
        start_inputs()

    for copy in own_a:
        copy.wait()

    @pl.when(enc)
    def _():
        for n in range(len(around)):
            d_out(n).start()
        ahead = [(m, j) for m in range(3) for j in straight[0][m] if j < HELP[0][m]]
        behind = [(m, j) for m in range(3) for j in straight[0][m] if j >= HELP[0][m]]
        for m, j in ahead + behind:
            w_y(m, j).start()
            if (m, j) == (0, 1):
                start_inputs()

    @pl.when(reg)
    def _():
        for n in range(len(around) + 1):
            if n < len(around):
                d_out(n).wait_recv()
                d_over(n).start()
            if n > 0:
                d_over(n - 1).wait_recv()
                d_back(n - 1).start()
            if n == max(len(around) - 1, 0):
                for m in range(3):
                    for j in straight[1][m]:
                        w_y(m, j).start()
                c_pg.start()
        for n in range(len(around)):
            d_over(n).wait_send()
            d_back(n).wait_send()

    def forward_w(m, j, sections=(enc, reg)):
        for s, flag in enumerate((enc, reg)):
            if any(flag is one for one in sections) and j < HELP[s][m]:
                @pl.when(flag)
                def _():
                    w_y(m, j).wait_recv()
                    w_z(m, j).start()

    def finish_w(m):
        for s, flag in enumerate((enc, reg)):
            @pl.when(flag)
            def _():
                for j in range(HELP[s][m], WP - HELP[s][m]):
                    w_y(m, j).wait_recv()
                for j in range(HELP[s][m]):
                    w_z(m, j, 1 - parity).wait_recv()

    for copy in own_small:
        copy.wait()
    rank = lax.broadcasted_iota(jnp.int32, (KEYS, KEYS), 0)
    across = lax.broadcasted_iota(jnp.int32, (KEYS, KEYS), 1)
    group = rank // SL
    y_of = y + (group % 2) * (1 - 2 * y)
    c_of = c + (group // 2) * (1 - 2 * c)
    slot = (2 * y_of + c_of) * SL + rank % SL
    here_slot = slot == across
    diagonal = rank == across
    slot_col = slot[:, 0:1]
    for i in range(I):
        picked = jnp.where(here_slot, mask_ref[pl.ds(y * I + i, 1), :].astype(F32), 0.0)
        marked = jnp.sum(picked, axis=1, keepdims=True) > 0.5
        valid = slot_col < len_ref[y * I + i]
        seen = jnp.where(jnp.logical_and(valid, marked), 1.0, 0.0)
        code = jnp.where(enc, seen, jnp.zeros_like(seen))
        seen_c[i] = seen
        cov_c[i] = jnp.where(valid, 1.0, 0.0) - seen
        code_c[i] = code
        key = jnp.where(valid, code, 2.0)
        key_r[i] = jnp.sum(jnp.where(diagonal, key, 0.0), axis=0, keepdims=True)

    g0, b0 = norm_ref[0:1, :], norm_ref[1:2, :]

    def lay(block):
        return block.reshape(BL, D)

    forward_w(0, 0)
    forward_w(0, 1)
    own_x.wait()
    c_x.wait_recv()
    c_xc1.start()

    def norm_rows(half):
        def one(i, carry):
            hat, _ = normal(lay(xall[half, i]).astype(F32))
            value = (hat * g0 + b0).astype(BF16)
            h[half, i] = value
            kv[half, i] = value
            return carry

        lax.fori_loop(0, I, one, 0)

    norm_rows(0)
    c_xc0.wait_recv()
    c_xc1.wait_recv()
    norm_rows(1)
    for j in range(2, MOST):
        forward_w(0, j)
    c_b0.wait_recv()
    c_b1.wait_recv()
    finish_w(0)

    def both_rows(first, many):
        return jnp.concatenate([wown[0, first:first + many], wy[0, first:first + many]], axis=0)

    bq = jnp.concatenate([qv_ref[0:1, :], qv_y[0:1, :]], axis=1)
    bv = jnp.concatenate([qv_ref[1:2, :], qv_y[1:2, :]], axis=1)

    def flat(ref, half):
        return ref[half].reshape(R, ref.shape[-1])

    def e_hop(i):
        return far(dlat.at[0, i], e_own.at[i], "e", to_s, i)

    def e_core(i):
        return far(e_own.at[i], e_oth.at[i], "ec", to_c, i)

    for half in range(2):
        q[half] = ((nt(flat(h, half), both_rows(0, PC)) + bq).astype(BF16) * 0.125).reshape(I, BL, PW)

    lane = lax.broadcasted_iota(jnp.int32, (KEYS, 2 * HD), 1)
    lanes = (lane < HD, lane >= HD)
    zero16 = jnp.zeros((KEYS, 2 * HD), BF16)

    def image(ref, i, pr):
        at = slice(pr * 2 * HD, (pr + 1) * 2 * HD)
        return jnp.concatenate([ref[0, i, :, at], ref[1, i, :, at]], axis=0)

    def put(ref, i, pr, value):
        at = slice(pr * 2 * HD, (pr + 1) * 2 * HD)
        ref[0, i, :, at] = value[:BL]
        ref[1, i, :, at] = value[BL:]

    def latent_keys(half, ref, i):
        hat, _ = normal(ref[i].astype(F32))
        value = (hat * g0 + b0).astype(BF16)
        seen = seen_c[i, half * BL:(half + 1) * BL] > 0.5
        kv[half, i] = jnp.where(seen, value, h[half, i])

    def arrive(i):
        @pl.when(reg)
        def _():
            e_hop(i).wait_recv()
            e_core(i).start()
            latent_keys(0, e_own, i)

    def attend(i):
        @pl.when(reg)
        def _():
            e_core(i).wait_recv()
            latent_keys(1, e_oth, i)

        rows_k = kv[:, i].reshape(KEYS, D)
        kk[:, i] = nt(rows_k, both_rows(PC, PC)).astype(BF16).reshape(2, BL, PW)
        vv[:, i] = (nt(rows_k, both_rows(2 * PC, PC)) + bv).astype(BF16).reshape(2, BL, PW)
        shut = jnp.where(code_c[i] == key_r[i], 0.0, MASKED)
        for pr in range(z.heads // 2):
            qp, kp, vp = image(q, i, pr), image(kk, i, pr), image(vv, i, pr)
            outs = []
            for sub in range(2):
                scores = nt(jnp.where(lanes[sub], qp, zero16), kp) + shut
                top_value = jnp.max(scores, axis=-1, keepdims=True)
                e = jnp.exp(scores - top_value)
                probs = (e * (1.0 / jnp.sum(e, axis=-1, keepdims=True))).astype(BF16)
                p[i, 2 * pr + sub] = probs
                outs.append(nn(probs, vp))
            put(o, i, pr, jnp.where(lanes[0], outs[0], outs[1]).astype(BF16))
        attn = nn(o[:, i].reshape(KEYS, PW), both_rows(3 * PC, PC))
        snd[0, i] = attn[BL:].astype(BF16)
        exchange(0, "attn", i).start()
        att[i] = attn[:BL]

    def exchange(slot, name, i):
        return far(snd.at[slot % 2, i], rcv.at[slot, i], name, to_c, i)

    def h2_core(i):
        return far(h2.at[0, i], h2.at[1, i], "h2", to_c, i)

    def middle(i):
        exchange(0, "attn", i).wait_recv()
        attn = att[i] + rcv[0, i].astype(F32) + norm_ref[2:3, :]
        att[i] = attn
        value = lay(xall[0, i]).astype(F32) + norm_ref[3:4, :] * attn
        mid[i] = value
        hat, _ = normal(value)
        h2[0, i] = (hat * norm_ref[4:5, :] + norm_ref[5:6, :]).astype(BF16)
        h2_core(i).start()

    TW = 256
    NT = D // TW

    def rows_at(i):
        return pl.ds(i * BL, BL)

    def up(i, w, w_ref, b_row):
        rows2 = h2[:, i].reshape(KEYS, D)

        def one(n, carry):
            at = pl.ds(pl.multiple_of(n * TW, TW), TW)
            u = nn(rows2, w_ref[:, at]) + b_row[:, at]
            cdf = 0.5 + 0.5 * lax.erf(u * 0.7071067811865476)
            act[w, :, rows_at(i), at] = (u * cdf).astype(BF16).reshape(2, BL, TW)
            slope = cdf + u * (0.3989422804014327 * jnp.exp(-0.5 * u * u))
            gp[w, :, rows_at(i), at] = slope.astype(BF16).reshape(2, BL, TW)
            return carry

        lax.fori_loop(0, NT, one, 0, unroll=True)

    def own_down(i):
        br = nn(act[0, :, rows_at(i)].reshape(KEYS, D), wown[2])
        brv[i] = br[:BL]
        dy[i] = br[BL:]

    def down(i):
        br = nn(act[1, :, rows_at(i)].reshape(KEYS, D), wy[2])
        snd[1, i] = (dy[i] + br[BL:]).astype(BF16)
        exchange(1, "br", i).start()
        brv[i] = brv[i] + br[:BL]

    def finish(i):
        exchange(1, "br", i).wait_recv()
        br = brv[i] + rcv[1, i].astype(F32) + norm_ref[6:7, :]
        brv[i] = br
        out = mid[i] + norm_ref[7:8, :] * br

        @pl.when(enc)
        def _():
            dlat[0, i] = (out * seen_c[i, :BL]).astype(BF16)
            e_hop(i).start()

        outb[0, i] = (out * cov_c[i, :BL]).astype(BF16).reshape(2, SL, D)

    def own_up(i):
        h2_core(i).wait_recv()
        up(i, 0, wown.at[1], mlp_ref)

    def other_up(i):
        up(i, 1, wy.at[1], mlp_y)

    def own_back(i):
        @pl.when(reg)
        def _():
            dy[i] = jnp.concatenate([pgr[0, i], pgr[1, i]], axis=0).astype(F32) * cov_c[i, :BL]

        @pl.when(enc)
        def _():
            d_hop(i).wait_recv()
            dy[i] = dlat[1, i].astype(F32) * seen_c[i, :BL]

        dbl[0, i] = (norm_ref[7:8, :] * dy[i]).astype(BF16)
        dbl_core(i).start()

    def d_hop(i):
        return far(dlat.at[0, i], dlat.at[1, i], "dlat", to_s, i)

    def dbl_core(i):
        return far(dbl.at[0, i], dbl.at[1, i], "dbl", to_c, i)

    for j in range(MOST):
        forward_w(1, j, (reg,))
    forward_w(2, 0, (reg,))

    for i in range(I):
        arrive(i)
        if i > 0:
            middle(i - 1)
        if i == 2:
            own_w[0].wait()
            own_up(0)
        if i == 0:
            forward_w(1, 0, (enc,))
        attend(i)
        if i == 0:
            for j in range(1, MOST):
                forward_w(1, j, (enc,))
            forward_w(2, 1, (reg,))
        if i == 1:
            forward_w(2, 0, (enc,))
            forward_w(2, 2, (reg,))
    forward_w(2, 1, (enc,))
    forward_w(2, 2, (enc,))
    for i in range(1, I - 1):
        own_up(i)
    middle(I - 1)
    finish_w(1)
    for i in range(I - 1):
        other_up(i)
    own_up(I - 1)
    other_up(I - 1)
    own_w[1].wait()
    for i in range(I):
        own_down(i)
    finish_w(2)
    for i in range(I):
        down(i)
        if i > 0:
            finish(i - 1)
    own_pg.wait()

    @pl.when(reg)
    def _():
        c_pg.wait_recv()
        for i in range(I):
            own_back(i)

    finish(I - 1)
    w_o = both_rows(3 * PC, PC)

    def deliver(which, number, ref):
        return (
            here(outb.at[which, :, 0], ref.at[y], number),
            far(outb.at[which, :, 1], ref.at[y], number, to_y),
        )

    for copy in deliver(0, "res", res_ref):
        copy.start()

    nacc[...] = jnp.zeros_like(nacc)
    small_in[...] = jnp.zeros_like(small_in)

    def add_norm(row, value):
        nacc[row:row + 1, :] += value

    @pl.when(enc)
    def _():
        for i in range(I):
            own_back(i)

    def branch_sums(i, carry):
        grad = dy[i]
        add_norm(7, column_sum(grad * brv[i]))
        add_norm(6, column_sum(norm_ref[7:8, :] * grad))
        return carry

    for i in range(I):
        dbl_core(i).wait_recv()

    N = z.parts
    PM = z.per_mat

    def part(k):
        return pl.ds(pl.multiple_of(k * GC, GC), GC)

    def y_part(k):
        at = part(k)
        return far(g.at[1, at], yr.at[at], "gy", to_y, k)

    def to_middle(k):
        at = part(k)

        @pl.when(is_mid)
        def _():
            far(g.at[0, at], zb.at[at], "ga", to_m, k, receive="gb").start()

        @pl.when(not_mid)
        def _():
            far(g.at[0, at], za.at[at], "ga", to_m, k).start()

    def from_away(k):
        at = part(k)
        return far(g.at[0, at], za.at[at], "ga", to_w, k)

    def total(k):
        at = part(k)
        return far(zb.at[at], zb.at[at], "gb", to_w, k)

    def stage0(k):
        at = part(k)
        y_part(k).wait_recv()
        g[0, at, :] = (g[0, at, :].astype(F32) + yr[at, :].astype(F32)).astype(BF16)

        @pl.when(is_end)
        def _():
            to_middle(k)

    def stage1(k):
        at = part(k)

        @pl.when(not_end)
        def _():
            from_away(k).wait_recv()
            g[0, at, :] = (g[0, at, :].astype(F32) + za[at, :].astype(F32)).astype(BF16)
            to_middle(k)

    def each_out(k, do):
        for m, ref in enumerate((gd_ref, gu_ref, ga_ref)):
            @pl.when(jnp.logical_and(k >= m * PM, k < (m + 1) * PM))
            def _():
                do(here(zb.at[part(k)], ref.at[part(k - m * PM)], ("g0", "g1", "g2")[m]))

    def stage2(k):
        at = part(k)
        total(k).wait_recv()

        @pl.when(is_mid)
        def _():
            zb[at, :] = (g[0, at, :].astype(F32) + zb[at, :].astype(F32)).astype(BF16)

        @pl.when(not_end)
        def _():
            total(k).start()

        each_out(k, lambda copy: copy.start())

    AWAY_LAG = 2
    MID_LAG = 4
    LAG = 8

    def small_middle(start):
        @pl.when(is_mid)
        def _():
            copy = far(sml.at[1], sml.at[4], "sa", to_m, receive="sb")
            copy.start() if start else copy.wait_send()

        @pl.when(not_mid)
        def _():
            copy = far(sml.at[1], sml.at[3], "sa", to_m)
            copy.start() if start else copy.wait_send()

    c_sy = far(small_in, sml.at[0], "sy", to_y)
    c_sc = far(sml.at[1], sml.at[2], "sc", to_c)
    s_total = far(sml.at[4], sml.at[4], "sb", to_w)

    def small0():
        c_sy.wait_recv()
        sml[1, 0:8, :] = small_in[0:8, :] + sml[0, 0:8, :]
        sml[1, 8:9, :] = small_in[8:9, :] + sml[0, 9:10, :]
        sml[1, 9:10, :] = jnp.zeros((1, D), F32)
        sml[1, 10:12, :] = small_in[10:12, :]
        sml[1, 12:14, :] = sml[0, 10:12, :]
        sml[1, 14:16, :] = jnp.zeros((2, D), F32)
        c_sc.start()

    def small1():
        c_sc.wait()
        sml[1, 0:8, :] = sml[1, 0:8, :] + sml[2, 0:8, :]

        @pl.when(is_end)
        def _():
            small_middle(True)

    def small2():
        @pl.when(not_end)
        def _():
            far(sml.at[1], sml.at[3], "sa", to_w).wait_recv()
            sml[1] = sml[1] + sml[3]
            small_middle(True)

    def small3():
        s_total.wait_recv()

        @pl.when(is_mid)
        def _():
            sml[4] = sml[1] + sml[4]

        @pl.when(not_end)
        def _():
            s_total.start()

        small_ref[...] = sml[4]

    def step(k, carry=0):
        @pl.when(k < N)
        def _():
            stage0(k)

        @pl.when(jnp.logical_and(k >= AWAY_LAG, k < N + AWAY_LAG))
        def _():
            stage1(k - AWAY_LAG)

        @pl.when(jnp.logical_and(is_mid, jnp.logical_and(k >= MID_LAG, k < N + MID_LAG)))
        def _():
            stage2(k - MID_LAG)

        @pl.when(jnp.logical_and(not_mid, jnp.logical_and(k >= LAG, k < N + LAG)))
        def _():
            stage2(k - LAG)

        pl.when(k == N - 6)(small0)
        pl.when(k == N - 5)(small1)
        pl.when(k == N - 4)(small2)
        pl.when(jnp.logical_and(is_mid, k == N - 2))(small3)
        pl.when(jnp.logical_and(not_mid, k == N))(small3)
        return carry

    done_steps = [0]

    def pump(many, index=0, times=1):
        first = done_steps[0] + index * many
        done_steps[0] += many * times

        @pl.when(enc)
        def _():
            lax.fori_loop(first, first + many, step, 0)

    first_down, first_up, first_attn = 0, PM, 2 * PM
    PT = TW // GC

    def outer_rows(left, right, w, first):
        def one(n, carry):
            at = pl.ds(pl.multiple_of(n * TW, TW), TW)
            to = pl.ds(pl.multiple_of(first * GC + n * TW, TW), TW)
            g[w, to, :] = tn(left(at), right()).astype(BF16)
            if w == 1:
                for k in range(PT):
                    y_part(first + n * PT + k).start()
            return carry

        lax.fori_loop(0, NT, one, 0, unroll=True)

    def wide(ref, w):
        return lambda at: ref[w, :, :, at].reshape(2 * R, at.size)

    def h2_cols(at):
        return jnp.concatenate(
            [h2[0, :, :, at].reshape(R, at.size), h2[1, :, :, at].reshape(R, at.size)], axis=0
        )

    def down_outer(w):
        outer_rows(wide(act, w), lambda: dbl[...].reshape(2 * R, D), w, first_down)

    def up_outer(w):
        outer_rows(h2_cols, lambda: gp[w].reshape(2 * R, D), w, first_up)

    @pl.when(enc)
    def _():
        down_outer(1)
        down_outer(0)

    def down_back(half, w, w_ref):
        rows = flat(dbl, half)

        def one(n, carry):
            at = pl.ds(pl.multiple_of(n * TW, TW), TW)
            du = nt(rows, w_ref[at, :]) * gp[w, half, :, at].astype(F32)
            small_in[8 + w:9 + w, at] += column_sum(du)
            gp[w, half, :, at] = du.astype(BF16)
            return carry

        lax.fori_loop(0, NT, one, 0, unroll=True)

    down_back(1, 1, wy.at[2])
    pump(1)
    down_back(1, 0, wown.at[2])
    pump(1)

    def up_back(half):
        return nt(gp[0, half], wown[1]) + nt(gp[1, half], wy[1])

    gone(snd.at[0], "attn", to_c)
    snd[0] = up_back(1).astype(BF16).reshape(I, BL, D)
    c_dh2 = far(snd.at[0], rcv.at[2], "dh2", to_c)
    c_dh2.start()
    lax.fori_loop(0, I, branch_sums, 0)
    pump(1)
    down_back(0, 1, wy.at[2])
    pump(1)
    down_back(0, 0, wown.at[2])

    @pl.when(enc)
    def _():
        up_outer(1)

    pump(1)

    @pl.when(enc)
    def _():
        up_outer(0)

    pump(1)
    back0 = up_back(0).reshape(I, BL, D)
    c_dh2.wait_recv()

    def dal_core(i):
        return far(dal.at[0, i], dal.at[1, i], "dal", to_c, i)

    for i in range(I):
        grad = back0[i] + rcv[2, i].astype(F32)
        hat, inverse = normal(mid[i])
        add_norm(4, column_sum(grad * hat))
        add_norm(5, column_sum(grad))
        d_mid = dy[i] + normal_back(hat, inverse, grad * norm_ref[4:5, :])
        dy[i] = d_mid
        add_norm(3, column_sum(d_mid * att[i]))
        d_att = norm_ref[3:4, :] * d_mid
        add_norm(2, column_sum(d_att))
        dal[0, i] = d_att.astype(BF16)
        dal_core(i).start()
    pump(1)

    def all_rows(ref):
        return ref[...].reshape(2 * R, ref.shape[-1])

    base = first_attn * GC

    def store_rows(value, first):
        g[0, base + first:base + first + PC, :] = value[:PC].astype(BF16)
        g[1, base + first:base + first + PC, :] = value[PC:].astype(BF16)

    def attend_back(i, between):
        dal_core(i).wait_recv()
        dol[:, i] = nt(dal[:, i].reshape(KEYS, D), w_o).astype(BF16).reshape(2, BL, PW)
        for pr in range(z.heads // 2):
            qp, kp, vp, gpair = image(q, i, pr), image(kk, i, pr), image(vv, i, pr), image(dol, i, pr)
            at = slice(pr * 2 * HD, (pr + 1) * 2 * HD)
            k_cols = jnp.transpose(kp)
            dqs, dks, dvs = [], [], []
            for sub in range(2):
                probs = jnp.transpose(p[i, 2 * pr + sub])
                wide_probs = probs.astype(F32)
                d_probs = nt(vp, jnp.where(lanes[sub], gpair, zero16))
                dvs.append(nn(probs, gpair))
                inner = jnp.sum(d_probs * wide_probs, axis=0, keepdims=True)
                ds = (wide_probs * (d_probs - inner)).astype(BF16)
                dqs.append(nn(k_cols, ds))
                dks.append(nn(ds, qp))
            d_q = jnp.transpose(jnp.concatenate([dqs[0][:HD], dqs[1][HD:]], axis=0)) * 0.125
            d_k = jnp.where(lanes[0], dks[0], dks[1])
            d_v = jnp.where(lanes[0], dvs[0], dvs[1])
            small_in[10:11, at] += column_sum(d_q)
            small_in[11:12, at] += column_sum(d_v)
            put(dq, i, pr, d_q.astype(BF16))
            put(dk, i, pr, d_k.astype(BF16))
            put(dv, i, pr, d_v.astype(BF16))
            if pr == 1:
                between()

    def dn_core(i):
        return far(snd.at[1, i], rcv.at[3, i], "dn", to_c, i)

    def input_back(i):
        grad = nn(dq[:, i].reshape(KEYS, PW), both_rows(0, PC))
        grad += nn(dk[:, i].reshape(KEYS, PW), both_rows(PC, PC))
        grad += nn(dv[:, i].reshape(KEYS, PW), both_rows(2 * PC, PC))
        snd[1, i] = grad[BL:].astype(BF16)
        dn_core(i).start()
        back1[i] = grad[:BL]

    def leave(i):
        dn_core(i).wait_recv()
        grad = back1[i] + rcv[3, i].astype(F32)
        extra = jnp.logical_and(seen_c[i, :BL] > 0.5, reg)

        @pl.when(reg)
        def _():
            other = jnp.where(extra, grad, 0.0)
            hat, inverse = normal(e_own[i].astype(F32))
            dlat[0, i] = normal_back(hat, inverse, other * g0).astype(BF16)
            d_hop(i).start()
            add_norm(0, column_sum(other * hat))
            add_norm(1, column_sum(other))

        own = jnp.where(extra, 0.0, grad)
        hat, inverse = normal(lay(xall[0, i]).astype(F32))
        add_norm(0, column_sum(own * hat))
        add_norm(1, column_sum(own))
        d_x = dy[i] + normal_back(hat, inverse, own * g0)
        outb[1, i] = d_x.astype(BF16).reshape(2, SL, D)

    back1 = brv
    gone(snd.at[1], "br", to_c)
    for i in range(I):
        attend_back(i, functools.partial(leave, i - 1) if i > 0 else lambda: None)
        pump(1)
        input_back(i)
        pump(1)
    leave(I - 1)
    pump(1)

    @pl.when(reg)
    def _():
        down_outer(1)
        down_outer(0)
        up_outer(1)
        up_outer(0)

    store_rows(tn(all_rows(dq), all_rows(h)), 0)
    pump(1)
    store_rows(tn(all_rows(dk), all_rows(kv)), PC)
    pump(1)
    store_rows(tn(all_rows(dv), all_rows(kv)), 2 * PC)
    pump(1)
    store_rows(tn(all_rows(o), all_rows(dal)), 3 * PC)
    small_in[0:8, :] = nacc[...]
    c_sy.start()
    for k in range(first_attn, z.parts):
        y_part(k).start()
    for copy in deliver(1, "gin", gin_ref):
        copy.start()

    lax.fori_loop(jnp.where(enc, done_steps[0], 0), N + LAG, step, 0)

    small_middle(False)
    gone(g.at[1], "gy", to_y)
    gone(g.at[0], "ga", to_m)

    @pl.when(not_end)
    def _():
        s_total.wait_send()
        gone(zb, "gb", to_w)

    c_sy.wait_send()
    for m, ref in enumerate((gd_ref, gu_ref, ga_ref)):
        here(zb.at[0:D], ref, ("g0", "g1", "g2")[m]).wait()
    for which, number, ref in ((0, "res", res_ref), (1, "gin", gin_ref)):
        for copy in deliver(which, number, ref):
            copy.wait()
    for copy in (c_x, c_b0, c_b1, c_xc0, c_xc1, c_dh2):
        copy.wait_send()
    gone(h2.at[0], "h2", to_c)
    gone(dbl.at[0], "dbl", to_c)
    gone(dal.at[0], "dal", to_c)
    gone(snd.at[1], "dn", to_c)

    @pl.when(enc)
    def _():
        if around:
            gone(g.at[0, 0:len(around) * CH], "d1", to_s)
        gone(e_own, "e", to_s)

    @pl.when(reg)
    def _():
        c_pg.wait_send()
        gone(e_own, "ec", to_c)
        gone(dlat.at[0], "dlat", to_s)

    for s, flag in enumerate((enc, reg)):
        @pl.when(flag)
        def _():
            gone(g.at[0, 0:sum(len(js) for js in straight[s]) * CH], "wy", to_y)
            gone(g.at[0, 0:sum(HELP[s]) * CH], "wz", pair_z)


def fused(z, x, pg, wqkv, wout, wu, wd, lengths, mask, qv, mlp, norms):
    *places, arrivals, departures, copies = plan(z)
    I, R, D, BL, SL = z.images, z.rows, z.width, z.block, z.slots
    PC, PW = z.piece, z.pair
    KEYS = 2 * BL
    vm = pl.BlockSpec(memory_space=pltpu.VMEM)
    sm = pl.BlockSpec(memory_space=pltpu.SMEM)
    hbm = pl.BlockSpec(memory_space=pl.ANY)

    def b16(*shape):
        return pltpu.VMEM(shape, BF16)

    def f32(*shape):
        return pltpu.VMEM(shape, F32)

    scratch = [
        pltpu.VMEM((2 * I, KEYS), jnp.int32), f32(2, PC), f32(1, D), f32(8, D),
        b16(3, D, D), b16(3, D, D),
        b16(2, I, 2, SL, D),
        b16(2, I, SL, D),
        f32(2, PC), f32(1, D),
        f32(I, KEYS, 1), f32(I, KEYS, 1), f32(I, KEYS, 1), f32(I, 1, KEYS),
        b16(I, BL, D), b16(I, BL, D),
        b16(2, I, BL, D), b16(2, I, BL, D),
        b16(2, I, BL, PW), b16(2, I, BL, PW), b16(2, I, BL, PW), b16(2, I, BL, PW),
        b16(I, z.heads, KEYS, KEYS),
        f32(I, BL, D), f32(I, BL, D),
        b16(2, I, BL, D),
        b16(2, 2, R, D), b16(2, 2, R, D),
        f32(I, BL, D), f32(I, BL, D),
        b16(2, I, BL, D), b16(4, I, BL, D),
        b16(2, I, BL, D), b16(2, I, BL, D),
        b16(2, I, BL, PW), b16(2, I, BL, PW), b16(2, I, BL, PW), b16(2, I, BL, PW),
        b16(2, 3 * D, D),
        b16(3 * D, D), b16(3 * D, D), b16(3 * D, D),
        b16(2, I, BL, D),
        b16(2, I, 2, SL, D),
        f32(8, D), f32(5, 16, D), f32(16, D),
        pltpu.SemaphoreType.DMA((departures,)),
        pltpu.SemaphoreType.DMA((arrivals,)),
        pltpu.SemaphoreType.DMA((copies,)),
    ]
    weight = jax.ShapeDtypeStruct((D, D), BF16)
    rows = jax.ShapeDtypeStruct((2, I, SL, D), BF16)
    return pl.pallas_call(
        functools.partial(body, z, places),
        out_shape=(rows, rows, weight, weight, weight, jax.ShapeDtypeStruct((16, D), F32)),
        in_specs=[hbm] * 6 + [sm] + [hbm] * 4,
        out_specs=(hbm, hbm, hbm, hbm, hbm, vm),
        scratch_shapes=scratch,
        compiler_params=pltpu.CompilerParams(
            collective_id=0, has_side_effects=True, vmem_limit_bytes=121 * 2**19
        ),
    )(x, pg, wqkv, wout, wu, wd, lengths, mask, qv, mlp, norms)


def widen(
    piece, n_qkv,
    res, gin, gd, gu, ga, small,
    o_res, o_gin, o_down, o_up, o_qkv, o_out, o_qv, o_mlp, o_norms,
):
    n = pl.program_id(0)
    o_res[...] = res[...]
    o_gin[...] = gin[...].astype(F32)
    o_down[...] = gd[...].astype(F32)
    o_up[...] = gu[...].astype(F32)

    @pl.when(n < n_qkv)
    def _():
        o_qkv[...] = ga[...].astype(F32)

    @pl.when(n >= n_qkv)
    def _():
        o_out[...] = ga[...].astype(F32)

    @pl.when(n == 0)
    def _():
        o_qv[...] = small[10:12, :piece] + small[12:14, piece:2 * piece]
        o_mlp[...] = small[8:9, :]
        o_norms[...] = small[0:8, :]


def outputs(z, res, gin, gd, gu, ga, small):
    D, PC = z.width, z.piece
    tile = 192
    steps = D // tile
    n_qkv = 3 * PC // tile
    token_rows = 2 * z.images * z.slots
    token_tile = token_rows // steps
    tokens = pl.BlockSpec((token_tile, D), lambda n: (n, 0))
    rows = pl.BlockSpec((tile, D), lambda n: (n, 0))
    once = lambda *shape: pl.BlockSpec(shape, lambda n: (0, 0))
    first = pl.BlockSpec((tile, D), lambda n: (jnp.minimum(n, n_qkv - 1), 0))
    last = pl.BlockSpec((tile, D), lambda n: (jnp.maximum(n - n_qkv, 0), 0))
    shape = jax.ShapeDtypeStruct
    return pl.pallas_call(
        functools.partial(widen, PC, n_qkv),
        grid=(steps,),
        out_shape=(
            shape((token_rows, D), BF16), shape((token_rows, D), F32), shape((D, D), F32), shape((D, D), F32),
            shape((3 * PC, D), F32), shape((PC, D), F32), shape((2, PC), F32), shape((1, D), F32), shape((8, D), F32),
        ),
        in_specs=[tokens, tokens, rows, rows, rows, once(16, D)],
        out_specs=(tokens, tokens, rows, rows, first, last, once(2, PC), once(1, D), once(8, D)),
    )(res.reshape(token_rows, D), gin.reshape(token_rows, D), gd, gu, ga, small)


def local(
    n_dp,
    block_in, lengths, patch_mask, pred_grad, w_qkv, w_out, w_up, w_down, qv_bias, mlp_bias, norms
):
    images, slots, width = block_in.shape[1:]
    piece = w_qkv.shape[3]
    z = Sizes(n_dp, images // 2, slots, width, piece)

    x = block_in.reshape(2, z.images, slots, width)
    pg = pred_grad.reshape(2, z.images, slots, width)
    wqkv = jnp.swapaxes(w_qkv[0], 1, 2).reshape(3 * piece, width)
    summed = fused(
        z, x, pg, wqkv, w_out[0], w_up[0], w_down[0], lengths, patch_mask, qv_bias[0], mlp_bias, norms[0]
    )
    res, gin, g_down, g_up, g_qkv, g_out, g_qv, g_mlp, g_norms = outputs(z, *summed)
    return (
        res.reshape(1, images, slots, width),
        gin.reshape(1, images, slots, width),
        jnp.swapaxes(g_qkv.reshape(3, piece, width), 1, 2)[None],
        g_out[None],
        g_up[None],
        g_down[None],
        g_qv[None],
        g_mlp,
        g_norms[None],
    )


def solution(mesh):
    return jax.shard_map(
        functools.partial(local, mesh.shape["dp"]),
        mesh=mesh,
        in_specs=(
            P("section", "dp", "tensor", None),
            P("dp"),
            P("dp", None),
            P("dp", "tensor", None),
            P("section", None, None, "tensor"),
            P("section", "tensor", None),
            P("section", None, "tensor"),
            P("section", "tensor", None),
            P("section", None, "tensor"),
            P("section", "tensor"),
            P("section", None, None),
        ),
        out_specs=(
            P("section", "dp", "tensor", None),
            P("section", "dp", "tensor", None),
            P("section", None, None, "tensor"),
            P("section", "tensor", None),
            P("section", None, "tensor"),
            P("section", "tensor", None),
            P("section", None, "tensor"),
            P("section", "tensor"),
            P("section", None, None),
        ),
        check_vma=False,
    )
```
